128 devices in a mesh: region: 8 (over z, core), dev: 16 (over x, y).
Axes of the slice: x: 4, y: 4, z: 4, core: 2. Of those that a mesh axis runs over, the one named last changes fastest.
Arguments:
- loads: float32 [1024, 32, 1024], P(('region', 'dev')), may hold values from -50 to 50
- factor: bfloat16 [1024, 1024, 1024], P(('region', 'dev')), may hold values from -1 to 1, as said below
- pivots: float32 [1024, 1024], P(('region', 'dev')), may hold values from 0.04 to 0.14, as said below
- lower: float32 [1024, 1024], P(('region', 'dev')), may hold values from -1 to -0.2
- upper: float32 [1024, 1024], P(('region', 'dev')), may hold values from 0.2 to 1
- incidence: int32 [1024, 16], P(('region', 'dev')), may hold values from 0 to 2047, as said below
- counts: int32 [1024], P(('region', 'dev')), may hold values from 8 to 16, as said below
Outputs:
- dispatch: float32 [1024, 32, 1024], P(('region', 'dev'))
- duals: float32 [1024, 16, 128], P(('region', 'dev'))
- residuals: float32 [14, 2], replicated
The draws below stay inside these ranges and needn't reach their ends.
Inputs may be any that keep to these rules, and one draw needn't show every extreme that they name: `incidence`: slot j of area a is live when j < counts[a]. Bus b is owned by device b // 16, devices numbered region-major. The live slots of one device name at most 8 buses owned by any one device of its own region and at most 8 buses owned in any one other region; in every draw every device reaches both bounds. A bus owned in another region is owned by the device with the same dev index there. `counts`: among the 8 areas of each device one has 16 live slots and the others at least 8. `factor`: unit lower triangular: ones on the diagonal, zeros above it. Rows below 64 of every area have inverse pivots of 0.10 or more; the other rows have them up to 0.14 as well.
All inputs are finite; a program needn't handle non-finite values.
Results may differ from the reference program's by a relative error of at most 0.005.
Values sent between devices are 32-bit elements; how exact they have to be, the bound alone decides.
No kernel may reach another device: no remote copies, remote signals or barrier semaphores. Data moves between devices by JAX's collectives and lax.ppermute only.
A program may use at most 64 MiB of HBM per device.

```python
import math
import jax
import jax.numpy as jnp
from jax import lax

K = 1024
S = 32
ROWS_SLOT = 4
BVAL = 128
NB = 16
AREA_DEV = 8
BUS_DEV = 16
CAP_IN = 8
CAP_X = 8
ITERS = 14
AREAS = 1024
NBUS = 2048
N_REGION = 8
N_DEV = 16


def device_buses(dev_key, device_index, area_counts):
    key_order, key_first, key_shift, key_pool, key_pick = jax.random.split(dev_key, 5)
    item_count = AREA_DEV * NB
    region_now = device_index // N_DEV
    column_now = device_index % N_DEV
    live_slot = (jnp.arange(NB)[None, :] < area_counts[:, None]).reshape(item_count)
    scores = jnp.where(live_slot, 0, item_count) + jax.random.permutation(key_order, item_count)
    ordering = jnp.argsort(scores)
    rank_of = jnp.argsort(ordering)
    first_peer = jax.random.randint(key_first, (), 0, N_DEV)
    far_shift = jax.random.randint(key_shift, (), 0, N_REGION - 1)
    far_region = (region_now + 1 + far_shift) % N_REGION
    peer_list = (first_peer + 1 + jnp.arange(N_DEV - 1)) % N_DEV
    near_pool = jnp.repeat(region_now * N_DEV + peer_list, CAP_IN)
    offsets = 1 + (far_shift + 1 + jnp.arange(N_REGION - 2)) % (N_REGION - 1)
    far_pool = jnp.repeat((region_now + offsets) % N_REGION * N_DEV + column_now, CAP_X)
    spare_pool = jax.random.permutation(key_pool, jnp.concatenate([near_pool, far_pool]))
    sequence = jnp.concatenate([jnp.full((CAP_IN,), region_now * N_DEV + first_peer), jnp.full((CAP_X,), far_region * N_DEV + column_now), spare_pool, jnp.full((item_count,), region_now * N_DEV + first_peer)])[:item_count]
    owner_dev = sequence[rank_of]
    bus_local = jax.random.randint(key_pick, (item_count,), 0, BUS_DEV)
    return (owner_dev * BUS_DEV + bus_local).astype(jnp.int32)


def routing_plan(key):
    devices = N_REGION * N_DEV
    key_count, key_full, key_devs = jax.random.split(key, 3)
    area_counts = jax.random.randint(key_count, (devices, AREA_DEV), NB // 2, NB + 1)
    full_area = jax.random.randint(key_full, (devices,), 0, AREA_DEV)
    area_counts = jnp.where(jnp.arange(AREA_DEV)[None, :] == full_area[:, None], NB, area_counts).astype(jnp.int32)
    device_keys = jax.random.split(key_devs, devices)
    bus_ids = jax.vmap(device_buses)(device_keys, jnp.arange(devices, dtype=jnp.int32), area_counts)
    return (area_counts.reshape(AREAS), bus_ids.reshape(AREAS, NB))


def draw_counts(key, part):
    return routing_plan(key)[0]


def draw_incidence(key, part):
    return routing_plan(key)[1]


def draw_factor(key, part):
    key = jax.random.fold_in(key, 11)
    spread = 0.6 / math.sqrt(K)
    below = jnp.arange(K)[:, None] > jnp.arange(K)[None, :]
    noise = jax.random.uniform(key, (AREAS, K, K), jnp.float32, -spread, spread)
    result = jnp.where(below[None, :, :], noise, 0.0) + jnp.eye(K, dtype=jnp.float32)[None, :, :]
    return result.astype(jnp.bfloat16)


def draw_pivots(key, part):
    key = jax.random.fold_in(key, 7)
    key_edge, key_rest = jax.random.split(key)
    edge_rows = jnp.arange(K)[None, :] < NB * ROWS_SLOT
    edge_value = jnp.exp(jax.random.uniform(key_edge, (AREAS, K), jnp.float32, math.log(0.1), math.log(0.14)))
    rest_value = jnp.exp(jax.random.uniform(key_rest, (AREAS, K), jnp.float32, math.log(0.04), math.log(0.14)))
    return jnp.clip(jnp.where(edge_rows, edge_value, rest_value), 0.04, 0.14)


def draw_loads(key, part):
    key = jax.random.fold_in(key, 5)
    key_rough, key_base = jax.random.split(key)
    rising = 1.0 + 2.0 * jnp.arange(AREAS, dtype=jnp.float32) / max(AREAS - 1, 1)
    rough = jnp.exp(jax.random.uniform(key_rough, (AREAS, 1, K), jnp.float32, 0.0, math.log(4.0)))
    base = jnp.clip(jax.random.normal(key_base, (AREAS, S, K), jnp.float32), -4.0, 4.0)
    return 0.6 * rising[:, None, None] * rough * base


def block_levels(key, dims, cuts, low, top_value):
    gain = 1.0
    for axis_at, shards_of in cuts:
        heights = jax.random.uniform(jax.random.fold_in(jax.random.fold_in(key, 6), axis_at), (shards_of,), jnp.float32, low / len(cuts), top_value / len(cuts))
        gain = gain * jnp.repeat(jnp.exp(heights), dims[axis_at] // shards_of).reshape((-1,) + (1,) * (len(dims) - 1 - axis_at))
    return gain


def setup_inputs(seed: int = 0) -> dict:
    splits = jax.random.split(jax.random.key(seed), 8)
    loads = draw_loads(jax.random.fold_in(splits[7], 71), 0)
    factor = draw_factor(jax.random.fold_in(splits[7], 71), 0)
    pivots = draw_pivots(jax.random.fold_in(splits[7], 71), 0)
    lower = jnp.clip(-1.0 + 0.8 * jax.random.uniform(splits[3], (AREAS, K), jnp.float32) ** block_levels(splits[3], (AREAS, K), ((0, 128),), -0.2, 0.2), -1.0, -0.2)
    upper = jnp.clip(0.2 + 0.8 * jax.random.uniform(splits[4], (AREAS, K), jnp.float32) ** block_levels(splits[4], (AREAS, K), ((0, 128),), -0.2, 0.2), 0.2, 1.0)
    incidence = draw_incidence(jax.random.fold_in(splits[7], 71), 0)
    counts = draw_counts(jax.random.fold_in(splits[7], 71), 0)
    return dict(loads=loads, factor=factor, pivots=pivots, lower=lower, upper=upper, incidence=incidence, counts=counts)


RHO = 4.0
SIGMA = 1.0


def to_blocks(state_field):
    leading = state_field[:, :, :NB * ROWS_SLOT].reshape(state_field.shape[0], S, NB, ROWS_SLOT)
    return jnp.transpose(leading, (0, 2, 1, 3)).reshape(state_field.shape[0], NB, BVAL)


def from_blocks(blocks):
    leading = jnp.transpose(blocks.reshape(blocks.shape[0], NB, S, ROWS_SLOT), (0, 2, 1, 3))
    leading = leading.reshape(blocks.shape[0], S, NB * ROWS_SLOT)
    return jnp.pad(leading, ((0, 0), (0, 0), (0, K - NB * ROWS_SLOT)))


def solve_area(packed):
    right_side, factor_one, pivot_one = packed
    forward = jnp.dot(right_side.astype(jnp.bfloat16), factor_one.T, preferred_element_type=jnp.float32)
    scaled = (forward * pivot_one[None, :]).astype(jnp.bfloat16)
    return jnp.dot(scaled, factor_one, preferred_element_type=jnp.float32)


def reference(loads, factor, pivots, lower, upper, incidence, counts):
    live_slot = (jnp.arange(NB)[None, :] < counts[:, None]).astype(jnp.float32)[:, :, None]
    flat_bus = incidence.reshape(-1)
    bus_count = jax.ops.segment_sum(live_slot.reshape(-1), flat_bus, num_segments=NBUS)
    bus_count = jnp.maximum(bus_count, 1.0)
    duals = jnp.zeros((AREAS, NB, BVAL), jnp.float32)
    z_slot = jnp.zeros((AREAS, NB, BVAL), jnp.float32)
    clipped = jnp.zeros_like(loads)
    offset = jnp.zeros_like(loads)
    z_prev = jnp.zeros((NBUS, BVAL), jnp.float32)
    dispatch = jnp.zeros_like(loads)
    history = []
    for step_num in range(ITERS):
        right_side = loads + RHO * from_blocks(live_slot * (z_slot - duals)) + SIGMA * (clipped - offset)
        dispatch = lax.map(solve_area, (right_side, factor, pivots))
        clipped_new = jnp.clip(dispatch + offset, lower[:, None, :], upper[:, None, :])
        offset = offset + dispatch - clipped_new
        clipped = clipped_new
        blocks = to_blocks(dispatch)
        values = live_slot * (blocks + duals)
        z_bus = jax.ops.segment_sum(values.reshape(-1, BVAL), flat_bus, num_segments=NBUS) / bus_count[:, None]
        z_slot = live_slot * z_bus[incidence]
        misfit = live_slot * (blocks - z_slot)
        duals = duals + misfit
        change = z_bus - z_prev
        history.append(jnp.stack([jnp.sum(misfit * misfit), RHO * RHO * jnp.sum(change * change)]))
        z_prev = z_bus
    residuals = jnp.stack(history) / (AREAS * BVAL)
    return dispatch, duals, residuals
```

```python
import jax
import jax.numpy as jnp
from jax import lax
from jax.experimental import pallas as pl
from jax.experimental.pallas import tpu as pltpu
from jax.sharding import PartitionSpec as P

K = 1024
S = 32
AREA = 8
NB = 16
ITEMS = AREA * NB
ROWS = 4
EDGE = NB * ROWS
CAP = 8
N_REGION = 8
N_DEV = 16
WORLD = N_REGION * N_DEV
BUS_DEV = 16
ITERS = 14
RHO = 4.0
SIGMA = 1.0
CELLS = 1024.0 * 128.0
BOTH = ("region", "dev")
F32 = jnp.float32
BF16 = jnp.bfloat16
VMEM_LIMIT = 56 * 1024 * 1024


def dot(left, right):
    return jnp.dot(left, right, preferred_element_type=F32)


def split3(x):
    high = x.astype(BF16)
    rest = x - high.astype(F32)
    middle = rest.astype(BF16)
    low = (rest - middle.astype(F32)).astype(BF16)
    return high, middle, low


def pick(x, onehot):
    count = x.shape[0]
    got = dot(jnp.concatenate(split3(x), axis=0), onehot)
    return got[:count] + got[count : 2 * count] + got[2 * count :]


def iota(shape, dim):
    return lax.broadcasted_iota(jnp.int32, shape, dim)


def edge_perm(area):
    row = iota((128, ROWS * ITEMS), 0)
    col = iota((128, ROWS * ITEMS), 1)
    target = (row & 3) * ITEMS + area * NB + (row >> 2)
    return jnp.where((row < EDGE) & (col == target), 1.0, 0.0).astype(BF16)


def edge_perm_t(area):
    row = iota((ROWS * ITEMS, 128), 0)
    col = iota((ROWS * ITEMS, 128), 1)
    target = (col & 3) * ITEMS + area * NB + (col >> 2)
    return jnp.where((col < EDGE) & (row == target), 1.0, 0.0).astype(BF16)


def call(kernel, out_shape, **kw):
    params = dict(vmem_limit_bytes=kw.pop("limit", VMEM_LIMIT))
    return pl.pallas_call(
        kernel,
        out_shape=out_shape,
        compiler_params=pltpu.CompilerParams(**params),
        **kw,
    )


def struct(shape, dtype=F32):
    return jax.ShapeDtypeStruct(shape, dtype)


def route_kernel(me_ref, ids_col, ids_row, live_col, live_row, p_ref, pt_ref, tag_ref):
    me = me_ref[0]

    def key_of(ids, live):
        region = ids >> 8
        peer = (ids >> 4) & 15
        return jnp.where(live > 0, jnp.where(region == me, peer, 16 + region), -1)

    key_c = key_of(ids_col[...], live_col[...])
    key_r = key_of(ids_row[...], live_row[...])
    same = (key_c == key_r) & (key_r >= 0)
    sub = iota((ITEMS, ITEMS), 0)
    lane = iota((ITEMS, ITEMS), 1)
    rank_c = jnp.sum(jnp.where(same & (lane < sub), 1.0, 0.0), axis=1, keepdims=True)
    rank_r = jnp.sum(jnp.where(same & (sub < lane), 1.0, 0.0), axis=0, keepdims=True)

    def place(key, rank):
        rank = rank.astype(jnp.int32)
        far = ITEMS + rank * N_REGION + key - 16
        return jnp.where(key < 0, -1, jnp.where(key < 16, rank * N_DEV + key, far))

    hit = iota((ITEMS, 256), 1) == place(key_c, rank_c)
    p_ref[...] = jnp.where(hit, 1.0, 0.0).astype(BF16)
    hit_t = iota((256, ITEMS), 0) == place(key_r, rank_r)
    pt_ref[...] = jnp.where(hit_t, 1.0, 0.0).astype(BF16)
    local = ((ids_col[...] & 15) + 1).astype(F32)
    tag = jnp.sum(jnp.where(hit, local, 0.0), axis=0, keepdims=True) - 1.0
    odd = iota((256, ITEMS), 0) & 1
    tag_ref[...] = jnp.where(odd == 0, tag[:, :ITEMS], tag[:, ITEMS:]).astype(jnp.int32)


def near_tile(ref, dev):
    return ref[pl.ds(2 * dev, N_REGION, stride=2 * N_DEV), :]


def far_tile(ref, region):
    return ref[pl.ds(2 * N_DEV * region + 1, N_DEV, stride=2), :]


def bus_sums(near, far, near_tags, far_tags):
    group = iota((N_REGION, 128), 1) >> 4
    halves = []
    far_sums = []
    for half in range(2):
        total = jnp.zeros((N_REGION, 128), F32)
        for low in range(8):
            bus = 8 * half + low
            acc = jnp.zeros((N_REGION, 128), F32)
            for dev in range(N_DEV):
                acc = acc + jnp.where(near_tags[dev] == bus, near[dev], 0.0)
            for shift in (16, 32, 64):
                acc = acc + pltpu.roll(acc, shift, 1)
            total = jnp.where(group == low, acc, total)
        halves.append(total)
        rows = []
        for low in range(8):
            bus = 8 * half + low
            acc = jnp.zeros((N_DEV, 128), F32)
            for region in range(N_REGION):
                acc = acc + jnp.where(far_tags[region] == bus, far[region], 0.0)
            rows.append(acc)
        turned = jnp.transpose(jnp.concatenate(rows, axis=0))
        total = turned[:8]
        for c in range(1, CAP):
            total = total + turned[8 * c : 8 * c + 8]
        far_sums.append(total)
    return jnp.concatenate([halves[0] + far_sums[0], halves[1] + far_sums[1]], axis=1)


def count_kernel(tag_ref, inv_ref):
    near_tags = [near_tile(tag_ref, d) for d in range(N_DEV)]
    far_tags = [far_tile(tag_ref, r) for r in range(N_REGION)]
    one_n = jnp.ones((N_REGION, 128), F32)
    one_f = jnp.ones((N_DEV, 128), F32)
    counts = bus_sums([one_n] * N_DEV, [one_f] * N_REGION, near_tags, far_tags)
    inv_ref[...] = 1.0 / jnp.maximum(counts, 1.0)


def owner_kernel(step_ref, got_ref, tag_ref, inv_ref, prev_ref, rec_in, out_ref, z_ref, rec_ref):
    near_tags = [near_tile(tag_ref, d) for d in range(N_DEV)]
    far_tags = [far_tile(tag_ref, r) for r in range(N_REGION)]
    near = [near_tile(got_ref, d) for d in range(N_DEV)]
    far = [far_tile(got_ref, r) for r in range(N_REGION)]
    z = bus_sums(near, far, near_tags, far_tags) * inv_ref[...]
    change = z - prev_ref[...]
    change = change * change
    row = jnp.sum(change[:, :128] + change[:, 128:], axis=0, keepdims=True)
    rec_ref[...] = rec_in[...]
    rec_ref[pl.ds(step_ref[0], 1), :] = row * (RHO * RHO / CELLS)
    z_ref[...] = z
    group = iota((N_REGION, 128), 1) >> 4
    spread = []
    turned = []
    for half in range(2):
        part = z[:, 128 * half : 128 * half + 128]
        for low in range(8):
            one = jnp.where(group == low, part, 0.0)
            for shift in (16, 32, 64):
                one = one + pltpu.roll(one, shift, 1)
            spread.append(one)
        turned.append(jnp.transpose(jnp.concatenate([part] * 16, axis=0)))
    for dev in range(N_DEV):
        tag = near_tags[dev]
        val = jnp.zeros((N_REGION, 128), F32)
        for bus in range(BUS_DEV):
            val = jnp.where(tag == bus, spread[bus], val)
        out_ref[pl.ds(2 * dev, N_REGION, stride=2 * N_DEV), :] = val
    for region in range(N_REGION):
        tag = far_tags[region]
        val = jnp.zeros((N_DEV, 128), F32)
        for bus in range(BUS_DEV):
            low = bus % 8
            val = jnp.where(tag == bus, turned[bus // 8][16 * low : 16 * low + 16], val)
        out_ref[pl.ds(2 * N_DEV * region + 1, N_DEV, stride=2), :] = val


def slot_kernel(
    step_ref, z_ref, p_ref, pt_ref, live_ref, blk_in, u_in, c_ref, bdh_ref, bdl_ref, rec_in,
    send_ref, e_ref, blk_ref, u_ref, rec_ref,
):
    z_got = jnp.concatenate(
        [z_ref[pl.ds(0, WORLD, stride=2), :], z_ref[pl.ds(1, WORLD, stride=2), :]], axis=1
    )
    z_slot = pick(z_got, pt_ref[...])
    gap = (blk_in[...] - z_slot) * live_ref[...]
    u = u_in[...] + gap
    u_ref[...] = u
    rec_ref[...] = rec_in[...]
    rec_ref[pl.ds(step_ref[0], 1), :] = jnp.sum(gap * gap, axis=0, keepdims=True) * (1.0 / CELLS)
    push = RHO * (z_slot - u)
    e = jnp.concatenate([push[S * r : S * r + S] for r in range(ROWS)], axis=1)
    e_ref[...] = e
    e_high = e.astype(BF16)
    e_low = (e - e_high.astype(F32)).astype(BF16)
    both = dot(jnp.concatenate([e_high, e_low], axis=0), bdh_ref[...])
    edge = c_ref[...] + both[:S] + both[S:] + dot(e_high, bdl_ref[...])
    blk = jnp.concatenate([edge[:, ITEMS * r : ITEMS * r + ITEMS] for r in range(ROWS)], axis=0)
    blk_ref[...] = blk
    send = pick(blk + u, p_ref[...])
    send_ref[pl.ds(0, WORLD, stride=2), :] = send[:, :128]
    send_ref[pl.ds(1, WORLD, stride=2), :] = send[:, 128:]


def edge_part(right_side, m_edge, diag_edge):
    return dot(right_side.astype(BF16), m_edge) + right_side[:, :128] * diag_edge


def setup_kernel(f_ref, p_ref, load_ref, m_ref, diag_ref, c_ref, bdh_ref, bdl_ref, acc, bd):
    area = pl.program_id(0)
    piv = p_ref[0]
    piv_col = jnp.transpose(jnp.broadcast_to(piv, (128, K)))
    step = 256
    for i in reversed(range(K // step)):
        w = (i + 1) * step
        rows = f_ref[0, i * step : w, :w]
        col = piv_col[i * step : w, :]
        scaled = jnp.concatenate(
            [
                (rows[:, 128 * q : 128 * q + 128].astype(F32) * col).astype(BF16)
                for q in range(w // 128)
            ],
            axis=1,
        )
        part = lax.dot_general(
            rows, scaled, (((0,), (0,)), ((), ())), preferred_element_type=F32
        )
        if w == K:
            acc[...] = part
        else:
            acc[:w, :w] = acc[:w, :w] + part
    eye = iota((step, step), 0) == iota((step, step), 1)
    fix = piv - piv.astype(BF16).astype(F32)
    diags = []
    for i in range(K // step):
        at = slice(i * step, (i + 1) * step)
        block = acc[at, at]
        diags.append(jnp.sum(jnp.where(eye, block, 0.0), axis=0, keepdims=True))
        acc[at, at] = jnp.where(eye, 0.0, block)
    diag = jnp.concatenate(diags, axis=1) + fix
    diag_ref[0] = diag
    m_ref[0] = acc[...].astype(BF16)
    edge_diag = diag[:, :128]
    perm = edge_perm(area)
    small_eye = iota((128, 128), 0) == iota((128, 128), 1)
    m_ee = jnp.where(small_eye, edge_diag, acc[:128, :128])
    spread = pick(m_ee, perm)
    block = dot(edge_perm_t(area), jnp.concatenate(split3(spread), axis=1))
    wide = ROWS * ITEMS
    block = block[:, :wide] + block[:, wide : 2 * wide] + block[:, 2 * wide :]
    c = pick(edge_part(load_ref[0], m_ref[0, :, :128], edge_diag), perm)

    @pl.when(area == 0)
    def _():
        bd[...] = block
        c_ref[...] = c

    @pl.when(area > 0)
    def _():
        bd[...] = bd[...] + block
        c_ref[...] = c_ref[...] + c

    @pl.when(area == AREA - 1)
    def _():
        full = bd[...]
        high = full.astype(BF16)
        bdh_ref[...] = high
        bdl_ref[...] = (full - high.astype(F32)).astype(BF16)


def area_kernel(
    m_ref, diag_ref, load_ref, lo_ref, hi_ref, e_ref, w_in, b_in, x_ref, w_ref, b_ref, c_ref, e_all
):
    area = pl.program_id(0)

    @pl.when(area == 0)
    def _():
        e3 = jnp.concatenate(split3(e_ref[...]), axis=0)
        for a in range(AREA):
            got = dot(e3, edge_perm_t(a))
            e_all[a] = got[:S] + got[S : 2 * S] + got[2 * S :]
        c_ref[...] = jnp.zeros_like(c_ref)

    base = b_in[0]
    right_side = jnp.concatenate([base[:, :128] + e_all[area], base[:, 128:]], axis=1)
    diag = diag_ref[0]
    x = dot(right_side.astype(BF16), m_ref[0]) + right_side * diag
    x_ref[0] = x
    moved = x + w_in[0]
    y = jnp.clip(moved, lo_ref[0], hi_ref[0])
    w = moved - y
    w_ref[0] = w
    b = load_ref[0] + SIGMA * (y - w)
    b_ref[0] = b
    c = edge_part(b, m_ref[0, :, :128], diag[:, :128])
    c_ref[...] = c_ref[...] + pick(c, edge_perm(area))


def area_block(rows):
    return pl.BlockSpec((1, rows, K), lambda a: (a, 0, 0))


def whole(shape):
    return pl.BlockSpec(shape, lambda a: (0,) * len(shape))


def cost(flops, nbytes):
    return pl.CostEstimate(flops=flops, bytes_accessed=nbytes, transcendentals=0)


SMEM = pl.BlockSpec(memory_space=pltpu.SMEM)
VM = pl.BlockSpec(memory_space=pltpu.VMEM)


def on_device(loads, factor, pivots, lower, upper, incidence, counts):
    wide = ROWS * ITEMS
    exchange = lambda x: lax.all_to_all(x, BOTH, split_axis=0, concat_axis=0, tiled=True)
    me = lax.axis_index("region").astype(jnp.int32).reshape(1)
    live = (jnp.arange(NB)[None, :] < counts[:, None]).astype(jnp.int32).reshape(1, ITEMS)
    ids = incidence.reshape(1, ITEMS)
    place, place_t, tags = call(
        route_kernel,
        (struct((ITEMS, 256), BF16), struct((256, ITEMS), BF16), struct((256, ITEMS), jnp.int32)),
        in_specs=[SMEM, VM, VM, VM, VM],
    )(me, ids.reshape(ITEMS, 1), ids, live.reshape(ITEMS, 1), live)
    live_row = live.astype(F32)
    tags = exchange(tags)

    matrix, diag, c_now, bd_high, bd_low = call(
        setup_kernel,
        (
            struct((AREA, K, K), BF16),
            struct((AREA, 1, K)),
            struct((S, wide)),
            struct((wide, wide), BF16),
            struct((wide, wide), BF16),
        ),
        grid=(AREA,),
        in_specs=[area_block(K), area_block(1), area_block(S)],
        out_specs=(
            area_block(K), area_block(1), whole((S, wide)), whole((wide, wide)), whole((wide, wide)),
        ),
        scratch_shapes=[pltpu.VMEM((K, K), F32), pltpu.VMEM((wide, wide), F32)],
        cost_estimate=cost(8 * 10**9, 34 * 2**20),
    )(factor, pivots.reshape(AREA, 1, K), loads)

    inverse = call(count_kernel, struct((N_REGION, 256)))(tags)
    floor_box = lower.reshape(AREA, 1, K)
    ceil_box = upper.reshape(AREA, 1, K)

    run_slots = call(
        slot_kernel,
        (
            struct((256, 128)),
            struct((S, wide)),
            struct((128, 128)),
            struct((128, 128)),
            struct((16, 128)),
        ),
        in_specs=[SMEM] + [VM] * 10,
        input_output_aliases={5: 2, 6: 3, 10: 4},
        cost_estimate=cost(10**8, 3 * 2**20),
        limit=16 * 2**20,
    )
    run_owner = call(
        owner_kernel,
        (struct((256, 128)), struct((N_REGION, 256)), struct((16, 128))),
        in_specs=[SMEM] + [VM] * 5,
        input_output_aliases={4: 1, 5: 2},
        cost_estimate=cost(10**7, 2**20),
        limit=16 * 2**20,
    )
    run_areas = call(
        area_kernel,
        (
            struct((AREA, S, K)), struct((AREA, S, K)), struct((AREA, S, K)), struct((S, wide)),
        ),
        grid=(AREA,),
        in_specs=[
            area_block(K), area_block(1), area_block(S), area_block(1), area_block(1),
            whole((S, wide)), area_block(S), area_block(S),
        ],
        out_specs=(area_block(S), area_block(S), area_block(S), whole((S, wide))),
        scratch_shapes=[pltpu.VMEM((AREA, S, 128), F32)],
        input_output_aliases={6: 1, 7: 2},
        cost_estimate=cost(6 * 10**8, 22 * 2**20),
        limit=24 * 2**20,
    )

    def slots(step, z_back, blk, u, c, rec):
        return run_slots(
            step.reshape(1), z_back, place, place_t, live_row, blk, u, c, bd_high, bd_low, rec
        )

    zero = jnp.zeros((128, 128), F32)
    rec = jnp.zeros((16, 128), F32)
    send, e, blk, u, prim = slots(
        jnp.int32(15), jnp.zeros((256, 128), F32), zero, zero, c_now, rec
    )

    def iterate(step, state):
        _, send, e, blk, u, prim, dual, z_prev, w, b = state
        got = exchange(send)
        x, w, b, c = run_areas(matrix, diag, loads, floor_box, ceil_box, e, w, b)
        step = step.astype(jnp.int32)
        back, z_prev, dual = run_owner(step.reshape(1), got, tags, inverse, z_prev, dual)
        z_back = exchange(back)
        send, e, blk, u, prim = slots(step, z_back, blk, u, c, prim)
        return (x, send, e, blk, u, prim, dual, z_prev, w, b)

    state = (
        jnp.zeros_like(loads), send, e, blk, u, prim, rec,
        jnp.zeros((N_REGION, 256), F32), jnp.zeros_like(loads), loads,
    )
    state = lax.fori_loop(0, ITERS, iterate, state)
    x, u, prim, dual = state[0], state[4], state[5], state[6]
    duals = jnp.transpose(u.reshape(ROWS, S, ITEMS), (2, 1, 0)).reshape(AREA, NB, 128)
    sums = jnp.concatenate(
        [jnp.sum(prim, axis=1)[:ITERS], jnp.sum(dual, axis=1)[:ITERS], jnp.zeros((100,), F32)]
    )
    shared = exchange(jnp.broadcast_to(sums[None, :], (WORLD, 128)))
    total = jnp.sum(shared, axis=0)
    record = jnp.stack([total[:ITERS], total[ITERS : 2 * ITERS]], axis=1)
    return (x, duals, record)


def solution(mesh):
    area_split = (
        P(BOTH, None, None),
        P(BOTH, None, None),
        P(BOTH, None),
        P(BOTH, None),
        P(BOTH, None),
        P(BOTH, None),
        P(BOTH),
    )
    return jax.shard_map(
        on_device,
        mesh=mesh,
        in_specs=area_split,
        out_specs=(P(BOTH, None, None), P(BOTH, None, None), P()),
        check_vma=False,
    )
```

```python
import functools

import jax
import jax.numpy as jnp
from jax import lax
from jax.experimental import pallas as pl
from jax.experimental.pallas import tpu as pltpu
from jax.sharding import PartitionSpec as P

K = 1024
S = 32
AREA = 8
NB = 16
ITEMS = AREA * NB
ROWS = 4
EDGE = NB * ROWS
CAP = 8
N_REGION = 8
N_DEV = 16
WORLD = N_REGION * N_DEV
BUS_DEV = 16
ITERS = 14
RHO = 4.0
SIGMA = 1.0
HALF = AREA // 2
CELLS = 1024.0 * 128.0
BOTH = ("region", "dev")
F32 = jnp.float32
BF16 = jnp.bfloat16


def dot(left, right):
    return jnp.dot(left, right, preferred_element_type=F32)


def split3(x):
    high = x.astype(BF16)
    rest = x - high.astype(F32)
    middle = rest.astype(BF16)
    low = (rest - middle.astype(F32)).astype(BF16)
    return high, middle, low


def pick(x, onehot):
    count = x.shape[0]
    got = dot(jnp.concatenate(split3(x), axis=0), onehot)
    return got[:count] + got[count : 2 * count] + got[2 * count :]


def iota(shape, dim):
    return lax.broadcasted_iota(jnp.int32, shape, dim)


def edge_order(transposed=False):
    old = iota((128, 128), 1 if transposed else 0)
    new = iota((128, 128), 0 if transposed else 1)
    target = jnp.where(old < EDGE, (old & 3) * NB + (old >> 2), old)
    return jnp.where(new == target, 1.0, 0.0).astype(BF16)


def struct(shape, dtype=F32):
    return jax.ShapeDtypeStruct(shape, dtype)


def cost(flops, nbytes):
    return pl.CostEstimate(flops=flops, bytes_accessed=nbytes, transcendentals=0)


SMEM = pl.BlockSpec(memory_space=pltpu.SMEM)
VM = pl.BlockSpec(memory_space=pltpu.VMEM)
ANY = pl.BlockSpec(memory_space=pl.ANY)


def call(kernel, out_shape, limit=16, **kw):
    return pl.pallas_call(
        kernel,
        out_shape=out_shape,
        compiler_params=pltpu.CompilerParams(vmem_limit_bytes=limit * 2**20),
        **kw,
    )


def route_kernel(me_ref, counts_ref, inc_ref, p_ref, pt_ref, tag_ref, live_ref):
    me = me_ref[0]
    lane = iota((ITEMS, ITEMS), 1)
    sub = iota((ITEMS, ITEMS), 0)
    area_of = iota((1, ITEMS), 1) >> 4
    wide = jnp.concatenate([inc_ref[...].astype(F32), jnp.zeros((AREA, 112), F32)], axis=1)
    ids = jnp.zeros((1, ITEMS), F32)
    count = jnp.zeros((1, ITEMS), jnp.int32)
    for a in range(AREA):
        row = wide[a : a + 1, :]
        if a:
            row = pltpu.roll(row, NB * a, 1)
        ids = jnp.where(area_of == a, row, ids)
        count = jnp.where(area_of == a, counts_ref[a], count)
    live = (iota((1, ITEMS), 1) & 15) < count
    live_ref[...] = jnp.where(live, 1.0, 0.0)
    bus = ids.astype(jnp.int32)
    region = bus >> 8
    peer = (bus >> 4) & 15
    key_r = jnp.where(live, jnp.where(region == me, peer, 16 + region), -1).astype(F32)
    key_c = jnp.transpose(jnp.broadcast_to(key_r, (ITEMS, ITEMS)))
    local_c = jnp.transpose(jnp.broadcast_to((bus & 15).astype(F32), (ITEMS, ITEMS)))
    same = (key_c == key_r) & (key_r >= 0.0)
    rank_c = jnp.sum(jnp.where(same & (lane < sub), 1.0, 0.0), axis=1, keepdims=True)
    rank_r = jnp.sum(jnp.where(same & (sub < lane), 1.0, 0.0), axis=0, keepdims=True)

    def place(key, rank):
        far = ITEMS + rank * N_REGION + key - 16.0
        return jnp.where(key < 0.0, -1.0, jnp.where(key < 16.0, rank * N_DEV + key, far))

    place_c = place(key_c, jnp.broadcast_to(rank_c, (ITEMS, ITEMS)))
    place_c = jnp.concatenate([place_c, place_c], axis=1)
    local_c = jnp.concatenate([local_c, local_c], axis=1)
    hit = iota((ITEMS, 256), 1).astype(F32) == place_c
    p_ref[...] = jnp.where(hit, 1.0, 0.0).astype(BF16)
    hit_t = iota((256, ITEMS), 0).astype(F32) == place(key_r, rank_r)
    pt_ref[...] = jnp.where(hit_t, 1.0, 0.0).astype(BF16)
    tag = jnp.sum(jnp.where(hit, local_c + 1.0, 0.0), axis=0, keepdims=True) - 1.0
    tag_ref[0:1, :] = tag[:, :128]
    tag_ref[1:2, :] = tag[:, 128:]


def near_rows(width, dev):
    return pl.ds(width * dev, N_REGION, stride=width * N_DEV)


def far_rows(width, region):
    return pl.ds(width * N_DEV * region + 1, N_DEV, stride=width)


def bus_sums(near, far, near_tags, far_tags):
    group = iota((N_REGION, 128), 1) >> 4
    halves = []
    for half in range(2):
        total = jnp.zeros((N_REGION, 128), F32)
        for low in range(8):
            bus = 8.0 * half + low
            acc = jnp.zeros((N_REGION, 128), F32)
            for dev in range(N_DEV):
                acc = acc + jnp.where(near_tags[dev] == bus, near[dev], 0.0)
            for shift in (16, 32, 64):
                acc = acc + pltpu.roll(acc, shift, 1)
            total = jnp.where(group == low, acc, total)
        rows = []
        for low in range(8):
            bus = 8.0 * half + low
            acc = jnp.zeros((N_DEV, 128), F32)
            for region in range(N_REGION):
                acc = acc + jnp.where(far_tags[region] == bus, far[region], 0.0)
            rows.append(acc)
        turned = jnp.transpose(jnp.concatenate(rows, axis=0))
        for c in range(CAP):
            total = total + turned[8 * c : 8 * c + 8]
        halves.append(total)
    return jnp.concatenate(halves, axis=1)


def owner_kernel(first, last, *refs):
    if first:
        got_ref, tie_ref, out_ref, z_ref, u_ref, rec_ref, tag_ref, inv_ref = refs
        near_tags = [got_ref[pl.ds(4 * d + 2, N_REGION, stride=4 * N_DEV), :] for d in range(N_DEV)]
        far_tags = [
            got_ref[pl.ds(4 * N_DEV * r + 3, N_DEV, stride=4), :] for r in range(N_REGION)
        ]
        one_n = jnp.ones((N_REGION, 128), F32)
        one_f = jnp.ones((N_DEV, 128), F32)
        counts = bus_sums([one_n] * N_DEV, [one_f] * N_REGION, near_tags, far_tags)
        inverse = 1.0 / jnp.maximum(counts, 1.0)
        inv_ref[...] = inverse
        for d in range(N_DEV):
            tag_ref[near_rows(2, d), :] = near_tags[d]
        for r in range(N_REGION):
            tag_ref[far_rows(2, r), :] = far_tags[r]
        rec_ref[...] = jnp.zeros((128, 128), F32)
        step = 0
    else:
        if last:
            step_ref, got_ref, tag_ref, inv_ref, tie_ref, prev_ref, u_in, rec_in, out_ref = refs
        else:
            (step_ref, got_ref, tag_ref, inv_ref, tie_ref, prev_ref, u_in, rec_in,
             out_ref, z_ref, u_ref, rec_ref) = refs
        near_tags = [tag_ref[near_rows(2, d), :] for d in range(N_DEV)]
        far_tags = [tag_ref[far_rows(2, r), :] for r in range(N_REGION)]
        inverse = inv_ref[...]
        step = step_ref[0]
    wide_in = 4 if first else 2
    wide_out = 4 if last else 2
    near = [got_ref[near_rows(wide_in, d), :] for d in range(N_DEV)]
    far = [got_ref[far_rows(wide_in, r), :] for r in range(N_REGION)]
    z = bus_sums(near, far, near_tags, far_tags) * inverse
    change = z if first else z - prev_ref[...]
    change = change * change
    dual = jnp.sum(change[:, :128] + change[:, 128:], axis=0, keepdims=True) * (RHO * RHO / CELLS)
    group = iota((N_REGION, 128), 1) >> 4
    spread = []
    turned = []
    for half in range(2):
        part = z[:, 128 * half : 128 * half + 128]
        for low in range(8):
            one = jnp.where(group == low, part, 0.0)
            for shift in (16, 32, 64):
                one = one + pltpu.roll(one, shift, 1)
            spread.append(one)
        turned.append(jnp.transpose(jnp.concatenate([part] * 16, axis=0)))
    primal = jnp.zeros((N_REGION, 128), F32)
    for dev in range(N_DEV):
        val = jnp.zeros((N_REGION, 128), F32)
        for bus in range(BUS_DEV):
            val = jnp.where(near_tags[dev] == float(bus), spread[bus], val)
        out_ref[near_rows(wide_out, dev), :] = val
        u = near[dev] - val
        gap = u if first else u - u_in[near_rows(2, dev), :]
        primal = primal + gap * gap
        if not last:
            u_ref[near_rows(2, dev), :] = u
    for region in range(N_REGION):
        val = jnp.zeros((N_DEV, 128), F32)
        for bus in range(BUS_DEV):
            low = bus % 8
            one = turned[bus // 8][16 * low : 16 * low + 16]
            val = jnp.where(far_tags[region] == float(bus), one, val)
        out_ref[far_rows(wide_out, region), :] = val
        u = far[region] - val
        gap = u if first else u - u_in[far_rows(2, region), :]
        square = gap * gap
        primal = primal + square[:8] + square[8:]
        if not last:
            u_ref[far_rows(2, region), :] = u
    primal = jnp.sum(primal, axis=0, keepdims=True) * (1.0 / CELLS)
    row = iota((128, 128), 0)
    if last:
        rec = jnp.where(row == step, primal, rec_in[...])
        rec = jnp.where(row == 16 + step, dual, rec)
        sums = jnp.sum(jnp.transpose(rec), axis=0, keepdims=True)
        out_ref[pl.ds(2, WORLD, stride=4), :] = jnp.broadcast_to(sums, (WORLD, 128))
        out_ref[pl.ds(3, WORLD, stride=4), :] = jnp.zeros((WORLD, 128), F32)
    else:
        if not first:
            rec_ref[...] = rec_in[...]
        rec_ref[pl.ds(step, 1), :] = primal
        rec_ref[pl.ds(16 + step, 1), :] = dual
        z_ref[...] = z


def by_lane(rows):
    return jnp.concatenate([rows[S * r : S * r + S] for r in range(ROWS)], axis=1)


def by_row(lanes):
    return jnp.concatenate([lanes[:, ITEMS * r : ITEMS * r + ITEMS] for r in range(ROWS)], axis=0)


def open_kernel(c_ref, p_ref, tag_ref, send_ref, e_ref, blk_ref, u_ref):
    blk = by_row(c_ref[...])
    blk_ref[...] = blk
    u_ref[...] = jnp.zeros_like(blk)
    e_ref[...] = jnp.zeros((S, ROWS * ITEMS), F32)
    send = pick(blk, p_ref[...])
    send_ref[pl.ds(0, WORLD, stride=4), :] = send[:, :128]
    send_ref[pl.ds(1, WORLD, stride=4), :] = send[:, 128:]
    send_ref[pl.ds(2, WORLD, stride=4), :] = jnp.broadcast_to(tag_ref[0:1, :], (WORLD, 128))
    send_ref[pl.ds(3, WORLD, stride=4), :] = jnp.broadcast_to(tag_ref[1:2, :], (WORLD, 128))


def take_means(z_ref, pt_ref, width):
    near = z_ref[pl.ds(0, WORLD, stride=width), :]
    far = z_ref[pl.ds(1, WORLD, stride=width), :]
    return pick(jnp.concatenate([near, far], axis=1), pt_ref[...])


def slot_kernel(
    z_ref, p_ref, pt_ref, live_ref, blk_in, u_in, c_ref, bdh_ref, bdl_ref,
    send_ref, e_ref, blk_ref, u_ref,
):
    z_slot = take_means(z_ref, pt_ref, 2)
    u = u_in[...] + (blk_in[...] - z_slot) * live_ref[...]
    u_ref[...] = u
    e = by_lane(RHO * (z_slot - u))
    e_ref[...] = e
    e_high = e.astype(BF16)
    e_low = (e - e_high.astype(F32)).astype(BF16)
    both = dot(jnp.concatenate([e_high, e_low], axis=0), bdh_ref[...])
    edge = c_ref[...] + both[:S] + both[S:] + dot(e_high, bdl_ref[...])
    blk = by_row(edge)
    blk_ref[...] = blk
    send = pick(blk + u, p_ref[...])
    send_ref[pl.ds(0, WORLD, stride=2), :] = send[:, :128]
    send_ref[pl.ds(1, WORLD, stride=2), :] = send[:, 128:]


def close_kernel(z_ref, pt_ref, live_ref, blk_in, u_in, dual_ref, record_ref):
    z_slot = take_means(z_ref, pt_ref, 4)
    u = u_in[...] + (blk_in[...] - z_slot) * live_ref[...]
    old = iota((128, 128), 0)
    order = jnp.where(iota((128, 128), 1) == (old & 31) * ROWS + (old >> 5), 1.0, 0.0)
    dual_ref[...] = pick(jnp.transpose(u), order.astype(BF16))
    sums = jnp.sum(z_ref[pl.ds(2, WORLD, stride=4), :], axis=0, keepdims=True)
    column = jnp.transpose(jnp.broadcast_to(sums, (128, 128)))
    first = iota((16, 128), 1) == 0
    both = jnp.where(first, column[:16], column[16:32])
    record_ref[...] = both[:ITERS, :2]


def edge_part(right_side, m_edge, diag_edge):
    return dot(right_side.astype(BF16), m_edge) + right_side[:, :128] * diag_edge


def setup_kernel(
    f_ref, p_ref, load_ref, lo_ref, hi_ref,
    m_ref, diag_ref, c_ref, bdh_ref, bdl_ref, load0_ref, load1_ref, lo_out, hi_out, ft, g,
):
    area = pl.program_id(0)
    order = edge_order()
    piv = p_ref[pl.ds(area, 1), :]
    piv_col = jnp.transpose(jnp.broadcast_to(piv, (128, K)))
    step = 256
    count = K // step
    head = dot(f_ref[0, :, :128], order)
    g[:, :128] = (head * piv_col).astype(BF16)
    f_head = head.astype(BF16)
    for q in range(1, K // 128):
        top = q // 2 * step
        part = f_ref[0, top:, 128 * q : 128 * q + 128].astype(F32)
        g[top:, 128 * q : 128 * q + 128] = (part * piv_col[top:]).astype(BF16)
    for i in range(count):
        at = slice(i * step, (i + 1) * step)
        w = (i + 1) * step
        rows = jnp.concatenate([f_head[at], f_ref[0, at, 128:w]], axis=1)
        ft[:w, at] = jnp.transpose(rows)
    eye = iota((step, step), 0) == iota((step, step), 1)
    fix = piv - piv.astype(BF16).astype(F32)
    fix = jnp.concatenate([pick(fix[:, :128], order), fix[:, 128:]], axis=1)
    edge_m = None
    edge_diag = None
    for i in range(count):
        at = slice(i * step, (i + 1) * step)
        w = (i + 1) * step
        column = dot(ft[:w, i * step :], g[i * step :, at])
        block = column[i * step :]
        diag = jnp.sum(jnp.where(eye, block, 0.0), axis=0, keepdims=True) + fix[:, at]
        diag_ref[pl.ds(area, 1), at] = diag
        block = jnp.where(eye, 0.0, block)
        if i == 0:
            edge_diag = diag[:, :128]
            edge_m = jnp.where(eye, diag, block)[:EDGE, :128]
        m_ref[0, at, at] = block.astype(BF16)
        if i:
            above = column[: i * step].astype(BF16)
            m_ref[0, : i * step, at] = above
            m_ref[0, at, : i * step] = jnp.transpose(above)
    mine = (iota((NB, 128), 1) >> 4) == area
    for r in range(ROWS):
        shift = lax.rem(area * NB + (128 - r * NB), 128)
        for r_in in range(ROWS):
            rows = edge_m[NB * r_in : NB * r_in + NB]
            rows = jnp.where(mine, pltpu.roll(rows, shift, 1), 0.0)
            high = rows.astype(BF16)
            at = pl.ds(pl.multiple_of(ITEMS * r_in + NB * area, NB), NB)
            bdh_ref[at, ITEMS * r : ITEMS * r + ITEMS] = high
            bdl_ref[at, ITEMS * r : ITEMS * r + ITEMS] = (rows - high.astype(F32)).astype(BF16)
    load = load_ref[0]
    load = jnp.concatenate([pick(load[:, :128], order), load[:, 128:]], axis=1)
    c = edge_part(load, m_ref[0, :, :128], edge_diag)

    @pl.when(area == 0)
    def _():
        c_ref[...] = jnp.zeros_like(c_ref)
        for source, out in ((lo_ref, lo_out), (hi_ref, hi_out)):
            out[:, :128] = pick(source[:, :128], order)
            out[:, 128:] = source[:, 128:]

    @pl.when(area < HALF)
    def _():
        load0_ref[0] = load

    @pl.when(area >= HALF)
    def _():
        load1_ref[0] = load

    lane_mine = (iota((S, 128), 1) >> 4) == area
    for r in range(ROWS):
        at = slice(ITEMS * r, ITEMS * r + ITEMS)
        moved = pltpu.roll(c, lax.rem(area * NB + (128 - r * NB), 128), 1)
        c_ref[:, at] = jnp.where(lane_mine, moved, c_ref[:, at])


def load_matrices(m_ref, first, buf, sem):
    copies = [pltpu.make_async_copy(m_ref.at[first + q], buf.at[q], sem.at[q]) for q in range(HALF)]
    for copy in copies:
        copy.start()
    return copies


def right_side_of(b_in, e_ref, q, area):
    group = iota((S, 128), 1) >> 4
    part = jnp.zeros((S, 128), F32)
    for r in range(ROWS):
        piece = e_ref[:, ITEMS * r : ITEMS * r + ITEMS]
        shift = (NB * (r - area)) % 128
        if shift:
            piece = pltpu.roll(piece, shift, 1)
        part = jnp.where(group == r, piece, part)
    base = b_in[q]
    return jnp.concatenate([base[:, :128] + part, base[:, 128:]], axis=1)


def area_kernel(first, m_ref, diag_ref, load_ref, lo_ref, hi_ref, e_ref, w_in, b_in, tie_ref, *refs):
    if first:
        c_in, w_ref, b_ref, c_ref, tie_out, buf, sem = refs
    else:
        w_ref, b_ref, c_ref, tie_out, buf, sem = refs
    copies = load_matrices(m_ref, first, buf, sem)
    sides = [right_side_of(b_in, e_ref, q, first + q) for q in range(HALF)]
    news = []
    for q in range(HALF):
        at = slice(first + q, first + q + 1)
        copies[q].wait()
        x = dot(sides[q].astype(BF16), buf[q]) + sides[q] * diag_ref[at, :]
        moved = x + w_in[q]
        y = jnp.clip(moved, lo_ref[at, :], hi_ref[at, :])
        w = moved - y
        w_ref[q] = w
        b = load_ref[q] + SIGMA * (y - w)
        b_ref[q] = b
        news.append(b)
    group = iota((S, 128), 1) >> 4
    edges = [c_in[:, ITEMS * r : ITEMS * r + ITEMS] if first else jnp.zeros((S, 128), F32) for r in range(ROWS)]
    for q in range(HALF):
        area = first + q
        c = edge_part(news[q], buf[q, :, :128], diag_ref[area : area + 1, :128])
        for r in range(ROWS):
            shift = (NB * (area - r)) % 128
            moved = pltpu.roll(c, shift, 1) if shift else c
            edges[r] = jnp.where(group == area, moved, edges[r])
    for r in range(ROWS):
        c_ref[:, ITEMS * r : ITEMS * r + ITEMS] = edges[r]
    tie_out[...] = edges[0][:8]


def last_kernel(first, m_ref, diag_ref, e_ref, b_in, tie_ref, *refs):
    if first:
        _, x_ref, buf, sem, x_buf, x_sem = refs
    else:
        x_ref, tie_out, buf, sem, x_buf, x_sem = refs
    copies = load_matrices(m_ref, first, buf, sem)
    order = edge_order(True)
    for q in range(HALF):
        area = first + q
        side = right_side_of(b_in, e_ref, q, area)
        copies[q].wait()
        x = dot(side.astype(BF16), buf[q]) + side * diag_ref[area : area + 1, :]
        x_buf[q] = jnp.concatenate([pick(x[:, :128], order), x[:, 128:]], axis=1)
    copy = pltpu.make_async_copy(x_buf, x_ref.at[pl.ds(first, HALF)], x_sem)
    copy.start()
    if not first:
        tie_out[...] = jnp.zeros((8, 128), F32)
    copy.wait()


def on_device(loads, factor, pivots, lower, upper, incidence, counts):
    wide = ROWS * ITEMS
    exchange = lambda x: lax.all_to_all(x, BOTH, split_axis=0, concat_axis=0, tiled=True)
    me = lax.axis_index("region").astype(jnp.int32).reshape(1)
    place, place_t, tags, live = call(
        route_kernel,
        (struct((ITEMS, 256), BF16), struct((256, ITEMS), BF16), struct((2, ITEMS)), struct((1, ITEMS))),
        in_specs=[SMEM, SMEM, VM],
    )(me, counts, incidence)

    area_block = lambda rows: pl.BlockSpec((1, rows, K), lambda a: (a, 0, 0))
    whole = lambda *shape: pl.BlockSpec(shape, lambda a: (0,) * len(shape))
    matrix, diag, c_now, bd_high, bd_low, load0, load1, floor_box, ceil_box = call(
        setup_kernel,
        (
            struct((AREA, K, K), BF16),
            struct((AREA, K)),
            struct((S, wide)),
            struct((wide, wide), BF16),
            struct((wide, wide), BF16),
            struct((HALF, S, K)),
            struct((HALF, S, K)),
            struct((AREA, K)),
            struct((AREA, K)),
        ),
        grid=(AREA,),
        in_specs=[area_block(K), whole(AREA, K), area_block(S), whole(AREA, K), whole(AREA, K)],
        out_specs=(
            area_block(K), whole(AREA, K), whole(S, wide), whole(wide, wide), whole(wide, wide),
            pl.BlockSpec((1, S, K), lambda a: (jnp.minimum(a, HALF - 1), 0, 0)),
            pl.BlockSpec((1, S, K), lambda a: (jnp.maximum(a - HALF, 0), 0, 0)),
            whole(AREA, K), whole(AREA, K),
        ),
        scratch_shapes=[pltpu.VMEM((K, K), BF16), pltpu.VMEM((K, K), BF16)],
        cost_estimate=cost(8 * 10**9, 34 * 2**20),
        limit=40,
    )(factor, pivots, loads, lower, upper)

    send, e, blk, u = call(
        open_kernel,
        (struct((512, 128)), struct((S, wide)), struct((128, 128)), struct((128, 128))),
        in_specs=[VM] * 3,
    )(c_now, place, tags)

    part_shape = struct((HALF, S, K))
    matrix_scratch = [pltpu.VMEM((HALF, K, K), BF16), pltpu.SemaphoreType.DMA((HALF,))]

    def run_areas(first, load, e, w, b, tie, c=None):
        return call(
            functools.partial(area_kernel, first),
            (part_shape, part_shape, struct((S, wide)), struct((8, 128))),
            in_specs=[ANY] + [VM] * (9 if first else 8),
            out_specs=(VM,) * 4,
            scratch_shapes=matrix_scratch,
            input_output_aliases={6: 0, 7: 1},
            cost_estimate=cost(4 * 10**8, 10 * 2**20),
            limit=20,
        )(matrix, diag, load, floor_box, ceil_box, e, w, b, tie, *((c,) if first else ()))

    def run_last(first, e, b, tie, x=None):
        x_shape = struct((AREA, S, K))
        return call(
            functools.partial(last_kernel, first),
            x_shape if first else (x_shape, struct((8, 128))),
            in_specs=[ANY, VM, VM, VM, VM] + ([ANY] if first else []),
            out_specs=ANY if first else (ANY, VM),
            scratch_shapes=matrix_scratch + [pltpu.VMEM((HALF, S, K), F32), pltpu.SemaphoreType.DMA],
            input_output_aliases={5: 0} if first else {},
            cost_estimate=cost(4 * 10**8, 10 * 2**20),
            limit=20,
        )(matrix, diag, e, b, tie, *((x,) if first else ()))

    z_shape = struct((N_REGION, 256))
    rows2 = struct((256, 128))
    rec_shape = struct((128, 128))
    small = cost(10**7, 2**20)
    owner_first = call(
        functools.partial(owner_kernel, True, False),
        (rows2, z_shape, rows2, rec_shape, rows2, z_shape),
        in_specs=[VM] * 2,
        cost_estimate=small,
    )
    owner_mid = call(
        functools.partial(owner_kernel, False, False),
        (rows2, z_shape, rows2, rec_shape),
        in_specs=[SMEM] + [VM] * 7,
        input_output_aliases={5: 1, 6: 2, 7: 3},
        cost_estimate=small,
    )
    owner_last = call(
        functools.partial(owner_kernel, False, True),
        struct((512, 128)),
        in_specs=[SMEM] + [VM] * 7,
        cost_estimate=small,
    )
    run_slots = call(
        slot_kernel,
        (rows2, struct((S, wide)), struct((128, 128)), struct((128, 128))),
        in_specs=[VM] * 9,
        input_output_aliases={4: 2, 5: 3},
        cost_estimate=cost(10**8, 3 * 2**20),
    )

    def iterate(step, state):
        send, e, blk, u, z, u_far, rec, w0, b0, w1, b1 = state[:11]
        got = exchange(send)
        w0, b0, c, tie = run_areas(0, load0, e, w0, b0, z)
        if step is None:
            back, z, u_far, rec, tags_at, inverse = owner_first(got, tie)
        else:
            tags_at, inverse = state[11:]
            at = jnp.asarray(step, jnp.int32).reshape(1)
            back, z, u_far, rec = owner_mid(at, got, tags_at, inverse, tie, z, u_far, rec)
        z_back = exchange(back)
        w1, b1, c, _ = run_areas(HALF, load1, e, w1, b1, z, c)
        send, e, blk, u = run_slots(z_back, place, place_t, live, blk, u, c, bd_high, bd_low)
        return (send, e, blk, u, z, u_far, rec, w0, b0, w1, b1, tags_at, inverse)

    zero = jnp.zeros((HALF, S, K), F32)
    state = (send, e, blk, u, jnp.zeros((N_REGION, 256), F32), None, None, zero, load0, zero, load1)
    state = iterate(None, state)
    state = lax.fori_loop(1, ITERS - 1, iterate, state)
    send, e, blk, u, z, u_far, rec, _, b0, _, b1, tags_at, inverse = state
    got = exchange(send)
    x, tie = run_last(0, e, b0, z)
    back = owner_last(
        jnp.full((1,), ITERS - 1, jnp.int32), got, tags_at, inverse, tie, z, u_far, rec
    )
    z_back = exchange(back)
    x = run_last(HALF, e, b1, back, x)
    duals, record = call(
        close_kernel, (struct((128, 128)), struct((ITERS, 2))), in_specs=[VM] * 5
    )(z_back, place_t, live, blk, u)
    return (x, duals.reshape(AREA, NB, 128), record)


def solution(mesh):
    area_split = (
        P(BOTH, None, None),
        P(BOTH, None, None),
        P(BOTH, None),
        P(BOTH, None),
        P(BOTH, None),
        P(BOTH, None),
        P(BOTH),
    )
    return jax.shard_map(
        on_device,
        mesh=mesh,
        in_specs=area_split,
        out_specs=(P(BOTH, None, None), P(BOTH, None, None), P()),
        check_vma=False,
    )
```

```python
import functools

import jax
import jax.numpy as jnp
from jax import lax
from jax.experimental import pallas as pl
from jax.experimental.pallas import tpu as pltpu
from jax.sharding import PartitionSpec as P

K = 1024
S = 32
AREA = 8
NB = 16
ITEMS = AREA * NB
ROWS = 4
EDGE = NB * ROWS
CAP = 8
N_REGION = 8
N_DEV = 16
WORLD = N_REGION * N_DEV
BUS_DEV = 16
ITERS = 14
RHO = 4.0
SIGMA = 1.0
HALF = AREA // 2
CELLS = 1024.0 * 128.0
BOTH = ("region", "dev")
F32 = jnp.float32
BF16 = jnp.bfloat16


def dot(left, right):
    return jnp.dot(left, right, preferred_element_type=F32)


def split3(x):
    high = x.astype(BF16)
    rest = x - high.astype(F32)
    middle = rest.astype(BF16)
    low = (rest - middle.astype(F32)).astype(BF16)
    return high, middle, low


def pick(x, onehot):
    count = x.shape[0]
    got = dot(jnp.concatenate(split3(x), axis=0), onehot)
    return got[:count] + got[count : 2 * count] + got[2 * count :]


def iota(shape, dim):
    return lax.broadcasted_iota(jnp.int32, shape, dim)


def edge_order(transposed=False):
    old = iota((128, 128), 1 if transposed else 0)
    new = iota((128, 128), 0 if transposed else 1)
    target = jnp.where(old < EDGE, (old & 3) * NB + (old >> 2), old)
    return jnp.where(new == target, 1.0, 0.0).astype(BF16)


def struct(shape, dtype=F32):
    return jax.ShapeDtypeStruct(shape, dtype)


def cost(flops, nbytes):
    return pl.CostEstimate(flops=flops, bytes_accessed=nbytes, transcendentals=0)


SMEM = pl.BlockSpec(memory_space=pltpu.SMEM)
VM = pl.BlockSpec(memory_space=pltpu.VMEM)
HBM = pl.BlockSpec(memory_space=pltpu.HBM)


def call(kernel, out_shape, limit=16, **kw):
    return pl.pallas_call(
        kernel,
        out_shape=out_shape,
        compiler_params=pltpu.CompilerParams(vmem_limit_bytes=limit * 2**20),
        **kw,
    )


def route_kernel(me_ref, counts_ref, inc_ref, p_ref, pt_ref, tag_ref, live_ref):
    me = me_ref[0]
    lane = iota((ITEMS, ITEMS), 1)
    sub = iota((ITEMS, ITEMS), 0)
    area_of = iota((1, ITEMS), 1) >> 4
    wide = jnp.concatenate([inc_ref[...].astype(F32), jnp.zeros((AREA, 112), F32)], axis=1)
    ids = jnp.zeros((1, ITEMS), F32)
    count = jnp.zeros((1, ITEMS), jnp.int32)
    for a in range(AREA):
        row = wide[a : a + 1, :]
        if a:
            row = pltpu.roll(row, NB * a, 1)
        ids = jnp.where(area_of == a, row, ids)
        count = jnp.where(area_of == a, counts_ref[a], count)
    live = (iota((1, ITEMS), 1) & 15) < count
    live_ref[...] = jnp.where(live, 1.0, 0.0)
    bus = ids.astype(jnp.int32)
    region = bus >> 8
    peer = (bus >> 4) & 15
    key_r = jnp.where(live, jnp.where(region == me, peer, 16 + region), -1).astype(F32)
    key_c = jnp.transpose(jnp.broadcast_to(key_r, (ITEMS, ITEMS)))
    local_c = jnp.transpose(jnp.broadcast_to((bus & 15).astype(F32), (ITEMS, ITEMS)))
    same = (key_c == key_r) & (key_r >= 0.0)
    rank_c = jnp.sum(jnp.where(same & (lane < sub), 1.0, 0.0), axis=1, keepdims=True)
    rank_r = jnp.sum(jnp.where(same & (sub < lane), 1.0, 0.0), axis=0, keepdims=True)

    def place(key, rank):
        far = ITEMS + rank * N_REGION + key - 16.0
        return jnp.where(key < 0.0, -1.0, jnp.where(key < 16.0, rank * N_DEV + key, far))

    place_c = place(key_c, jnp.broadcast_to(rank_c, (ITEMS, ITEMS)))
    place_c = jnp.concatenate([place_c, place_c], axis=1)
    local_c = jnp.concatenate([local_c, local_c], axis=1)
    hit = iota((ITEMS, 256), 1).astype(F32) == place_c
    p_ref[...] = jnp.where(hit, 1.0, 0.0).astype(BF16)
    hit_t = iota((256, ITEMS), 0).astype(F32) == place(key_r, rank_r)
    pt_ref[...] = jnp.where(hit_t, 1.0, 0.0).astype(BF16)
    tag = jnp.sum(jnp.where(hit, local_c + 1.0, 0.0), axis=0, keepdims=True) - 1.0
    tag_ref[0:1, :] = tag[:, :128]
    tag_ref[1:2, :] = tag[:, 128:]


def near_rows(width, dev):
    return pl.ds(width * dev, N_REGION, stride=width * N_DEV)


def far_rows(width, region):
    return pl.ds(width * N_DEV * region + 1, N_DEV, stride=width)


def bus_sums(near, far, near_tags, far_tags):
    group = iota((N_REGION, 128), 1) >> 4
    halves = []
    for half in range(2):
        total = jnp.zeros((N_REGION, 128), F32)
        for low in range(8):
            bus = 8.0 * half + low
            acc = jnp.zeros((N_REGION, 128), F32)
            for dev in range(N_DEV):
                acc = acc + jnp.where(near_tags[dev] == bus, near[dev], 0.0)
            for shift in (16, 32, 64):
                acc = acc + pltpu.roll(acc, shift, 1)
            total = jnp.where(group == low, acc, total)
        rows = []
        for low in range(8):
            bus = 8.0 * half + low
            acc = jnp.zeros((N_DEV, 128), F32)
            for region in range(N_REGION):
                acc = acc + jnp.where(far_tags[region] == bus, far[region], 0.0)
            rows.append(acc)
        turned = jnp.transpose(jnp.concatenate(rows, axis=0))
        for c in range(CAP):
            total = total + turned[8 * c : 8 * c + 8]
        halves.append(total)
    return jnp.concatenate(halves, axis=1)


def owner_kernel(first, last, *refs):
    if first:
        got_ref, tie_ref, out_ref, z_ref, u_ref, rec_ref, tag_ref, inv_ref = refs
        near_tags = [got_ref[pl.ds(4 * d + 2, N_REGION, stride=4 * N_DEV), :] for d in range(N_DEV)]
        far_tags = [
            got_ref[pl.ds(4 * N_DEV * r + 3, N_DEV, stride=4), :] for r in range(N_REGION)
        ]
        one_n = jnp.ones((N_REGION, 128), F32)
        one_f = jnp.ones((N_DEV, 128), F32)
        counts = bus_sums([one_n] * N_DEV, [one_f] * N_REGION, near_tags, far_tags)
        inverse = 1.0 / jnp.maximum(counts, 1.0)
        inv_ref[...] = inverse
        for d in range(N_DEV):
            tag_ref[near_rows(2, d), :] = near_tags[d]
        for r in range(N_REGION):
            tag_ref[far_rows(2, r), :] = far_tags[r]
        rec_ref[...] = jnp.zeros((32, 128), F32)
        step = 0
    else:
        if last:
            step_ref, got_ref, tag_ref, inv_ref, tie_ref, prev_ref, u_in, rec_in, out_ref = refs
        else:
            (step_ref, got_ref, tag_ref, inv_ref, tie_ref, prev_ref, u_in, rec_in,
             out_ref, z_ref, u_ref, rec_ref) = refs
        near_tags = [tag_ref[near_rows(2, d), :] for d in range(N_DEV)]
        far_tags = [tag_ref[far_rows(2, r), :] for r in range(N_REGION)]
        inverse = inv_ref[...]
        step = step_ref[0]
    wide_in = 4 if first else 2
    wide_out = 4 if last else 2
    near = [got_ref[near_rows(wide_in, d), :] for d in range(N_DEV)]
    far = [got_ref[far_rows(wide_in, r), :] for r in range(N_REGION)]
    z = bus_sums(near, far, near_tags, far_tags) * inverse
    change = z if first else z - prev_ref[...]
    change = change * change
    dual = jnp.sum(change[:, :128] + change[:, 128:], axis=0, keepdims=True) * (RHO * RHO / CELLS)
    group = iota((N_REGION, 128), 1) >> 4
    spread = []
    turned = []
    for half in range(2):
        part = z[:, 128 * half : 128 * half + 128]
        for low in range(8):
            one = jnp.where(group == low, part, 0.0)
            for shift in (16, 32, 64):
                one = one + pltpu.roll(one, shift, 1)
            spread.append(one)
        turned.append(jnp.transpose(jnp.concatenate([part] * 16, axis=0)))
    primal = jnp.zeros((N_REGION, 128), F32)
    for dev in range(N_DEV):
        val = jnp.zeros((N_REGION, 128), F32)
        for bus in range(BUS_DEV):
            val = jnp.where(near_tags[dev] == float(bus), spread[bus], val)
        out_ref[near_rows(wide_out, dev), :] = val
        u = near[dev] - val
        gap = u if first else u - u_in[near_rows(2, dev), :]
        primal = primal + gap * gap
        if not last:
            u_ref[near_rows(2, dev), :] = u
    for region in range(N_REGION):
        val = jnp.zeros((N_DEV, 128), F32)
        for bus in range(BUS_DEV):
            low = bus % 8
            one = turned[bus // 8][16 * low : 16 * low + 16]
            val = jnp.where(far_tags[region] == float(bus), one, val)
        out_ref[far_rows(wide_out, region), :] = val
        u = far[region] - val
        gap = u if first else u - u_in[far_rows(2, region), :]
        square = gap * gap
        primal = primal + square[:8] + square[8:]
        if not last:
            u_ref[far_rows(2, region), :] = u
    primal = jnp.sum(primal, axis=0, keepdims=True) * (1.0 / CELLS)
    row = iota((32, 128), 0)
    if last:
        rec = jnp.where(row == step, primal, rec_in[...])
        rec = jnp.where(row == 16 + step, dual, rec)
        rec = jnp.concatenate([rec, jnp.zeros((96, 128), F32)], axis=0)
        sums = jnp.sum(jnp.transpose(rec), axis=0, keepdims=True)
        out_ref[pl.ds(2, WORLD, stride=4), :] = jnp.broadcast_to(sums, (WORLD, 128))
        out_ref[pl.ds(3, WORLD, stride=4), :] = jnp.zeros((WORLD, 128), F32)
    else:
        if not first:
            rec_ref[...] = rec_in[...]
        rec_ref[pl.ds(step, 1), :] = primal
        rec_ref[pl.ds(16 + step, 1), :] = dual
        z_ref[...] = z


def by_lane(rows):
    return jnp.concatenate([rows[S * r : S * r + S] for r in range(ROWS)], axis=1)


def by_row(lanes):
    return jnp.concatenate([lanes[:, ITEMS * r : ITEMS * r + ITEMS] for r in range(ROWS)], axis=0)


def open_kernel(c_ref, p_ref, tag_ref, send_ref, e_ref, val_ref):
    val = by_row(c_ref[...])
    val_ref[...] = val
    e_ref[...] = jnp.zeros((S, ROWS * ITEMS), F32)
    send = pick(val, p_ref[...])
    send_ref[pl.ds(0, WORLD, stride=4), :] = send[:, :128]
    send_ref[pl.ds(1, WORLD, stride=4), :] = send[:, 128:]
    send_ref[pl.ds(2, WORLD, stride=4), :] = jnp.broadcast_to(tag_ref[0:1, :], (WORLD, 128))
    send_ref[pl.ds(3, WORLD, stride=4), :] = jnp.broadcast_to(tag_ref[1:2, :], (WORLD, 128))


def take_means(z_ref, pt_ref, width):
    near = z_ref[pl.ds(0, WORLD, stride=width), :]
    far = z_ref[pl.ds(1, WORLD, stride=width), :]
    return pick(jnp.concatenate([near, far], axis=1), pt_ref[...])


def slot_kernel(
    z_ref, p_ref, pt_ref, live_ref, val_in, c_ref, bd_ref, bdiag_ref, send_ref, e_ref, val_ref
):
    z_slot = take_means(z_ref, pt_ref, 2)
    u = val_in[...] * live_ref[...] - z_slot
    e = by_lane(RHO * (z_slot - u))
    e_ref[...] = e
    e_high = e.astype(BF16)
    e_low = (e - e_high.astype(F32)).astype(BF16)
    both = dot(jnp.concatenate([e_high, e_low], axis=0), bd_ref[...])
    edge = c_ref[...] + e * bdiag_ref[...] + both[:S] + both[S:]
    val = by_row(edge) + u
    val_ref[...] = val
    send = pick(val, p_ref[...])
    send_ref[pl.ds(0, WORLD, stride=2), :] = send[:, :128]
    send_ref[pl.ds(1, WORLD, stride=2), :] = send[:, 128:]


def close_kernel(z_ref, pt_ref, live_ref, val_in, dual_ref, record_ref):
    z_slot = take_means(z_ref, pt_ref, 4)
    u = val_in[...] * live_ref[...] - z_slot
    old = iota((128, 128), 0)
    order = jnp.where(iota((128, 128), 1) == (old & 31) * ROWS + (old >> 5), 1.0, 0.0)
    dual_ref[...] = pick(jnp.transpose(u), order.astype(BF16))
    sums = jnp.sum(z_ref[pl.ds(2, WORLD, stride=4), :], axis=0, keepdims=True)
    both = jnp.concatenate([sums, pltpu.roll(sums, 112, 1)], axis=0)
    record_ref[...] = both[:, :ITERS]


def edge_part(right_side, m_edge, diag_edge):
    return dot(right_side.astype(BF16), m_edge) + right_side[:, :128] * diag_edge


def setup_kernel(
    f_ref, p_hbm, load_hbm, lo_hbm, hi_hbm,
    m_ref, diag_ref, c_ref, bd_ref, bdiag_ref, load_out, lo_out, hi_out,
    ft, g, p_ref, loads, lo_ref, hi_ref, sem,
):
    area = pl.program_id(0)
    order = edge_order()
    fetch = [
        pltpu.make_async_copy(source, target, sem.at[n])
        for n, (source, target) in enumerate(
            ((p_hbm, p_ref), (load_hbm, loads), (lo_hbm, lo_ref), (hi_hbm, hi_ref))
        )
    ]

    @pl.when(area == 0)
    def _():
        for copy in fetch:
            copy.start()
        for copy in fetch:
            copy.wait()

    piv = p_ref[pl.ds(area, 1), :]
    piv_col = jnp.transpose(jnp.broadcast_to(piv, (128, K)))
    step = 256
    count = K // step
    head = dot(f_ref[0, :, :128], order)
    g[:, :128] = (head * piv_col).astype(BF16)
    f_head = head.astype(BF16)
    for q in range(1, K // 128):
        top = q // 2 * step
        part = f_ref[0, top:, 128 * q : 128 * q + 128].astype(F32)
        g[top:, 128 * q : 128 * q + 128] = (part * piv_col[top:]).astype(BF16)
    for i in range(count):
        at = slice(i * step, (i + 1) * step)
        w = (i + 1) * step
        rows = jnp.concatenate([f_head[at], f_ref[0, at, 128:w]], axis=1)
        ft[:w, at] = jnp.transpose(rows)
    eye = iota((step, step), 0) == iota((step, step), 1)
    fix = piv - piv.astype(BF16).astype(F32)
    fix = jnp.concatenate([pick(fix[:, :128], order), fix[:, 128:]], axis=1)
    edge_m = None
    edge_diag = None
    for i in range(count):
        at = slice(i * step, (i + 1) * step)
        w = (i + 1) * step
        column = dot(ft[:w, i * step :], g[i * step :, at])
        block = column[i * step :]
        diag = jnp.sum(jnp.where(eye, block, 0.0), axis=0, keepdims=True) + fix[:, at]
        diag_ref[pl.ds(area, 1), at] = diag
        block = jnp.where(eye, 0.0, block)
        if i == 0:
            edge_diag = diag[:, :128]
            edge_m = block[:EDGE, :128]
        m_ref[0, at, at] = block.astype(BF16)
        if i:
            above = column[: i * step].astype(BF16)
            m_ref[0, : i * step, at] = above
            m_ref[0, at, : i * step] = jnp.transpose(above)
    mine = (iota((NB, 128), 1) >> 4) == area
    for r in range(ROWS):
        shift = lax.rem(area * NB + (128 - r * NB), 128)
        for r_in in range(ROWS):
            rows = edge_m[NB * r_in : NB * r_in + NB]
            rows = jnp.where(mine, pltpu.roll(rows, shift, 1), 0.0)
            at = pl.ds(pl.multiple_of(ITEMS * r_in + NB * area, NB), NB)
            bd_ref[at, ITEMS * r : ITEMS * r + ITEMS] = rows.astype(BF16)
    load = loads[area]
    load = jnp.concatenate([pick(load[:, :128], order), load[:, 128:]], axis=1)
    load_out[0] = load
    c = edge_part(load, m_ref[0, :, :128], edge_diag)

    @pl.when(area == 0)
    def _():
        c_ref[...] = jnp.zeros_like(c_ref)
        bdiag_ref[...] = jnp.zeros_like(bdiag_ref)
        for source, out in ((lo_ref, lo_out), (hi_ref, hi_out)):
            out[:, :128] = pick(source[:, :128], order)
            out[:, 128:] = source[:, 128:]

    lane_mine = (iota((S, 128), 1) >> 4) == area
    for r in range(ROWS):
        at = slice(ITEMS * r, ITEMS * r + ITEMS)
        moved = pltpu.roll(c, lax.rem(area * NB + (128 - r * NB), 128), 1)
        c_ref[:, at] = jnp.where(lane_mine, moved, c_ref[:, at])
        moved = pltpu.roll(edge_diag, lax.rem(area * NB + (128 - r * NB), 128), 1)
        bdiag_ref[:, at] = jnp.where(lane_mine[:1], moved, bdiag_ref[:, at])


def fetch_areas(first, m_ref, buf, sem):
    half = K // 2
    copies = [
        [
            pltpu.make_async_copy(
                m_ref.at[first + q, pl.ds(half * n, half)],
                buf.at[q, pl.ds(half * n, half)],
                sem.at[q, n],
            )
            for n in range(2)
        ]
        for q in range(HALF)
    ]
    for group in copies:
        for copy in group:
            copy.start()
    return copies


def product(first, q, copies, buf, load_ref, diag_ref, lo_ref, hi_ref, e_ref, moved_in):
    area = first + q
    at = slice(area, area + 1)
    group = iota((S, 128), 1) >> 4
    part = jnp.zeros((S, 128), F32)
    for r in range(ROWS):
        piece = e_ref[:, ITEMS * r : ITEMS * r + ITEMS]
        shift = (NB * (r - area)) % 128
        if shift:
            piece = pltpu.roll(piece, shift, 1)
        part = jnp.where(group == r, piece, part)
    moved = moved_in[q]
    y = jnp.clip(moved, lo_ref[at, :], hi_ref[at, :])
    w = moved - y
    base = load_ref[area] + SIGMA * (y - w)
    side = jnp.concatenate([base[:, :128] + part, base[:, 128:]], axis=1)
    rounded = side.astype(BF16)
    half = K // 2
    copies[q][0].wait()
    x = side * diag_ref[at, :] + dot(rounded[:, :half], buf[q, :half])
    copies[q][1].wait()
    return x + dot(rounded[:, half:], buf[q, half:]), w


def area_kernel(
    first, m_ref, load_ref, diag_ref, lo_ref, hi_ref, e_ref, moved_in, tie_ref, *refs
):
    if first:
        c_in, moved_ref, c_ref, buf, sem = refs
    else:
        moved_ref, c_ref, tie_out, buf, sem = refs
    copies = fetch_areas(first, m_ref, buf, sem)
    group = iota((S, 128), 1) >> 4
    edges = [
        c_in[:, ITEMS * r : ITEMS * r + ITEMS] if first else jnp.zeros((S, 128), F32)
        for r in range(ROWS)
    ]
    news = []
    for q in range(HALF + 1):
        if q < HALF:
            at = slice(first + q, first + q + 1)
            x, w = product(first, q, copies, buf, load_ref, diag_ref, lo_ref, hi_ref, e_ref, moved_in)
            moved = x + w
            moved_ref[q] = moved
            y = jnp.clip(moved, lo_ref[at, :], hi_ref[at, :])
            news.append(load_ref[first + q] + SIGMA * (y - (moved - y)))
        if q > 0:
            area = first + q - 1
            diag = diag_ref[area : area + 1, :128]
            c = edge_part(news[q - 1], buf[q - 1, :, :128], diag)
            for r in range(ROWS):
                shift = (NB * (area - r)) % 128
                turned = pltpu.roll(c, shift, 1) if shift else c
                edges[r] = jnp.where(group == area, turned, edges[r])
    for r in range(ROWS):
        c_ref[:, ITEMS * r : ITEMS * r + ITEMS] = edges[r]
    if not first:
        tie_out[...] = edges[0][:8]


def last_kernel(
    first, m_ref, load_ref, diag_ref, lo_ref, hi_ref, e_ref, moved_in, tie_ref, *refs
):
    if first:
        _, x_ref, buf, sem, x_buf, x_sem = refs
    else:
        x_ref, tie_out, buf, sem, x_buf, x_sem = refs
    copies = fetch_areas(first, m_ref, buf, sem)
    order = edge_order(True)
    writes = []
    for q in range(HALF):
        x, _ = product(first, q, copies, buf, load_ref, diag_ref, lo_ref, hi_ref, e_ref, moved_in)
        x_buf[q] = jnp.concatenate([pick(x[:, :128], order), x[:, 128:]], axis=1)
        writes.append(pltpu.make_async_copy(x_buf.at[q], x_ref.at[first + q], x_sem.at[q]))
        writes[-1].start()
    if not first:
        tie_out[...] = jnp.zeros((8, 128), F32)
    for copy in writes:
        copy.wait()


def on_device(loads, factor, pivots, lower, upper, incidence, counts):
    wide = ROWS * ITEMS
    exchange = lambda x: lax.all_to_all(x, BOTH, split_axis=0, concat_axis=0, tiled=True)
    me = lax.axis_index("region").astype(jnp.int32).reshape(1)
    place, place_t, tags, live = call(
        route_kernel,
        (struct((ITEMS, 256), BF16), struct((256, ITEMS), BF16), struct((2, ITEMS)), struct((1, ITEMS))),
        in_specs=[SMEM, SMEM, VM],
    )(me, counts, incidence)

    area_block = lambda rows: pl.BlockSpec((1, rows, K), lambda a: (a, 0, 0))
    whole = lambda *shape: pl.BlockSpec(shape, lambda a: (0,) * len(shape))
    matrix, diag, c_now, bd, bd_diag, load, floor_box, ceil_box = call(
        setup_kernel,
        (
            struct((AREA, K, K), BF16),
            struct((AREA, K)),
            struct((S, wide)),
            struct((wide, wide), BF16),
            struct((1, wide)),
            struct((AREA, S, K)),
            struct((AREA, K)),
            struct((AREA, K)),
        ),
        grid=(AREA,),
        in_specs=[area_block(K), HBM, HBM, HBM, HBM],
        out_specs=(
            area_block(K), whole(AREA, K), whole(S, wide), whole(wide, wide), whole(1, wide),
            area_block(S), whole(AREA, K), whole(AREA, K),
        ),
        scratch_shapes=[
            pltpu.VMEM((K, K), BF16),
            pltpu.VMEM((K, K), BF16),
            pltpu.VMEM((AREA, K), F32),
            pltpu.VMEM((AREA, S, K), F32),
            pltpu.VMEM((AREA, K), F32),
            pltpu.VMEM((AREA, K), F32),
            pltpu.SemaphoreType.DMA((4,)),
        ],
        cost_estimate=cost(8 * 10**9, 34 * 2**20),
        limit=60,
    )(factor, pivots, loads, lower, upper)

    send, e, val = call(
        open_kernel,
        (struct((512, 128)), struct((S, wide)), struct((128, 128))),
        in_specs=[VM] * 3,
    )(c_now, place, tags)

    part_shape = struct((HALF, S, K))
    scratch = [
        pltpu.VMEM((HALF, K, K), BF16),
        pltpu.SemaphoreType.DMA((HALF, 2)),
    ]

    def run_areas(first, e, moved, tie, c=None):
        return call(
            functools.partial(area_kernel, first),
            (part_shape, struct((S, wide))) + (() if first else (struct((8, 128)),)),
            in_specs=[HBM] + [VM] * (8 if first else 7),
            out_specs=(VM,) * (2 if first else 3),
            scratch_shapes=scratch,
            input_output_aliases={6: 0},
            cost_estimate=cost(4 * 10**8, 10 * 2**20),
            limit=20,
        )(matrix, load, diag, floor_box, ceil_box, e, moved, tie, *((c,) if first else ()))

    def run_last(first, e, moved, tie, x=None):
        x_shape = struct((AREA, S, K))
        return call(
            functools.partial(last_kernel, first),
            x_shape if first else (x_shape, struct((8, 128))),
            in_specs=[HBM] + [VM] * 7 + ([HBM] if first else []),
            out_specs=HBM if first else (HBM, VM),
            scratch_shapes=scratch
            + [pltpu.VMEM((HALF, S, K), F32), pltpu.SemaphoreType.DMA((HALF,))],
            input_output_aliases={8: 0} if first else {},
            cost_estimate=cost(4 * 10**8, 10 * 2**20),
            limit=20,
        )(matrix, load, diag, floor_box, ceil_box, e, moved, tie, *((x,) if first else ()))

    z_shape = struct((N_REGION, 256))
    rows2 = struct((256, 128))
    rec_shape = struct((32, 128))
    small = cost(10**7, 2**20)
    owner_first = call(
        functools.partial(owner_kernel, True, False),
        (rows2, z_shape, rows2, rec_shape, rows2, z_shape),
        in_specs=[VM] * 2,
        cost_estimate=small,
    )
    owner_mid = call(
        functools.partial(owner_kernel, False, False),
        (rows2, z_shape, rows2, rec_shape),
        in_specs=[SMEM] + [VM] * 7,
        input_output_aliases={5: 1, 6: 2, 7: 3},
        cost_estimate=small,
    )
    owner_last = call(
        functools.partial(owner_kernel, False, True),
        struct((512, 128)),
        in_specs=[SMEM] + [VM] * 7,
        cost_estimate=small,
    )
    run_slots = call(
        slot_kernel,
        (rows2, struct((S, wide)), struct((128, 128))),
        in_specs=[VM] * 8,
        input_output_aliases={4: 2},
        cost_estimate=cost(10**8, 3 * 2**20),
    )

    def iterate(step, state):
        send, e, val, z, u_far, rec, moved0, moved1 = state[:8]
        got = exchange(send)
        moved0, c, tie = run_areas(0, e, moved0, z)
        if step is None:
            back, z, u_far, rec, tags_at, inverse = owner_first(got, tie)
        else:
            tags_at, inverse = state[8:]
            at = jnp.asarray(step, jnp.int32).reshape(1)
            back, z, u_far, rec = owner_mid(at, got, tags_at, inverse, tie, z, u_far, rec)
        z_back = exchange(back)
        moved1, c = run_areas(HALF, e, moved1, z, c)
        send, e, val = run_slots(z_back, place, place_t, live, val, c, bd, bd_diag)
        return (send, e, val, z, u_far, rec, moved0, moved1, tags_at, inverse)

    zero = jnp.zeros((HALF, S, K), F32)
    state = (send, e, val, jnp.zeros((N_REGION, 256), F32), None, None, zero, zero)
    state = iterate(None, state)
    state = lax.fori_loop(1, ITERS - 1, iterate, state)
    send, e, val, z, u_far, rec, moved0, moved1, tags_at, inverse = state
    got = exchange(send)
    x, tie = run_last(0, e, moved0, z)
    back = owner_last(
        jnp.full((1,), ITERS - 1, jnp.int32), got, tags_at, inverse, tie, z, u_far, rec
    )
    z_back = exchange(back)
    x = run_last(HALF, e, moved1, back, x)
    duals, record = call(
        close_kernel, (struct((128, 128)), struct((2, ITERS))), in_specs=[VM] * 4
    )(z_back, place_t, live, val)
    return (x, duals.reshape(AREA, NB, 128), record.T)


def solution(mesh):
    area_split = (
        P(BOTH, None, None),
        P(BOTH, None, None),
        P(BOTH, None),
        P(BOTH, None),
        P(BOTH, None),
        P(BOTH, None),
        P(BOTH),
    )
    return jax.shard_map(
        on_device,
        mesh=mesh,
        in_specs=area_split,
        out_specs=(P(BOTH, None, None), P(BOTH, None, None), P()),
        check_vma=False,
    )
```

```python
import functools

import jax
import jax.numpy as jnp
from jax import lax
from jax.experimental import pallas as pl
from jax.experimental.pallas import tpu as pltpu
from jax.sharding import PartitionSpec as P

K = 1024
S = 32
AREA = 8
NB = 16
ITEMS = AREA * NB
ROWS = 4
EDGE = NB * ROWS
CAP = 8
N_REGION = 8
N_DEV = 16
WORLD = N_REGION * N_DEV
BUS_DEV = 16
ITERS = 14
RHO = 4.0
SIGMA = 1.0
HALF = AREA // 2
CELLS = 1024.0 * 128.0
BOTH = ("region", "dev")
F32 = jnp.float32
BF16 = jnp.bfloat16


def dot(left, right):
    return jnp.dot(left, right, preferred_element_type=F32)


def split3(x):
    high = x.astype(BF16)
    rest = x - high.astype(F32)
    middle = rest.astype(BF16)
    low = (rest - middle.astype(F32)).astype(BF16)
    return high, middle, low


def pick(x, onehot):
    count = x.shape[0]
    got = dot(jnp.concatenate(split3(x), axis=0), onehot)
    return got[:count] + got[count : 2 * count] + got[2 * count :]


def iota(shape, dim):
    return lax.broadcasted_iota(jnp.int32, shape, dim)


def edge_order(transposed=False):
    old = iota((128, 128), 1 if transposed else 0)
    new = iota((128, 128), 0 if transposed else 1)
    target = jnp.where(old < EDGE, (old & 3) * NB + (old >> 2), old)
    return jnp.where(new == target, 1.0, 0.0).astype(BF16)


def struct(shape, dtype=F32):
    return jax.ShapeDtypeStruct(shape, dtype)


def cost(flops, nbytes):
    return pl.CostEstimate(flops=flops, bytes_accessed=nbytes, transcendentals=0)


SMEM = pl.BlockSpec(memory_space=pltpu.SMEM)
VM = pl.BlockSpec(memory_space=pltpu.VMEM)
HBM = pl.BlockSpec(memory_space=pltpu.HBM)


def call(kernel, out_shape, limit=16, **kw):
    return pl.pallas_call(
        kernel,
        out_shape=out_shape,
        compiler_params=pltpu.CompilerParams(vmem_limit_bytes=limit * 2**20),
        **kw,
    )


def route(me_ref, counts_ref, inc_ref, p_ref, pt_ref, tag_ref, live_ref):
    me = me_ref[0]
    lane = iota((ITEMS, ITEMS), 1)
    sub = iota((ITEMS, ITEMS), 0)
    area_of = iota((1, ITEMS), 1) >> 4
    wide = jnp.concatenate([inc_ref[...].astype(F32), jnp.zeros((AREA, 112), F32)], axis=1)
    ids = jnp.zeros((1, ITEMS), F32)
    count = jnp.zeros((1, ITEMS), jnp.int32)
    for a in range(AREA):
        row = wide[a : a + 1, :]
        if a:
            row = pltpu.roll(row, NB * a, 1)
        ids = jnp.where(area_of == a, row, ids)
        count = jnp.where(area_of == a, counts_ref[a], count)
    live = (iota((1, ITEMS), 1) & 15) < count
    live_ref[...] = jnp.where(live, 1.0, 0.0)
    bus = ids.astype(jnp.int32)
    region = bus >> 8
    peer = (bus >> 4) & 15
    key_r = jnp.where(live, jnp.where(region == me, peer, 16 + region), -1).astype(F32)
    key_c = jnp.transpose(jnp.broadcast_to(key_r, (ITEMS, ITEMS)))
    local_c = jnp.transpose(jnp.broadcast_to((bus & 15).astype(F32), (ITEMS, ITEMS)))
    same = (key_c == key_r) & (key_r >= 0.0)
    rank_c = jnp.sum(jnp.where(same & (lane < sub), 1.0, 0.0), axis=1, keepdims=True)
    rank_r = jnp.sum(jnp.where(same & (sub < lane), 1.0, 0.0), axis=0, keepdims=True)

    def place(key, rank):
        far = ITEMS + rank * N_REGION + key - 16.0
        return jnp.where(key < 0.0, -1.0, jnp.where(key < 16.0, rank * N_DEV + key, far))

    place_c = place(key_c, jnp.broadcast_to(rank_c, (ITEMS, ITEMS)))
    place_c = jnp.concatenate([place_c, place_c], axis=1)
    local_c = jnp.concatenate([local_c, local_c], axis=1)
    hit = iota((ITEMS, 256), 1).astype(F32) == place_c
    p_ref[...] = jnp.where(hit, 1.0, 0.0).astype(BF16)
    hit_t = iota((256, ITEMS), 0).astype(F32) == place(key_r, rank_r)
    pt_ref[...] = jnp.where(hit_t, 1.0, 0.0).astype(BF16)
    tag = jnp.sum(jnp.where(hit, local_c + 1.0, 0.0), axis=0, keepdims=True) - 1.0
    tag_ref[0:1, :] = tag[:, :128]
    tag_ref[1:2, :] = tag[:, 128:]


def near_rows(width, dev):
    return pl.ds(width * dev, N_REGION, stride=width * N_DEV)


def far_rows(width, region):
    return pl.ds(width * N_DEV * region + 1, N_DEV, stride=width)


def near_tile(dev):
    return pl.ds(N_REGION * dev, N_REGION)


def far_tile(region):
    return pl.ds(WORLD + N_DEV * region, N_DEV)


def bus_sums(near, far, near_tags, far_tags):
    group = iota((N_REGION, 128), 1) >> 4
    halves = []
    for half in range(2):
        total = jnp.zeros((N_REGION, 128), F32)
        for low in range(8):
            bus = 8.0 * half + low
            acc = jnp.zeros((N_REGION, 128), F32)
            for dev in range(N_DEV):
                acc = acc + jnp.where(near_tags[dev] == bus, near[dev], 0.0)
            for shift in (16, 32, 64):
                acc = acc + pltpu.roll(acc, shift, 1)
            total = jnp.where(group == low, acc, total)
        rows = []
        for low in range(8):
            bus = 8.0 * half + low
            acc = jnp.zeros((N_DEV, 128), F32)
            for region in range(N_REGION):
                acc = acc + jnp.where(far_tags[region] == bus, far[region], 0.0)
            rows.append(acc)
        turned = jnp.transpose(jnp.concatenate(rows, axis=0))
        for c in range(CAP):
            total = total + turned[8 * c : 8 * c + 8]
        halves.append(total)
    return jnp.concatenate(halves, axis=1)


def owner_kernel(first, last, *refs):
    if first:
        got_ref, tie_ref, out_ref, z_ref, u_ref, rec_ref, tag_ref, inv_ref = refs
        near_tags = [got_ref[pl.ds(4 * d + 2, N_REGION, stride=4 * N_DEV), :] for d in range(N_DEV)]
        far_tags = [
            got_ref[pl.ds(4 * N_DEV * r + 3, N_DEV, stride=4), :] for r in range(N_REGION)
        ]
        one_n = jnp.ones((N_REGION, 128), F32)
        one_f = jnp.ones((N_DEV, 128), F32)
        counts = bus_sums([one_n] * N_DEV, [one_f] * N_REGION, near_tags, far_tags)
        inverse = 1.0 / jnp.maximum(counts, 1.0)
        inv_ref[...] = inverse
        for d in range(N_DEV):
            tag_ref[near_tile(d), :] = near_tags[d]
        for r in range(N_REGION):
            tag_ref[far_tile(r), :] = far_tags[r]
        rec_ref[...] = jnp.zeros((32, 128), F32)
        step = 0
    else:
        if last:
            step_ref, got_ref, tag_ref, inv_ref, tie_ref, prev_ref, u_in, rec_in, out_ref = refs
        else:
            (step_ref, got_ref, tag_ref, inv_ref, tie_ref, prev_ref, u_in, rec_in,
             out_ref, z_ref, u_ref, rec_ref) = refs
        near_tags = [tag_ref[near_tile(d), :] for d in range(N_DEV)]
        far_tags = [tag_ref[far_tile(r), :] for r in range(N_REGION)]
        inverse = inv_ref[...]
        step = step_ref[0]
    wide_in = 4 if first else 2
    wide_out = 4 if last else 2
    near = [got_ref[near_rows(wide_in, d), :] for d in range(N_DEV)]
    far = [got_ref[far_rows(wide_in, r), :] for r in range(N_REGION)]
    z = bus_sums(near, far, near_tags, far_tags) * inverse
    change = z if first else z - prev_ref[...]
    change = change * change
    dual = jnp.sum(change[:, :128] + change[:, 128:], axis=0, keepdims=True) * (RHO * RHO / CELLS)
    group = iota((N_REGION, 128), 1) >> 4
    spread = []
    turned = []
    for half in range(2):
        part = z[:, 128 * half : 128 * half + 128]
        for low in range(8):
            one = jnp.where(group == low, part, 0.0)
            for shift in (16, 32, 64):
                one = one + pltpu.roll(one, shift, 1)
            spread.append(one)
        turned.append(jnp.transpose(jnp.concatenate([part] * 16, axis=0)))
    primal = jnp.zeros((N_REGION, 128), F32)
    for dev in range(N_DEV):
        val = jnp.zeros((N_REGION, 128), F32)
        for bus in range(BUS_DEV):
            val = jnp.where(near_tags[dev] == float(bus), spread[bus], val)
        out_ref[near_rows(wide_out, dev), :] = val
        u = near[dev] - val
        gap = u if first else u - u_in[near_tile(dev), :]
        primal = primal + gap * gap
        if not last:
            u_ref[near_tile(dev), :] = u
    for region in range(N_REGION):
        val = jnp.zeros((N_DEV, 128), F32)
        for bus in range(BUS_DEV):
            low = bus % 8
            one = turned[bus // 8][16 * low : 16 * low + 16]
            val = jnp.where(far_tags[region] == float(bus), one, val)
        out_ref[far_rows(wide_out, region), :] = val
        u = far[region] - val
        gap = u if first else u - u_in[far_tile(region), :]
        square = gap * gap
        primal = primal + square[:8] + square[8:]
        if not last:
            u_ref[far_tile(region), :] = u
    primal = jnp.sum(primal, axis=0, keepdims=True) * (1.0 / CELLS)
    row = iota((32, 128), 0)
    if last:
        rec = jnp.where(row == step, primal, rec_in[...])
        rec = jnp.where(row == 16 + step, dual, rec)
        rec = jnp.concatenate([rec, jnp.zeros((96, 128), F32)], axis=0)
        sums = jnp.sum(jnp.transpose(rec), axis=0, keepdims=True)
        out_ref[pl.ds(2, WORLD, stride=4), :] = jnp.broadcast_to(sums, (WORLD, 128))
        out_ref[pl.ds(3, WORLD, stride=4), :] = jnp.zeros((WORLD, 128), F32)
    else:
        if not first:
            rec_ref[...] = rec_in[...]
        rec_ref[pl.ds(step, 1), :] = primal
        rec_ref[pl.ds(16 + step, 1), :] = dual
        z_ref[...] = z


def by_lane(rows):
    return jnp.concatenate([rows[S * r : S * r + S] for r in range(ROWS)], axis=1)


def by_row(lanes):
    return jnp.concatenate([lanes[:, ITEMS * r : ITEMS * r + ITEMS] for r in range(ROWS)], axis=0)


def open_exchange(c_ref, p_ref, tag_ref, send_ref, e_ref, val_ref):
    val = by_row(c_ref[...])
    val_ref[...] = val
    e_ref[...] = jnp.zeros((S, ROWS * ITEMS), F32)
    send = pick(val, p_ref[...])
    send_ref[pl.ds(0, WORLD, stride=4), :] = send[:, :128]
    send_ref[pl.ds(1, WORLD, stride=4), :] = send[:, 128:]
    send_ref[pl.ds(2, WORLD, stride=4), :] = jnp.broadcast_to(tag_ref[0:1, :], (WORLD, 128))
    send_ref[pl.ds(3, WORLD, stride=4), :] = jnp.broadcast_to(tag_ref[1:2, :], (WORLD, 128))


def take_means(z_ref, pt_ref, width):
    near = z_ref[pl.ds(0, WORLD, stride=width), :]
    far = z_ref[pl.ds(1, WORLD, stride=width), :]
    return pick(jnp.concatenate([near, far], axis=1), pt_ref[...])


def slot_kernel(
    z_ref, p_ref, pt_ref, live_ref, val_in, c_ref, bd_ref, bdiag_ref, send_ref, e_ref, val_ref
):
    z_slot = take_means(z_ref, pt_ref, 2)
    u = val_in[...] * live_ref[...] - z_slot
    e = by_lane(RHO * (z_slot - u))
    e_ref[...] = e
    e_high = e.astype(BF16)
    e_low = (e - e_high.astype(F32)).astype(BF16)
    both = dot(jnp.concatenate([e_high, e_low], axis=0), bd_ref[...])
    edge = c_ref[...] + e * bdiag_ref[...] + both[:S] + both[S:]
    val = by_row(edge) + u
    val_ref[...] = val
    send = pick(val, p_ref[...])
    send_ref[pl.ds(0, WORLD, stride=2), :] = send[:, :128]
    send_ref[pl.ds(1, WORLD, stride=2), :] = send[:, 128:]


def close_kernel(z_ref, pt_ref, live_ref, val_in, dual_ref, record_ref):
    z_slot = take_means(z_ref, pt_ref, 4)
    u = val_in[...] * live_ref[...] - z_slot
    old = iota((128, 128), 0)
    order = jnp.where(iota((128, 128), 1) == (old & 31) * ROWS + (old >> 5), 1.0, 0.0)
    dual_ref[...] = pick(jnp.transpose(u), order.astype(BF16))
    sums = jnp.sum(z_ref[pl.ds(2, WORLD, stride=4), :], axis=0, keepdims=True)
    both = jnp.concatenate([sums, pltpu.roll(sums, 112, 1)], axis=0)
    record_ref[...] = both[:, :ITERS]


def edge_part(right_side, m_edge, diag_edge):
    return dot(right_side.astype(BF16), m_edge) + right_side[:, :128] * diag_edge


def setup_kernel(
    me_ref, counts_ref, f0_ref, f1_ref, f2_ref, f3_ref, p_hbm, load_hbm, lo_hbm, hi_hbm, inc_hbm,
    m_ref, diag_ref, bd_ref, bdiag_ref, load_out, lo_out, hi_out,
    place_ref, place_t_ref, live_ref, send_ref, e_ref, val_ref,
    ft, g, p_ref, loads, lo_ref, hi_ref, inc_ref, tag_ref, c_ref, sem,
):
    area = pl.program_id(0)
    order = edge_order()
    pairs = ((p_hbm, p_ref), (load_hbm, loads), (lo_hbm, lo_ref), (hi_hbm, hi_ref), (inc_hbm, inc_ref))
    fetch = [
        pltpu.make_async_copy(source, target, sem.at[n])
        for n, (source, target) in enumerate(pairs)
    ]

    @pl.when(area == 0)
    def _():
        for copy in fetch:
            copy.start()
        fetch[0].wait()

    piv = p_ref[pl.ds(area, 1), :]
    piv_col = jnp.transpose(jnp.broadcast_to(piv, (128, K)))
    step = 256
    count = K // step
    stripes = (f0_ref, f1_ref, f2_ref, f3_ref)
    head = jnp.concatenate([dot(f[0, :, :128], order) for f in stripes], axis=0)
    g[:, :128] = (head * piv_col).astype(BF16)
    f_head = head.astype(BF16)
    for i in range(count):
        at = slice(i * step, (i + 1) * step)
        w = (i + 1) * step
        for q in range(1, w // 128):
            part = stripes[i][0, :, 128 * q : 128 * q + 128].astype(F32)
            g[at, 128 * q : 128 * q + 128] = (part * piv_col[at]).astype(BF16)
        rows = jnp.concatenate([f_head[at], stripes[i][0, :, 128:]], axis=1)
        ft[:w, at] = jnp.transpose(rows)
    eye = iota((step, step), 0) == iota((step, step), 1)
    fix = piv - piv.astype(BF16).astype(F32)
    fix = jnp.concatenate([pick(fix[:, :128], order), fix[:, 128:]], axis=1)
    edge_m = None
    edge_diag = None
    for i in range(count):
        at = slice(i * step, (i + 1) * step)
        w = (i + 1) * step
        column = dot(ft[:w, i * step :], g[i * step :, at])
        block = column[i * step :]
        diag = jnp.sum(jnp.where(eye, block, 0.0), axis=0, keepdims=True) + fix[:, at]
        diag_ref[pl.ds(area, 1), at] = diag
        block = jnp.where(eye, 0.0, block)
        if i == 0:
            edge_diag = diag[:, :128]
            edge_m = block[:EDGE, :128]
        m_ref[0, at, at] = block.astype(BF16)
        if i:
            above = column[: i * step].astype(BF16)
            m_ref[0, : i * step, at] = above
            m_ref[0, at, : i * step] = jnp.transpose(above)
    mine = (iota((NB, 128), 1) >> 4) == area
    for r in range(ROWS):
        shift = lax.rem(area * NB + (128 - r * NB), 128)
        for r_in in range(ROWS):
            rows = edge_m[NB * r_in : NB * r_in + NB]
            rows = jnp.where(mine, pltpu.roll(rows, shift, 1), 0.0)
            at = pl.ds(pl.multiple_of(ITEMS * r_in + NB * area, NB), NB)
            bd_ref[at, ITEMS * r : ITEMS * r + ITEMS] = rows.astype(BF16)

    @pl.when(area == 0)
    def _():
        for copy in fetch[1:]:
            copy.wait()
        route(me_ref, counts_ref, inc_ref, place_ref, place_t_ref, tag_ref, live_ref)

    load = loads[area]
    load = jnp.concatenate([pick(load[:, :128], order), load[:, 128:]], axis=1)
    load_out[0] = load
    c = edge_part(load, m_ref[0, :, :128], edge_diag)

    @pl.when(area == 0)
    def _():
        c_ref[...] = jnp.zeros_like(c_ref)
        bdiag_ref[...] = jnp.zeros_like(bdiag_ref)
        for source, out in ((lo_ref, lo_out), (hi_ref, hi_out)):
            out[:, :128] = pick(source[:, :128], order)
            out[:, 128:] = source[:, 128:]

    lane_mine = (iota((S, 128), 1) >> 4) == area
    for r in range(ROWS):
        at = slice(ITEMS * r, ITEMS * r + ITEMS)
        moved = pltpu.roll(c, lax.rem(area * NB + (128 - r * NB), 128), 1)
        c_ref[:, at] = jnp.where(lane_mine, moved, c_ref[:, at])
        moved = pltpu.roll(edge_diag, lax.rem(area * NB + (128 - r * NB), 128), 1)
        bdiag_ref[:, at] = jnp.where(lane_mine[:1], moved, bdiag_ref[:, at])

    @pl.when(area == AREA - 1)
    def _():
        open_exchange(c_ref, place_ref, tag_ref, send_ref, e_ref, val_ref)


def fetch_areas(first, m_ref, buf, sem):
    half = K // 2
    copies = [
        [
            pltpu.make_async_copy(
                m_ref.at[first + q, pl.ds(half * n, half)],
                buf.at[q, pl.ds(half * n, half)],
                sem.at[q, n],
            )
            for n in range(2)
        ]
        for q in range(HALF)
    ]
    for group in copies:
        for copy in group:
            copy.start()
    return copies


def product(first, q, copies, buf, load_ref, diag_ref, lo_ref, hi_ref, e_ref, moved_in):
    area = first + q
    at = slice(area, area + 1)
    group = iota((S, 128), 1) >> 4
    part = jnp.zeros((S, 128), F32)
    for r in range(ROWS):
        piece = e_ref[:, ITEMS * r : ITEMS * r + ITEMS]
        shift = (NB * (r - area)) % 128
        if shift:
            piece = pltpu.roll(piece, shift, 1)
        part = jnp.where(group == r, piece, part)
    moved = moved_in[q]
    y = jnp.clip(moved, lo_ref[at, :], hi_ref[at, :])
    w = moved - y
    base = load_ref[area] + SIGMA * (y - w)
    side = jnp.concatenate([base[:, :128] + part, base[:, 128:]], axis=1)
    rounded = side.astype(BF16)
    half = K // 2
    copies[q][0].wait()
    x = side * diag_ref[at, :] + dot(rounded[:, :half], buf[q, :half])
    copies[q][1].wait()
    return x + dot(rounded[:, half:], buf[q, half:]), w


def area_kernel(
    first, m_ref, load_ref, diag_ref, lo_ref, hi_ref, e_ref, moved_in, tie_ref, *refs
):
    if first:
        c_in, moved_ref, c_ref, buf, sem = refs
    else:
        moved_ref, c_ref, tie_out, buf, sem = refs
    copies = fetch_areas(first, m_ref, buf, sem)
    group = iota((S, 128), 1) >> 4
    edges = [
        c_in[:, ITEMS * r : ITEMS * r + ITEMS] if first else jnp.zeros((S, 128), F32)
        for r in range(ROWS)
    ]
    news = []
    for q in range(HALF + 1):
        if q < HALF:
            at = slice(first + q, first + q + 1)
            x, w = product(first, q, copies, buf, load_ref, diag_ref, lo_ref, hi_ref, e_ref, moved_in)
            moved = x + w
            moved_ref[q] = moved
            y = jnp.clip(moved, lo_ref[at, :], hi_ref[at, :])
            news.append(load_ref[first + q] + SIGMA * (y - (moved - y)))
        if q > 0:
            area = first + q - 1
            diag = diag_ref[area : area + 1, :128]
            c = edge_part(news[q - 1], buf[q - 1, :, :128], diag)
            for r in range(ROWS):
                shift = (NB * (area - r)) % 128
                turned = pltpu.roll(c, shift, 1) if shift else c
                edges[r] = jnp.where(group == area, turned, edges[r])
    for r in range(ROWS):
        c_ref[:, ITEMS * r : ITEMS * r + ITEMS] = edges[r]
    if not first:
        tie_out[...] = edges[0][:8]


def last_kernel(
    first, m_ref, load_ref, diag_ref, lo_ref, hi_ref, e_ref, moved_in, tie_ref, *refs
):
    if first:
        _, x_ref, buf, sem, x_buf, x_sem = refs
    else:
        x_ref, tie_out, buf, sem, x_buf, x_sem = refs
    copies = fetch_areas(first, m_ref, buf, sem)
    order = edge_order(True)
    writes = []
    for q in range(HALF):
        x, _ = product(first, q, copies, buf, load_ref, diag_ref, lo_ref, hi_ref, e_ref, moved_in)
        x_buf[q] = jnp.concatenate([pick(x[:, :128], order), x[:, 128:]], axis=1)
        writes.append(pltpu.make_async_copy(x_buf.at[q], x_ref.at[first + q], x_sem.at[q]))
        writes[-1].start()
    if not first:
        tie_out[...] = jnp.zeros((8, 128), F32)
    for copy in writes:
        copy.wait()


def on_device(loads, factor, pivots, lower, upper, incidence, counts):
    wide = ROWS * ITEMS
    exchange = lambda x: lax.all_to_all(x, BOTH, split_axis=0, concat_axis=0, tiled=True)
    me = lax.axis_index("region").astype(jnp.int32).reshape(1)
    area_block = lambda rows: pl.BlockSpec((1, rows, K), lambda a: (a, 0, 0))
    whole = lambda *shape: pl.BlockSpec(shape, lambda a: (0,) * len(shape))
    stripe = lambda i: pl.BlockSpec((1, K // 4, (i + 1) * K // 4), lambda a: (a, i, 0))
    outs = (
        (struct((AREA, K, K), BF16), area_block(K)),
        (struct((AREA, K)), whole(AREA, K)),
        (struct((wide, wide), BF16), whole(wide, wide)),
        (struct((1, wide)), whole(1, wide)),
        (struct((AREA, S, K)), area_block(S)),
        (struct((AREA, K)), whole(AREA, K)),
        (struct((AREA, K)), whole(AREA, K)),
        (struct((ITEMS, 256), BF16), whole(ITEMS, 256)),
        (struct((256, ITEMS), BF16), whole(256, ITEMS)),
        (struct((1, ITEMS)), whole(1, ITEMS)),
        (struct((512, 128)), whole(512, 128)),
        (struct((S, wide)), whole(S, wide)),
        (struct((128, 128)), whole(128, 128)),
    )
    (matrix, diag, bd, bd_diag, load, floor_box, ceil_box, place, place_t, live, send, e, val) = call(
        setup_kernel,
        tuple(shape for shape, _ in outs),
        grid=(AREA,),
        in_specs=[SMEM, SMEM] + [stripe(i) for i in range(4)] + [HBM] * 5,
        out_specs=tuple(spec for _, spec in outs),
        scratch_shapes=[
            pltpu.VMEM((K, K), BF16),
            pltpu.VMEM((K, K), BF16),
            pltpu.VMEM((AREA, K), F32),
            pltpu.VMEM((AREA, S, K), F32),
            pltpu.VMEM((AREA, K), F32),
            pltpu.VMEM((AREA, K), F32),
            pltpu.VMEM((AREA, NB), jnp.int32),
            pltpu.VMEM((2, ITEMS), F32),
            pltpu.VMEM((S, wide), F32),
            pltpu.SemaphoreType.DMA((5,)),
        ],
        cost_estimate=cost(8 * 10**9, 34 * 2**20),
        limit=60,
    )(me, counts, *[factor] * 4, pivots, loads, lower, upper, incidence)

    part_shape = struct((HALF, S, K))
    scratch = [
        pltpu.VMEM((HALF, K, K), BF16),
        pltpu.SemaphoreType.DMA((HALF, 2)),
    ]

    def run_areas(first, e, moved, tie, c=None):
        return call(
            functools.partial(area_kernel, first),
            (part_shape, struct((S, wide))) + (() if first else (struct((8, 128)),)),
            in_specs=[HBM] + [VM] * (8 if first else 7),
            out_specs=(VM,) * (2 if first else 3),
            scratch_shapes=scratch,
            input_output_aliases={6: 0},
            cost_estimate=cost(4 * 10**8, 10 * 2**20),
            limit=20,
        )(matrix, load, diag, floor_box, ceil_box, e, moved, tie, *((c,) if first else ()))

    def run_last(first, e, moved, tie, x=None):
        x_shape = struct((AREA, S, K))
        return call(
            functools.partial(last_kernel, first),
            x_shape if first else (x_shape, struct((8, 128))),
            in_specs=[HBM] + [VM] * 7 + ([HBM] if first else []),
            out_specs=HBM if first else (HBM, VM),
            scratch_shapes=scratch
            + [pltpu.VMEM((HALF, S, K), F32), pltpu.SemaphoreType.DMA((HALF,))],
            input_output_aliases={8: 0} if first else {},
            cost_estimate=cost(4 * 10**8, 10 * 2**20),
            limit=20,
        )(matrix, load, diag, floor_box, ceil_box, e, moved, tie, *((x,) if first else ()))

    z_shape = struct((N_REGION, 256))
    rows2 = struct((256, 128))
    rec_shape = struct((32, 128))
    small = cost(10**7, 2**20)
    owner_first = call(
        functools.partial(owner_kernel, True, False),
        (rows2, z_shape, rows2, rec_shape, rows2, z_shape),
        in_specs=[VM] * 2,
        cost_estimate=small,
    )
    owner_mid = call(
        functools.partial(owner_kernel, False, False),
        (rows2, z_shape, rows2, rec_shape),
        in_specs=[SMEM] + [VM] * 7,
        input_output_aliases={5: 1, 6: 2, 7: 3},
        cost_estimate=small,
    )
    owner_last = call(
        functools.partial(owner_kernel, False, True),
        struct((512, 128)),
        in_specs=[SMEM] + [VM] * 7,
        cost_estimate=small,
    )
    run_slots = call(
        slot_kernel,
        (rows2, struct((S, wide)), struct((128, 128))),
        in_specs=[VM] * 8,
        input_output_aliases={4: 2},
        cost_estimate=cost(10**8, 3 * 2**20),
    )

    def iterate(step, state):
        send, e, val, z, u_far, rec, moved0, moved1 = state[:8]
        got = exchange(send)
        moved0, c, tie = run_areas(0, e, moved0, z)
        if step is None:
            back, z, u_far, rec, tags_at, inverse = owner_first(got, tie)
        else:
            tags_at, inverse = state[8:]
            at = jnp.asarray(step, jnp.int32).reshape(1)
            back, z, u_far, rec = owner_mid(at, got, tags_at, inverse, tie, z, u_far, rec)
        z_back = exchange(back)
        moved1, c = run_areas(HALF, e, moved1, z, c)
        send, e, val = run_slots(z_back, place, place_t, live, val, c, bd, bd_diag)
        return (send, e, val, z, u_far, rec, moved0, moved1, tags_at, inverse)

    zero = jnp.zeros((HALF, S, K), F32)
    state = (send, e, val, jnp.zeros((N_REGION, 256), F32), None, None, zero, zero)
    state = iterate(None, state)
    state = lax.fori_loop(1, ITERS - 1, iterate, state)
    send, e, val, z, u_far, rec, moved0, moved1, tags_at, inverse = state
    got = exchange(send)
    x, tie = run_last(0, e, moved0, z)
    back = owner_last(
        jnp.full((1,), ITERS - 1, jnp.int32), got, tags_at, inverse, tie, z, u_far, rec
    )
    z_back = exchange(back)
    x = run_last(HALF, e, moved1, back, x)
    duals, record = call(
        close_kernel, (struct((128, 128)), struct((2, ITERS))), in_specs=[VM] * 4
    )(z_back, place_t, live, val)
    return (x, duals.reshape(AREA, NB, 128), record.T)


def solution(mesh):
    area_split = (
        P(BOTH, None, None),
        P(BOTH, None, None),
        P(BOTH, None),
        P(BOTH, None),
        P(BOTH, None),
        P(BOTH, None),
        P(BOTH),
    )
    return jax.shard_map(
        on_device,
        mesh=mesh,
        in_specs=area_split,
        out_specs=(P(BOTH, None, None), P(BOTH, None, None), P()),
        check_vma=False,
    )
```

```python
import functools

import jax
import jax.numpy as jnp
from jax import lax
from jax.experimental import pallas as pl
from jax.experimental.pallas import tpu as pltpu
from jax.sharding import PartitionSpec as P

K = 1024
S = 32
AREA = 8
NB = 16
ITEMS = AREA * NB
ROWS = 4
EDGE = NB * ROWS
CAP = 8
N_REGION = 8
N_DEV = 16
WORLD = N_REGION * N_DEV
BUS_DEV = 16
ITERS = 14
RHO = 4.0
SIGMA = 1.0
HALF = AREA // 2
CELLS = 1024.0 * 128.0
BOTH = ("region", "dev")
F32 = jnp.float32
BF16 = jnp.bfloat16


def dot(left, right):
    return jnp.dot(left, right, preferred_element_type=F32)


def split3(x):
    high = x.astype(BF16)
    rest = x - high.astype(F32)
    middle = rest.astype(BF16)
    low = (rest - middle.astype(F32)).astype(BF16)
    return high, middle, low


def pick(x, onehot):
    count = x.shape[0]
    got = dot(jnp.concatenate(split3(x), axis=0), onehot)
    return got[:count] + got[count : 2 * count] + got[2 * count :]


def iota(shape, dim):
    return lax.broadcasted_iota(jnp.int32, shape, dim)


def edge_order(transposed=False):
    old = iota((128, 128), 1 if transposed else 0)
    new = iota((128, 128), 0 if transposed else 1)
    target = jnp.where(old < EDGE, (old & 3) * NB + (old >> 2), old)
    return jnp.where(new == target, 1.0, 0.0).astype(BF16)


def struct(shape, dtype=F32):
    return jax.ShapeDtypeStruct(shape, dtype)


def cost(flops, nbytes):
    return pl.CostEstimate(flops=flops, bytes_accessed=nbytes, transcendentals=0)


SMEM = pl.BlockSpec(memory_space=pltpu.SMEM)
VM = pl.BlockSpec(memory_space=pltpu.VMEM)
HBM = pl.BlockSpec(memory_space=pltpu.HBM)


def call(kernel, out_shape, limit=16, **kw):
    return pl.pallas_call(
        kernel,
        out_shape=out_shape,
        compiler_params=pltpu.CompilerParams(vmem_limit_bytes=limit * 2**20),
        **kw,
    )


def route(me_ref, counts_ref, inc_ref, p_ref, pt_ref, tag_ref, live_ref):
    me = me_ref[0]
    lane = iota((ITEMS, ITEMS), 1)
    sub = iota((ITEMS, ITEMS), 0)
    area_of = iota((1, ITEMS), 1) >> 4
    wide = jnp.concatenate([inc_ref[...].astype(F32), jnp.zeros((AREA, 112), F32)], axis=1)
    ids = jnp.zeros((1, ITEMS), F32)
    count = jnp.zeros((1, ITEMS), jnp.int32)
    for a in range(AREA):
        row = wide[a : a + 1, :]
        if a:
            row = pltpu.roll(row, NB * a, 1)
        ids = jnp.where(area_of == a, row, ids)
        count = jnp.where(area_of == a, counts_ref[a], count)
    live = (iota((1, ITEMS), 1) & 15) < count
    live_ref[...] = jnp.where(live, 1.0, 0.0)
    bus = ids.astype(jnp.int32)
    region = bus >> 8
    peer = (bus >> 4) & 15
    key_r = jnp.where(live, jnp.where(region == me, peer, 16 + region), -1).astype(F32)
    key_c = jnp.transpose(jnp.broadcast_to(key_r, (ITEMS, ITEMS)))
    local_c = jnp.transpose(jnp.broadcast_to((bus & 15).astype(F32), (ITEMS, ITEMS)))
    same = (key_c == key_r) & (key_r >= 0.0)
    rank_c = jnp.sum(jnp.where(same & (lane < sub), 1.0, 0.0), axis=1, keepdims=True)
    rank_r = jnp.sum(jnp.where(same & (sub < lane), 1.0, 0.0), axis=0, keepdims=True)

    def place(key, rank):
        far = ITEMS + rank * N_REGION + key - 16.0
        return jnp.where(key < 0.0, -1.0, jnp.where(key < 16.0, rank * N_DEV + key, far))

    place_c = place(key_c, jnp.broadcast_to(rank_c, (ITEMS, ITEMS)))
    place_c = jnp.concatenate([place_c, place_c], axis=1)
    local_c = jnp.concatenate([local_c, local_c], axis=1)
    hit = iota((ITEMS, 256), 1).astype(F32) == place_c
    p_ref[...] = jnp.where(hit, 1.0, 0.0).astype(BF16)
    hit_t = iota((256, ITEMS), 0).astype(F32) == place(key_r, rank_r)
    pt_ref[...] = jnp.where(hit_t, 1.0, 0.0).astype(BF16)
    tag = jnp.sum(jnp.where(hit, local_c + 1.0, 0.0), axis=0, keepdims=True) - 1.0
    tag_ref[0:1, :] = tag[:, :128]
    tag_ref[1:2, :] = tag[:, 128:]


def near_rows(width, dev):
    return pl.ds(width * dev, N_REGION, stride=width * N_DEV)


def far_rows(width, region):
    return pl.ds(width * N_DEV * region + 1, N_DEV, stride=width)


def near_tile(dev):
    return pl.ds(N_REGION * dev, N_REGION)


def far_tile(region):
    return pl.ds(WORLD + N_DEV * region, N_DEV)


def bus_sums(near, far, near_tags, far_tags):
    group = iota((N_REGION, 128), 1) >> 4
    halves = []
    for half in range(2):
        total = jnp.zeros((N_REGION, 128), F32)
        for low in range(8):
            bus = 8.0 * half + low
            acc = jnp.zeros((N_REGION, 128), F32)
            for dev in range(N_DEV):
                acc = acc + jnp.where(near_tags[dev] == bus, near[dev], 0.0)
            for shift in (16, 32, 64):
                acc = acc + pltpu.roll(acc, shift, 1)
            total = jnp.where(group == low, acc, total)
        rows = []
        for low in range(8):
            bus = 8.0 * half + low
            acc = jnp.zeros((N_DEV, 128), F32)
            for region in range(N_REGION):
                acc = acc + jnp.where(far_tags[region] == bus, far[region], 0.0)
            rows.append(acc)
        turned = jnp.transpose(jnp.concatenate(rows, axis=0))
        for c in range(CAP):
            total = total + turned[8 * c : 8 * c + 8]
        halves.append(total)
    return jnp.concatenate(halves, axis=1)


def owner_kernel(first, last, *refs):
    if first:
        got_ref, tie_ref, out_ref, z_ref, u_ref, rec_ref, tag_ref, inv_ref = refs
        near_tags = [got_ref[pl.ds(4 * d + 2, N_REGION, stride=4 * N_DEV), :] for d in range(N_DEV)]
        far_tags = [
            got_ref[pl.ds(4 * N_DEV * r + 3, N_DEV, stride=4), :] for r in range(N_REGION)
        ]
        one_n = jnp.ones((N_REGION, 128), F32)
        one_f = jnp.ones((N_DEV, 128), F32)
        counts = bus_sums([one_n] * N_DEV, [one_f] * N_REGION, near_tags, far_tags)
        inverse = 1.0 / jnp.maximum(counts, 1.0)
        inv_ref[...] = inverse
        for d in range(N_DEV):
            tag_ref[near_tile(d), :] = near_tags[d]
        for r in range(N_REGION):
            tag_ref[far_tile(r), :] = far_tags[r]
        rec_ref[...] = jnp.zeros((32, 128), F32)
        step = 0
    else:
        if last:
            step_ref, got_ref, tag_ref, inv_ref, tie_ref, prev_ref, u_in, rec_in, out_ref = refs
        else:
            (step_ref, got_ref, tag_ref, inv_ref, tie_ref, prev_ref, u_in, rec_in,
             out_ref, z_ref, u_ref, rec_ref) = refs
        near_tags = [tag_ref[near_tile(d), :] for d in range(N_DEV)]
        far_tags = [tag_ref[far_tile(r), :] for r in range(N_REGION)]
        inverse = inv_ref[...]
        step = step_ref[0]
    wide_in = 4 if first else 2
    wide_out = 4 if last else 2
    near = [got_ref[near_rows(wide_in, d), :] for d in range(N_DEV)]
    far = [got_ref[far_rows(wide_in, r), :] for r in range(N_REGION)]
    z = bus_sums(near, far, near_tags, far_tags) * inverse
    change = z if first else z - prev_ref[...]
    change = change * change
    dual = jnp.sum(change[:, :128] + change[:, 128:], axis=0, keepdims=True) * (RHO * RHO / CELLS)
    group = iota((N_REGION, 128), 1) >> 4
    spread = []
    turned = []
    for half in range(2):
        part = z[:, 128 * half : 128 * half + 128]
        for low in range(8):
            one = jnp.where(group == low, part, 0.0)
            for shift in (16, 32, 64):
                one = one + pltpu.roll(one, shift, 1)
            spread.append(one)
        turned.append(jnp.transpose(jnp.concatenate([part] * 16, axis=0)))
    primal = jnp.zeros((N_REGION, 128), F32)
    for dev in range(N_DEV):
        val = jnp.zeros((N_REGION, 128), F32)
        for bus in range(BUS_DEV):
            val = jnp.where(near_tags[dev] == float(bus), spread[bus], val)
        out_ref[near_rows(wide_out, dev), :] = val
        u = near[dev] - val
        gap = u if first else u - u_in[near_tile(dev), :]
        primal = primal + gap * gap
        if not last:
            u_ref[near_tile(dev), :] = u
    for region in range(N_REGION):
        val = jnp.zeros((N_DEV, 128), F32)
        for bus in range(BUS_DEV):
            low = bus % 8
            one = turned[bus // 8][16 * low : 16 * low + 16]
            val = jnp.where(far_tags[region] == float(bus), one, val)
        out_ref[far_rows(wide_out, region), :] = val
        u = far[region] - val
        gap = u if first else u - u_in[far_tile(region), :]
        square = gap * gap
        primal = primal + square[:8] + square[8:]
        if not last:
            u_ref[far_tile(region), :] = u
    primal = jnp.sum(primal, axis=0, keepdims=True) * (1.0 / CELLS)
    row = iota((32, 128), 0)
    if last:
        rec = jnp.where(row == step, primal, rec_in[...])
        rec = jnp.where(row == 16 + step, dual, rec)
        rec = jnp.concatenate([rec, jnp.zeros((96, 128), F32)], axis=0)
        sums = jnp.sum(jnp.transpose(rec), axis=0, keepdims=True)
        out_ref[pl.ds(2, WORLD, stride=4), :] = jnp.broadcast_to(sums, (WORLD, 128))
        out_ref[pl.ds(3, WORLD, stride=4), :] = jnp.zeros((WORLD, 128), F32)
    else:
        if not first:
            rec_ref[...] = rec_in[...]
        rec_ref[pl.ds(step, 1), :] = primal
        rec_ref[pl.ds(16 + step, 1), :] = dual
        z_ref[...] = z


def by_lane(rows):
    return jnp.concatenate([rows[S * r : S * r + S] for r in range(ROWS)], axis=1)


def by_row(lanes):
    return jnp.concatenate([lanes[:, ITEMS * r : ITEMS * r + ITEMS] for r in range(ROWS)], axis=0)


def open_exchange(c_ref, p_ref, tag_ref, send_ref, e_ref, val_ref):
    val = by_row(c_ref[...])
    val_ref[...] = val
    e_ref[...] = jnp.zeros((S, ROWS * ITEMS), F32)
    send = pick(val, p_ref[...])
    send_ref[pl.ds(0, WORLD, stride=4), :] = send[:, :128]
    send_ref[pl.ds(1, WORLD, stride=4), :] = send[:, 128:]
    send_ref[pl.ds(2, WORLD, stride=4), :] = jnp.broadcast_to(tag_ref[0:1, :], (WORLD, 128))
    send_ref[pl.ds(3, WORLD, stride=4), :] = jnp.broadcast_to(tag_ref[1:2, :], (WORLD, 128))


def take_means(z_ref, pt_ref, width):
    near = z_ref[pl.ds(0, WORLD, stride=width), :]
    far = z_ref[pl.ds(1, WORLD, stride=width), :]
    return pick(jnp.concatenate([near, far], axis=1), pt_ref[...])


def slot_kernel(
    z_ref, p_ref, pt_ref, live_ref, val_in, c_ref, bd_ref, bdiag_ref, send_ref, e_ref, val_ref
):
    z_slot = take_means(z_ref, pt_ref, 2)
    u = val_in[...] * live_ref[...] - z_slot
    e = by_lane(RHO * (z_slot - u))
    e_ref[...] = e
    e_high = e.astype(BF16)
    e_low = (e - e_high.astype(F32)).astype(BF16)
    both = dot(jnp.concatenate([e_high, e_low], axis=0), bd_ref[...])
    edge = c_ref[...] + e * bdiag_ref[...] + both[:S] + both[S:]
    val = by_row(edge) + u
    val_ref[...] = val
    send = pick(val, p_ref[...])
    send_ref[pl.ds(0, WORLD, stride=2), :] = send[:, :128]
    send_ref[pl.ds(1, WORLD, stride=2), :] = send[:, 128:]


def close_kernel(z_ref, pt_ref, live_ref, val_in, dual_ref, record_ref):
    z_slot = take_means(z_ref, pt_ref, 4)
    u = val_in[...] * live_ref[...] - z_slot
    old = iota((128, 128), 0)
    order = jnp.where(iota((128, 128), 1) == (old & 31) * ROWS + (old >> 5), 1.0, 0.0)
    dual_ref[...] = pick(jnp.transpose(u), order.astype(BF16))
    sums = jnp.sum(z_ref[pl.ds(2, WORLD, stride=4), :], axis=0, keepdims=True)
    both = jnp.concatenate([sums, pltpu.roll(sums, 112, 1)], axis=0)
    record_ref[...] = both[:, :ITERS]


def edge_part(right_side, m_edge, diag_edge):
    return dot(right_side.astype(BF16), m_edge) + right_side[:, :128] * diag_edge


def setup_area(area, sub, stripes, piv, load, order, m_ref, diag_ref, bd_ref, ft, g):
    piv_col = jnp.transpose(jnp.broadcast_to(piv, (128, K)))
    step = 256
    count = K // step
    head = jnp.concatenate([dot(f[sub, :, :128], order) for f in stripes], axis=0)
    g[:, :128] = (head * piv_col).astype(BF16)
    f_head = head.astype(BF16)
    for i in range(count):
        at = slice(i * step, (i + 1) * step)
        w = (i + 1) * step
        for q in range(1, w // 128):
            part = stripes[i][sub, :, 128 * q : 128 * q + 128].astype(F32)
            g[at, 128 * q : 128 * q + 128] = (part * piv_col[at]).astype(BF16)
        rows = jnp.concatenate([f_head[at], stripes[i][sub, :, 128:]], axis=1)
        ft[:w, at] = jnp.transpose(rows)
    eye = iota((step, step), 0) == iota((step, step), 1)
    fix = piv - piv.astype(BF16).astype(F32)
    fix = jnp.concatenate([pick(fix[:, :128], order), fix[:, 128:]], axis=1)
    edge_m = None
    edge_diag = None
    for i in range(count):
        at = slice(i * step, (i + 1) * step)
        w = (i + 1) * step
        column = dot(ft[:w, i * step :], g[i * step :, at])
        block = column[i * step :]
        diag = jnp.sum(jnp.where(eye, block, 0.0), axis=0, keepdims=True) + fix[:, at]
        diag_ref[pl.ds(area, 1), at] = diag
        block = jnp.where(eye, 0.0, block)
        if i == 0:
            edge_diag = diag[:, :128]
            edge_m = block[:EDGE, :128]
        m_ref[sub, at, at] = block.astype(BF16)
        if i:
            above = column[: i * step].astype(BF16)
            m_ref[sub, : i * step, at] = above
            m_ref[sub, at, : i * step] = jnp.transpose(above)
    mine = (iota((NB, 128), 1) >> 4) == area
    for r in range(ROWS):
        shift = lax.rem(area * NB + (128 - r * NB), 128)
        for r_in in range(ROWS):
            rows = edge_m[NB * r_in : NB * r_in + NB]
            rows = jnp.where(mine, pltpu.roll(rows, shift, 1), 0.0)
            at = pl.ds(pl.multiple_of(ITEMS * r_in + NB * area, NB), NB)
            bd_ref[at, ITEMS * r : ITEMS * r + ITEMS] = rows.astype(BF16)
    return edge_diag, edge_part(load, m_ref[sub, :, :128], edge_diag)


def setup_kernel(
    me_ref, counts_ref, f0_ref, f1_ref, f2_ref, f3_ref, p_hbm, load_hbm, lo_hbm, hi_hbm, inc_hbm,
    m_ref, diag_ref, bd_ref, bdiag_ref, load_out, lo_out, hi_out,
    place_ref, place_t_ref, live_ref, send_ref, e_ref, val_ref,
    ft0, g0, ft1, g1, p_ref, loads, lo_ref, hi_ref, inc_ref, tag_ref, c_ref, sem,
):
    pair = pl.program_id(0)
    order = edge_order()

    @pl.when(pair == 0)
    def _():
        pairs = (
            (p_hbm, p_ref), (load_hbm, loads), (lo_hbm, lo_ref), (hi_hbm, hi_ref), (inc_hbm, inc_ref),
        )
        fetch = [
            pltpu.make_async_copy(source, target, sem.at[n])
            for n, (source, target) in enumerate(pairs)
        ]
        for copy in fetch:
            copy.start()
        for copy in fetch:
            copy.wait()
        route(me_ref, counts_ref, inc_ref, place_ref, place_t_ref, tag_ref, live_ref)
        c_ref[...] = jnp.zeros_like(c_ref)
        bdiag_ref[...] = jnp.zeros_like(bdiag_ref)
        for source, out in ((lo_ref, lo_out), (hi_ref, hi_out)):
            out[:, :128] = pick(source[:, :128], order)
            out[:, 128:] = source[:, 128:]

    stripes = (f0_ref, f1_ref, f2_ref, f3_ref)
    found = []
    for sub, (ft, g) in enumerate(((ft0, g0), (ft1, g1))):
        area = 2 * pair + sub
        piv = p_ref[pl.ds(area, 1), :]
        load = loads[area]
        load = jnp.concatenate([pick(load[:, :128], order), load[:, 128:]], axis=1)
        load_out[sub] = load
        found.append(
            setup_area(area, sub, stripes, piv, load, order, m_ref, diag_ref, bd_ref, ft, g)
        )
    for sub, (edge_diag, c) in enumerate(found):
        area = 2 * pair + sub
        lane_mine = (iota((S, 128), 1) >> 4) == area
        for r in range(ROWS):
            at = slice(ITEMS * r, ITEMS * r + ITEMS)
            shift = lax.rem(area * NB + (128 - r * NB), 128)
            c_ref[:, at] = jnp.where(lane_mine, pltpu.roll(c, shift, 1), c_ref[:, at])
            moved = pltpu.roll(edge_diag, shift, 1)
            bdiag_ref[:, at] = jnp.where(lane_mine[:1], moved, bdiag_ref[:, at])

    @pl.when(pair == AREA // 2 - 1)
    def _():
        open_exchange(c_ref, place_ref, tag_ref, send_ref, e_ref, val_ref)


def fetch_areas(first, m_ref, buf, sem):
    half = K // 2
    copies = [
        [
            pltpu.make_async_copy(
                m_ref.at[first + q, pl.ds(half * n, half)],
                buf.at[q, pl.ds(half * n, half)],
                sem.at[q, n],
            )
            for n in range(2)
        ]
        for q in range(HALF)
    ]
    for group in copies:
        for copy in group:
            copy.start()
    return copies


def product(first, q, copies, buf, load_ref, diag_ref, lo_ref, hi_ref, e_ref, moved_in):
    area = first + q
    at = slice(area, area + 1)
    group = iota((S, 128), 1) >> 4
    part = jnp.zeros((S, 128), F32)
    for r in range(ROWS):
        piece = e_ref[:, ITEMS * r : ITEMS * r + ITEMS]
        shift = (NB * (r - area)) % 128
        if shift:
            piece = pltpu.roll(piece, shift, 1)
        part = jnp.where(group == r, piece, part)
    moved = moved_in[q]
    y = jnp.clip(moved, lo_ref[at, :], hi_ref[at, :])
    w = moved - y
    base = load_ref[area] + SIGMA * (y - w)
    side = jnp.concatenate([base[:, :128] + part, base[:, 128:]], axis=1)
    rounded = side.astype(BF16)
    half = K // 2
    copies[q][0].wait()
    x = side * diag_ref[at, :] + dot(rounded[:, :half], buf[q, :half])
    copies[q][1].wait()
    return x + dot(rounded[:, half:], buf[q, half:]), w


def area_kernel(
    first, m_ref, load_ref, diag_ref, lo_ref, hi_ref, e_ref, moved_in, tie_ref, *refs
):
    if first:
        c_in, moved_ref, c_ref, buf, sem = refs
    else:
        moved_ref, c_ref, tie_out, buf, sem = refs
    copies = fetch_areas(first, m_ref, buf, sem)
    group = iota((S, 128), 1) >> 4
    edges = [
        c_in[:, ITEMS * r : ITEMS * r + ITEMS] if first else jnp.zeros((S, 128), F32)
        for r in range(ROWS)
    ]
    news = []
    for q in range(HALF + 1):
        if q < HALF:
            at = slice(first + q, first + q + 1)
            x, w = product(first, q, copies, buf, load_ref, diag_ref, lo_ref, hi_ref, e_ref, moved_in)
            moved = x + w
            moved_ref[q] = moved
            y = jnp.clip(moved, lo_ref[at, :], hi_ref[at, :])
            news.append(load_ref[first + q] + SIGMA * (y - (moved - y)))
        if q > 0:
            area = first + q - 1
            diag = diag_ref[area : area + 1, :128]
            c = edge_part(news[q - 1], buf[q - 1, :, :128], diag)
            for r in range(ROWS):
                shift = (NB * (area - r)) % 128
                turned = pltpu.roll(c, shift, 1) if shift else c
                edges[r] = jnp.where(group == area, turned, edges[r])
    for r in range(ROWS):
        c_ref[:, ITEMS * r : ITEMS * r + ITEMS] = edges[r]
    if not first:
        tie_out[...] = edges[0][:8]


def last_kernel(
    first, m_ref, load_ref, diag_ref, lo_ref, hi_ref, e_ref, moved_in, tie_ref, *refs
):
    if first:
        _, x_ref, buf, sem, x_buf, x_sem = refs
    else:
        x_ref, tie_out, buf, sem, x_buf, x_sem = refs
    copies = fetch_areas(first, m_ref, buf, sem)
    order = edge_order(True)
    writes = []
    for q in range(HALF):
        x, _ = product(first, q, copies, buf, load_ref, diag_ref, lo_ref, hi_ref, e_ref, moved_in)
        x_buf[q] = jnp.concatenate([pick(x[:, :128], order), x[:, 128:]], axis=1)
        writes.append(pltpu.make_async_copy(x_buf.at[q], x_ref.at[first + q], x_sem.at[q]))
        writes[-1].start()
    if not first:
        tie_out[...] = jnp.zeros((8, 128), F32)
    for copy in writes:
        copy.wait()


def on_device(loads, factor, pivots, lower, upper, incidence, counts):
    wide = ROWS * ITEMS
    exchange = lambda x: lax.all_to_all(x, BOTH, split_axis=0, concat_axis=0, tiled=True)
    me = lax.axis_index("region").astype(jnp.int32).reshape(1)
    area_block = lambda rows: pl.BlockSpec((2, rows, K), lambda a: (a, 0, 0))
    whole = lambda *shape: pl.BlockSpec(shape, lambda a: (0,) * len(shape))
    stripe = lambda i: pl.BlockSpec((2, K // 4, (i + 1) * K // 4), lambda a: (a, i, 0))
    outs = (
        (struct((AREA, K, K), BF16), area_block(K)),
        (struct((AREA, K)), whole(AREA, K)),
        (struct((wide, wide), BF16), whole(wide, wide)),
        (struct((1, wide)), whole(1, wide)),
        (struct((AREA, S, K)), area_block(S)),
        (struct((AREA, K)), whole(AREA, K)),
        (struct((AREA, K)), whole(AREA, K)),
        (struct((ITEMS, 256), BF16), whole(ITEMS, 256)),
        (struct((256, ITEMS), BF16), whole(256, ITEMS)),
        (struct((1, ITEMS)), whole(1, ITEMS)),
        (struct((512, 128)), whole(512, 128)),
        (struct((S, wide)), whole(S, wide)),
        (struct((128, 128)), whole(128, 128)),
    )
    (matrix, diag, bd, bd_diag, load, floor_box, ceil_box, place, place_t, live, send, e, val) = call(
        setup_kernel,
        tuple(shape for shape, _ in outs),
        grid=(AREA // 2,),
        in_specs=[SMEM, SMEM] + [stripe(i) for i in range(4)] + [HBM] * 5,
        out_specs=tuple(spec for _, spec in outs),
        scratch_shapes=[
            pltpu.VMEM((K, K), BF16),
            pltpu.VMEM((K, K), BF16),
            pltpu.VMEM((K, K), BF16),
            pltpu.VMEM((K, K), BF16),
            pltpu.VMEM((AREA, K), F32),
            pltpu.VMEM((AREA, S, K), F32),
            pltpu.VMEM((AREA, K), F32),
            pltpu.VMEM((AREA, K), F32),
            pltpu.VMEM((AREA, NB), jnp.int32),
            pltpu.VMEM((2, ITEMS), F32),
            pltpu.VMEM((S, wide), F32),
            pltpu.SemaphoreType.DMA((5,)),
        ],
        cost_estimate=cost(8 * 10**9, 34 * 2**20),
        limit=60,
    )(me, counts, *[factor] * 4, pivots, loads, lower, upper, incidence)

    part_shape = struct((HALF, S, K))
    scratch = [
        pltpu.VMEM((HALF, K, K), BF16),
        pltpu.SemaphoreType.DMA((HALF, 2)),
    ]

    def run_areas(first, e, moved, tie, c=None):
        return call(
            functools.partial(area_kernel, first),
            (part_shape, struct((S, wide))) + (() if first else (struct((8, 128)),)),
            in_specs=[HBM] + [VM] * (8 if first else 7),
            out_specs=(VM,) * (2 if first else 3),
            scratch_shapes=scratch,
            input_output_aliases={6: 0},
            cost_estimate=cost(4 * 10**8, 10 * 2**20),
            limit=20,
        )(matrix, load, diag, floor_box, ceil_box, e, moved, tie, *((c,) if first else ()))

    def run_last(first, e, moved, tie, x=None):
        x_shape = struct((AREA, S, K))
        return call(
            functools.partial(last_kernel, first),
            x_shape if first else (x_shape, struct((8, 128))),
            in_specs=[HBM] + [VM] * 7 + ([HBM] if first else []),
            out_specs=HBM if first else (HBM, VM),
            scratch_shapes=scratch
            + [pltpu.VMEM((HALF, S, K), F32), pltpu.SemaphoreType.DMA((HALF,))],
            input_output_aliases={8: 0} if first else {},
            cost_estimate=cost(4 * 10**8, 10 * 2**20),
            limit=20,
        )(matrix, load, diag, floor_box, ceil_box, e, moved, tie, *((x,) if first else ()))

    z_shape = struct((N_REGION, 256))
    rows2 = struct((256, 128))
    rec_shape = struct((32, 128))
    small = cost(10**7, 2**20)
    owner_first = call(
        functools.partial(owner_kernel, True, False),
        (rows2, z_shape, rows2, rec_shape, rows2, z_shape),
        in_specs=[VM] * 2,
        cost_estimate=small,
    )
    owner_mid = call(
        functools.partial(owner_kernel, False, False),
        (rows2, z_shape, rows2, rec_shape),
        in_specs=[SMEM] + [VM] * 7,
        input_output_aliases={5: 1, 6: 2, 7: 3},
        cost_estimate=small,
    )
    owner_last = call(
        functools.partial(owner_kernel, False, True),
        struct((512, 128)),
        in_specs=[SMEM] + [VM] * 7,
        cost_estimate=small,
    )
    run_slots = call(
        slot_kernel,
        (rows2, struct((S, wide)), struct((128, 128))),
        in_specs=[VM] * 8,
        input_output_aliases={4: 2},
        cost_estimate=cost(10**8, 3 * 2**20),
    )

    def iterate(step, state):
        send, e, val, z, u_far, rec, moved0, moved1 = state[:8]
        got = exchange(send)
        moved0, c, tie = run_areas(0, e, moved0, z)
        if step is None:
            back, z, u_far, rec, tags_at, inverse = owner_first(got, tie)
        else:
            tags_at, inverse = state[8:]
            at = jnp.asarray(step, jnp.int32).reshape(1)
            back, z, u_far, rec = owner_mid(at, got, tags_at, inverse, tie, z, u_far, rec)
        z_back = exchange(back)
        moved1, c = run_areas(HALF, e, moved1, z, c)
        send, e, val = run_slots(z_back, place, place_t, live, val, c, bd, bd_diag)
        return (send, e, val, z, u_far, rec, moved0, moved1, tags_at, inverse)

    zero = jnp.zeros((HALF, S, K), F32)
    state = (send, e, val, jnp.zeros((N_REGION, 256), F32), None, None, zero, zero)
    state = iterate(None, state)
    state = lax.fori_loop(1, ITERS - 1, iterate, state)
    send, e, val, z, u_far, rec, moved0, moved1, tags_at, inverse = state
    got = exchange(send)
    x, tie = run_last(0, e, moved0, z)
    back = owner_last(
        jnp.full((1,), ITERS - 1, jnp.int32), got, tags_at, inverse, tie, z, u_far, rec
    )
    z_back = exchange(back)
    x = run_last(HALF, e, moved1, back, x)
    duals, record = call(
        close_kernel, (struct((128, 128)), struct((2, ITERS))), in_specs=[VM] * 4
    )(z_back, place_t, live, val)
    return (x, duals.reshape(AREA, NB, 128), record.T)


def solution(mesh):
    area_split = (
        P(BOTH, None, None),
        P(BOTH, None, None),
        P(BOTH, None),
        P(BOTH, None),
        P(BOTH, None),
        P(BOTH, None),
        P(BOTH),
    )
    return jax.shard_map(
        on_device,
        mesh=mesh,
        in_specs=area_split,
        out_specs=(P(BOTH, None, None), P(BOTH, None, None), P()),
        check_vma=False,
    )
```

```python
import functools

import jax
import jax.numpy as jnp
from jax import lax
from jax.experimental import pallas as pl
from jax.experimental.pallas import tpu as pltpu
from jax.sharding import PartitionSpec as P

K = 1024
S = 32
AREA = 8
NB = 16
ITEMS = AREA * NB
ROWS = 4
EDGE = NB * ROWS
CAP = 8
N_REGION = 8
N_DEV = 16
WORLD = N_REGION * N_DEV
BUS_DEV = 16
ITERS = 14
RHO = 4.0
SIGMA = 1.0
HALF = AREA // 2
CELLS = 1024.0 * 128.0
BOTH = ("region", "dev")
F32 = jnp.float32
BF16 = jnp.bfloat16


def dot(left, right):
    return jnp.dot(left, right, preferred_element_type=F32)


def split3(x):
    high = x.astype(BF16)
    rest = x - high.astype(F32)
    middle = rest.astype(BF16)
    low = (rest - middle.astype(F32)).astype(BF16)
    return high, middle, low


def pick(x, onehot):
    count = x.shape[0]
    got = dot(jnp.concatenate(split3(x), axis=0), onehot)
    return got[:count] + got[count : 2 * count] + got[2 * count :]


def iota(shape, dim):
    return lax.broadcasted_iota(jnp.int32, shape, dim)


def edge_order(transposed=False):
    old = iota((128, 128), 1 if transposed else 0)
    new = iota((128, 128), 0 if transposed else 1)
    target = jnp.where(old < EDGE, (old & 3) * NB + (old >> 2), old)
    return jnp.where(new == target, 1.0, 0.0).astype(BF16)


def struct(shape, dtype=F32):
    return jax.ShapeDtypeStruct(shape, dtype)


def cost(flops, nbytes):
    return pl.CostEstimate(flops=flops, bytes_accessed=nbytes, transcendentals=0)


SMEM = pl.BlockSpec(memory_space=pltpu.SMEM)
VM = pl.BlockSpec(memory_space=pltpu.VMEM)
HBM = pl.BlockSpec(memory_space=pltpu.HBM)


def call(kernel, out_shape, limit=16, **kw):
    return pl.pallas_call(
        kernel,
        out_shape=out_shape,
        compiler_params=pltpu.CompilerParams(vmem_limit_bytes=limit * 2**20),
        **kw,
    )


def route(me_ref, counts_ref, inc_ref, p_ref, pt_ref, tag_ref, live_ref):
    me = me_ref[0]
    lane = iota((ITEMS, ITEMS), 1)
    sub = iota((ITEMS, ITEMS), 0)
    area_of = iota((1, ITEMS), 1) >> 4
    wide = jnp.concatenate([inc_ref[...].astype(F32), jnp.zeros((AREA, 112), F32)], axis=1)
    ids = jnp.zeros((1, ITEMS), F32)
    count = jnp.zeros((1, ITEMS), jnp.int32)
    for a in range(AREA):
        row = wide[a : a + 1, :]
        if a:
            row = pltpu.roll(row, NB * a, 1)
        ids = jnp.where(area_of == a, row, ids)
        count = jnp.where(area_of == a, counts_ref[a], count)
    live = (iota((1, ITEMS), 1) & 15) < count
    live_ref[...] = jnp.where(live, 1.0, 0.0)
    bus = ids.astype(jnp.int32)
    region = bus >> 8
    peer = (bus >> 4) & 15
    key_r = jnp.where(live, jnp.where(region == me, peer, 16 + region), -1).astype(F32)
    key_c = jnp.transpose(jnp.broadcast_to(key_r, (ITEMS, ITEMS)))
    local_c = jnp.transpose(jnp.broadcast_to((bus & 15).astype(F32), (ITEMS, ITEMS)))
    same = (key_c == key_r) & (key_r >= 0.0)
    rank_c = jnp.sum(jnp.where(same & (lane < sub), 1.0, 0.0), axis=1, keepdims=True)
    rank_r = jnp.sum(jnp.where(same & (sub < lane), 1.0, 0.0), axis=0, keepdims=True)

    def place(key, rank):
        far = ITEMS + rank * N_REGION + key - 16.0
        return jnp.where(key < 0.0, -1.0, jnp.where(key < 16.0, rank * N_DEV + key, far))

    place_c = place(key_c, jnp.broadcast_to(rank_c, (ITEMS, ITEMS)))
    place_c = jnp.concatenate([place_c, place_c], axis=1)
    local_c = jnp.concatenate([local_c, local_c], axis=1)
    hit = iota((ITEMS, 256), 1).astype(F32) == place_c
    p_ref[...] = jnp.where(hit, 1.0, 0.0).astype(BF16)
    hit_t = iota((256, ITEMS), 0).astype(F32) == place(key_r, rank_r)
    pt_ref[...] = jnp.where(hit_t, 1.0, 0.0).astype(BF16)
    tag = jnp.sum(jnp.where(hit, local_c + 1.0, 0.0), axis=0, keepdims=True) - 1.0
    tag_ref[0:1, :] = tag[:, :128]
    tag_ref[1:2, :] = tag[:, 128:]


def near_rows(width, dev):
    return pl.ds(width * dev, N_REGION, stride=width * N_DEV)


def far_rows(width, region):
    return pl.ds(width * N_DEV * region + 1, N_DEV, stride=width)


def near_tile(dev):
    return pl.ds(N_REGION * dev, N_REGION)


def far_tile(region):
    return pl.ds(WORLD + N_DEV * region, N_DEV)


def bus_sums(near, far, near_tags, far_tags):
    group = iota((N_REGION, 128), 1) >> 4
    halves = []
    for half in range(2):
        total = jnp.zeros((N_REGION, 128), F32)
        for low in range(8):
            bus = 8.0 * half + low
            acc = jnp.zeros((N_REGION, 128), F32)
            for dev in range(N_DEV):
                acc = acc + jnp.where(near_tags[dev] == bus, near[dev], 0.0)
            for shift in (16, 32, 64):
                acc = acc + pltpu.roll(acc, shift, 1)
            total = jnp.where(group == low, acc, total)
        rows = []
        for low in range(8):
            bus = 8.0 * half + low
            acc = jnp.zeros((N_DEV, 128), F32)
            for region in range(N_REGION):
                acc = acc + jnp.where(far_tags[region] == bus, far[region], 0.0)
            rows.append(acc)
        turned = jnp.transpose(jnp.concatenate(rows, axis=0))
        for c in range(CAP):
            total = total + turned[8 * c : 8 * c + 8]
        halves.append(total)
    return jnp.concatenate(halves, axis=1)


def owner_kernel(first, last, *refs):
    if first:
        got_ref, tie_ref, out_ref, z_ref, u_ref, rec_ref, tag_ref, inv_ref = refs
        near_tags = [got_ref[pl.ds(4 * d + 2, N_REGION, stride=4 * N_DEV), :] for d in range(N_DEV)]
        far_tags = [
            got_ref[pl.ds(4 * N_DEV * r + 3, N_DEV, stride=4), :] for r in range(N_REGION)
        ]
        one_n = jnp.ones((N_REGION, 128), F32)
        one_f = jnp.ones((N_DEV, 128), F32)
        counts = bus_sums([one_n] * N_DEV, [one_f] * N_REGION, near_tags, far_tags)
        inverse = 1.0 / jnp.maximum(counts, 1.0)
        inv_ref[...] = inverse
        for d in range(N_DEV):
            tag_ref[near_tile(d), :] = near_tags[d]
        for r in range(N_REGION):
            tag_ref[far_tile(r), :] = far_tags[r]
        rec_ref[...] = jnp.zeros((32, 128), F32)
        step = 0
    else:
        if last:
            step_ref, got_ref, tag_ref, inv_ref, tie_ref, prev_ref, u_in, rec_in, out_ref = refs
        else:
            (step_ref, got_ref, tag_ref, inv_ref, tie_ref, prev_ref, u_in, rec_in,
             out_ref, z_ref, u_ref, rec_ref) = refs
        near_tags = [tag_ref[near_tile(d), :] for d in range(N_DEV)]
        far_tags = [tag_ref[far_tile(r), :] for r in range(N_REGION)]
        inverse = inv_ref[...]
        step = step_ref[0]
    wide_in = 4 if first else 2
    wide_out = 4 if last else 2
    near = [got_ref[near_rows(wide_in, d), :] for d in range(N_DEV)]
    far = [got_ref[far_rows(wide_in, r), :] for r in range(N_REGION)]
    z = bus_sums(near, far, near_tags, far_tags) * inverse
    change = z if first else z - prev_ref[...]
    change = change * change
    dual = jnp.sum(change[:, :128] + change[:, 128:], axis=0, keepdims=True) * (RHO * RHO / CELLS)
    group = iota((N_REGION, 128), 1) >> 4
    spread = []
    turned = []
    for half in range(2):
        part = z[:, 128 * half : 128 * half + 128]
        for low in range(8):
            one = jnp.where(group == low, part, 0.0)
            for shift in (16, 32, 64):
                one = one + pltpu.roll(one, shift, 1)
            spread.append(one)
        turned.append(jnp.transpose(jnp.concatenate([part] * 16, axis=0)))
    primal = jnp.zeros((N_REGION, 128), F32)
    for dev in range(N_DEV):
        val = jnp.zeros((N_REGION, 128), F32)
        for bus in range(BUS_DEV):
            val = jnp.where(near_tags[dev] == float(bus), spread[bus], val)
        out_ref[near_rows(wide_out, dev), :] = val
        u = near[dev] - val
        gap = u if first else u - u_in[near_tile(dev), :]
        primal = primal + gap * gap
        if not last:
            u_ref[near_tile(dev), :] = u
    for region in range(N_REGION):
        val = jnp.zeros((N_DEV, 128), F32)
        for bus in range(BUS_DEV):
            low = bus % 8
            one = turned[bus // 8][16 * low : 16 * low + 16]
            val = jnp.where(far_tags[region] == float(bus), one, val)
        out_ref[far_rows(wide_out, region), :] = val
        u = far[region] - val
        gap = u if first else u - u_in[far_tile(region), :]
        square = gap * gap
        primal = primal + square[:8] + square[8:]
        if not last:
            u_ref[far_tile(region), :] = u
    primal = jnp.sum(primal, axis=0, keepdims=True) * (1.0 / CELLS)
    row = iota((32, 128), 0)
    if last:
        rec = jnp.where(row == step, primal, rec_in[...])
        rec = jnp.where(row == 16 + step, dual, rec)
        rec = jnp.concatenate([rec, jnp.zeros((96, 128), F32)], axis=0)
        sums = jnp.sum(jnp.transpose(rec), axis=0, keepdims=True)
        out_ref[pl.ds(2, WORLD, stride=4), :] = jnp.broadcast_to(sums, (WORLD, 128))
        out_ref[pl.ds(3, WORLD, stride=4), :] = jnp.zeros((WORLD, 128), F32)
    else:
        if not first:
            rec_ref[...] = rec_in[...]
        rec_ref[pl.ds(step, 1), :] = primal
        rec_ref[pl.ds(16 + step, 1), :] = dual
        z_ref[...] = z


def by_lane(rows):
    return jnp.concatenate([rows[S * r : S * r + S] for r in range(ROWS)], axis=1)


def by_row(lanes):
    return jnp.concatenate([lanes[:, ITEMS * r : ITEMS * r + ITEMS] for r in range(ROWS)], axis=0)


def open_exchange(c_ref, p_ref, tag_ref, send_ref, e_ref, val_ref):
    val = by_row(c_ref[...])
    val_ref[...] = val
    e_ref[...] = jnp.zeros((S, ROWS * ITEMS), F32)
    send = pick(val, p_ref[...])
    send_ref[pl.ds(0, WORLD, stride=4), :] = send[:, :128]
    send_ref[pl.ds(1, WORLD, stride=4), :] = send[:, 128:]
    send_ref[pl.ds(2, WORLD, stride=4), :] = jnp.broadcast_to(tag_ref[0:1, :], (WORLD, 128))
    send_ref[pl.ds(3, WORLD, stride=4), :] = jnp.broadcast_to(tag_ref[1:2, :], (WORLD, 128))


def take_means(z_ref, pt_ref, width):
    near = z_ref[pl.ds(0, WORLD, stride=width), :]
    far = z_ref[pl.ds(1, WORLD, stride=width), :]
    return pick(jnp.concatenate([near, far], axis=1), pt_ref[...])


def slot_kernel(
    z_ref, p_ref, pt_ref, live_ref, val_in, c_ref, bd_ref, bdiag_ref, send_ref, e_ref, val_ref
):
    z_slot = take_means(z_ref, pt_ref, 2)
    u = val_in[...] * live_ref[...] - z_slot
    e = by_lane(RHO * (z_slot - u))
    e_ref[...] = e
    e_high = e.astype(BF16)
    e_low = (e - e_high.astype(F32)).astype(BF16)
    both = dot(jnp.concatenate([e_high, e_low], axis=0), bd_ref[...])
    edge = c_ref[...] + e * bdiag_ref[...] + both[:S] + both[S:]
    val = by_row(edge) + u
    val_ref[...] = val
    send = pick(val, p_ref[...])
    send_ref[pl.ds(0, WORLD, stride=2), :] = send[:, :128]
    send_ref[pl.ds(1, WORLD, stride=2), :] = send[:, 128:]


def close_kernel(z_ref, pt_ref, live_ref, val_in, dual_ref, record_ref):
    z_slot = take_means(z_ref, pt_ref, 4)
    u = val_in[...] * live_ref[...] - z_slot
    old = iota((128, 128), 0)
    order = jnp.where(iota((128, 128), 1) == (old & 31) * ROWS + (old >> 5), 1.0, 0.0)
    dual_ref[...] = pick(jnp.transpose(u), order.astype(BF16))
    sums = jnp.sum(z_ref[pl.ds(2, WORLD, stride=4), :], axis=0, keepdims=True)
    both = jnp.concatenate([sums, pltpu.roll(sums, 112, 1)], axis=0)
    record_ref[...] = both[:, :ITERS]


def edge_part(right_side, m_edge, diag_edge):
    return dot(right_side.astype(BF16), m_edge) + right_side[:, :128] * diag_edge


def setup_area(area, sub, stripes, piv, load, order, m_ref, diag_ref, bd_ref, ft, g):
    piv_col = jnp.transpose(jnp.broadcast_to(piv, (128, K)))
    step = 256
    count = K // step
    head = jnp.concatenate([dot(f[sub, :, :128], order) for f in stripes], axis=0)
    g[:, :128] = (head * piv_col).astype(BF16)
    f_head = head.astype(BF16)
    for i in range(count):
        at = slice(i * step, (i + 1) * step)
        w = (i + 1) * step
        for q in range(1, w // 128):
            part = stripes[i][sub, :, 128 * q : 128 * q + 128].astype(F32)
            g[at, 128 * q : 128 * q + 128] = (part * piv_col[at]).astype(BF16)
        rows = jnp.concatenate([f_head[at], stripes[i][sub, :, 128:]], axis=1)
        ft[:w, at] = jnp.transpose(rows)
    eye = iota((step, step), 0) == iota((step, step), 1)
    fix = piv - piv.astype(BF16).astype(F32)
    fix = jnp.concatenate([pick(fix[:, :128], order), fix[:, 128:]], axis=1)
    edge_m = None
    edge_diag = None
    for i in range(count):
        at = slice(i * step, (i + 1) * step)
        w = (i + 1) * step
        column = dot(ft[:w, i * step :], g[i * step :, at])
        block = column[i * step :]
        diag = jnp.sum(jnp.where(eye, block, 0.0), axis=0, keepdims=True) + fix[:, at]
        diag_ref[pl.ds(area, 1), at] = diag
        block = jnp.where(eye, 0.0, block)
        if i == 0:
            edge_diag = diag[:, :128]
            edge_m = block[:EDGE, :128]
        m_ref[sub, at, at] = block.astype(BF16)
        if i:
            above = column[: i * step].astype(BF16)
            m_ref[sub, : i * step, at] = above
            m_ref[sub, at, : i * step] = jnp.transpose(above)
    mine = (iota((NB, 128), 1) >> 4) == area
    for r in range(ROWS):
        shift = lax.rem(area * NB + (128 - r * NB), 128)
        for r_in in range(ROWS):
            rows = edge_m[NB * r_in : NB * r_in + NB]
            rows = jnp.where(mine, pltpu.roll(rows, shift, 1), 0.0)
            at = pl.ds(pl.multiple_of(ITEMS * r_in + NB * area, NB), NB)
            bd_ref[at, ITEMS * r : ITEMS * r + ITEMS] = rows.astype(BF16)
    return edge_diag, edge_part(load, m_ref[sub, :, :128], edge_diag)


def setup_kernel(
    me_ref, counts_ref, f0_ref, f1_ref, f2_ref, f3_ref, p_ref, load_ref, lo_ref, hi_ref, inc_ref,
    m_ref, diag_ref, bd_ref, bdiag_ref, load_out, lo_out, hi_out,
    place_ref, place_t_ref, live_ref, send_ref, e_ref, val_ref,
    ft0, g0, ft1, g1, tag_ref, c_ref,
):
    pair = pl.program_id(0)
    order = edge_order()

    @pl.when(pair == 0)
    def _():
        route(me_ref, counts_ref, inc_ref, place_ref, place_t_ref, tag_ref, live_ref)
        c_ref[...] = jnp.zeros_like(c_ref)
        bdiag_ref[...] = jnp.zeros_like(bdiag_ref)
        for source, out in ((lo_ref, lo_out), (hi_ref, hi_out)):
            out[:, :128] = pick(source[:, :128], order)
            out[:, 128:] = source[:, 128:]

    stripes = (f0_ref, f1_ref, f2_ref, f3_ref)
    found = []
    for sub, (ft, g) in enumerate(((ft0, g0), (ft1, g1))):
        area = 2 * pair + sub
        piv = p_ref[pl.ds(area, 1), :]
        load = load_ref[sub]
        load = jnp.concatenate([pick(load[:, :128], order), load[:, 128:]], axis=1)
        load_out[sub] = load
        found.append(
            setup_area(area, sub, stripes, piv, load, order, m_ref, diag_ref, bd_ref, ft, g)
        )
    for sub, (edge_diag, c) in enumerate(found):
        area = 2 * pair + sub
        lane_mine = (iota((S, 128), 1) >> 4) == area
        for r in range(ROWS):
            at = slice(ITEMS * r, ITEMS * r + ITEMS)
            shift = lax.rem(area * NB + (128 - r * NB), 128)
            c_ref[:, at] = jnp.where(lane_mine, pltpu.roll(c, shift, 1), c_ref[:, at])
            moved = pltpu.roll(edge_diag, shift, 1)
            bdiag_ref[:, at] = jnp.where(lane_mine[:1], moved, bdiag_ref[:, at])

    @pl.when(pair == AREA // 2 - 1)
    def _():
        open_exchange(c_ref, place_ref, tag_ref, send_ref, e_ref, val_ref)


def fetch_areas(first, m_ref, buf, sem):
    half = K // 2
    copies = [
        [
            pltpu.make_async_copy(
                m_ref.at[first + q, pl.ds(half * n, half)],
                buf.at[q, pl.ds(half * n, half)],
                sem.at[q, n],
            )
            for n in range(2)
        ]
        for q in range(HALF)
    ]
    for group in copies:
        for copy in group:
            copy.start()
    return copies


def product(first, q, copies, buf, load_ref, diag_ref, lo_ref, hi_ref, e_ref, moved_in):
    area = first + q
    at = slice(area, area + 1)
    group = iota((S, 128), 1) >> 4
    part = jnp.zeros((S, 128), F32)
    for r in range(ROWS):
        piece = e_ref[:, ITEMS * r : ITEMS * r + ITEMS]
        shift = (NB * (r - area)) % 128
        if shift:
            piece = pltpu.roll(piece, shift, 1)
        part = jnp.where(group == r, piece, part)
    moved = moved_in[q]
    y = jnp.clip(moved, lo_ref[at, :], hi_ref[at, :])
    w = moved - y
    base = load_ref[area] + SIGMA * (y - w)
    side = jnp.concatenate([base[:, :128] + part, base[:, 128:]], axis=1)
    rounded = side.astype(BF16)
    half = K // 2
    copies[q][0].wait()
    x = side * diag_ref[at, :] + dot(rounded[:, :half], buf[q, :half])
    copies[q][1].wait()
    return x + dot(rounded[:, half:], buf[q, half:]), w


def area_kernel(
    first, m_ref, load_ref, diag_ref, lo_ref, hi_ref, e_ref, moved_in, tie_ref, *refs
):
    if first:
        c_in, moved_ref, c_ref, buf, sem = refs
    else:
        moved_ref, c_ref, tie_out, buf, sem = refs
    copies = fetch_areas(first, m_ref, buf, sem)
    group = iota((S, 128), 1) >> 4
    edges = [
        c_in[:, ITEMS * r : ITEMS * r + ITEMS] if first else jnp.zeros((S, 128), F32)
        for r in range(ROWS)
    ]
    news = []
    for q in range(HALF + 1):
        if q < HALF:
            at = slice(first + q, first + q + 1)
            x, w = product(first, q, copies, buf, load_ref, diag_ref, lo_ref, hi_ref, e_ref, moved_in)
            moved = x + w
            moved_ref[q] = moved
            y = jnp.clip(moved, lo_ref[at, :], hi_ref[at, :])
            news.append(load_ref[first + q] + SIGMA * (y - (moved - y)))
        if q > 0:
            area = first + q - 1
            diag = diag_ref[area : area + 1, :128]
            c = edge_part(news[q - 1], buf[q - 1, :, :128], diag)
            for r in range(ROWS):
                shift = (NB * (area - r)) % 128
                turned = pltpu.roll(c, shift, 1) if shift else c
                edges[r] = jnp.where(group == area, turned, edges[r])
    for r in range(ROWS):
        c_ref[:, ITEMS * r : ITEMS * r + ITEMS] = edges[r]
    if not first:
        tie_out[...] = edges[0][:8]


def last_kernel(
    first, m_ref, load_ref, diag_ref, lo_ref, hi_ref, e_ref, moved_in, tie_ref, *refs
):
    if first:
        _, x_ref, buf, sem, x_buf, x_sem = refs
    else:
        x_ref, tie_out, buf, sem, x_buf, x_sem = refs
    copies = fetch_areas(first, m_ref, buf, sem)
    order = edge_order(True)
    writes = []
    for q in range(HALF):
        x, _ = product(first, q, copies, buf, load_ref, diag_ref, lo_ref, hi_ref, e_ref, moved_in)
        x_buf[q] = jnp.concatenate([pick(x[:, :128], order), x[:, 128:]], axis=1)
        writes.append(pltpu.make_async_copy(x_buf.at[q], x_ref.at[first + q], x_sem.at[q]))
        writes[-1].start()
    if not first:
        tie_out[...] = jnp.zeros((8, 128), F32)
    for copy in writes:
        copy.wait()


def on_device(loads, factor, pivots, lower, upper, incidence, counts):
    wide = ROWS * ITEMS
    exchange = lambda x: lax.all_to_all(x, BOTH, split_axis=0, concat_axis=0, tiled=True)
    me = lax.axis_index("region").astype(jnp.int32).reshape(1)
    area_block = lambda rows: pl.BlockSpec((2, rows, K), lambda a: (a, 0, 0))
    whole = lambda *shape: pl.BlockSpec(shape, lambda a: (0,) * len(shape))
    stripe = lambda i: pl.BlockSpec((2, K // 4, (i + 1) * K // 4), lambda a: (a, i, 0))
    outs = (
        (struct((AREA, K, K), BF16), area_block(K)),
        (struct((AREA, K)), whole(AREA, K)),
        (struct((wide, wide), BF16), whole(wide, wide)),
        (struct((1, wide)), whole(1, wide)),
        (struct((AREA, S, K)), area_block(S)),
        (struct((AREA, K)), whole(AREA, K)),
        (struct((AREA, K)), whole(AREA, K)),
        (struct((ITEMS, 256), BF16), whole(ITEMS, 256)),
        (struct((256, ITEMS), BF16), whole(256, ITEMS)),
        (struct((1, ITEMS)), whole(1, ITEMS)),
        (struct((512, 128)), whole(512, 128)),
        (struct((S, wide)), whole(S, wide)),
        (struct((128, 128)), whole(128, 128)),
    )
    (matrix, diag, bd, bd_diag, load, floor_box, ceil_box, place, place_t, live, send, e, val) = call(
        setup_kernel,
        tuple(shape for shape, _ in outs),
        grid=(AREA // 2,),
        in_specs=[SMEM, SMEM] + [stripe(i) for i in range(4)]
        + [whole(AREA, K), area_block(S), whole(AREA, K), whole(AREA, K), whole(AREA, NB)],
        out_specs=tuple(spec for _, spec in outs),
        scratch_shapes=[
            pltpu.VMEM((K, K), BF16),
            pltpu.VMEM((K, K), BF16),
            pltpu.VMEM((K, K), BF16),
            pltpu.VMEM((K, K), BF16),
            pltpu.VMEM((2, ITEMS), F32),
            pltpu.VMEM((S, wide), F32),
        ],
        cost_estimate=cost(8 * 10**9, 34 * 2**20),
        limit=60,
    )(me, counts, *[factor] * 4, pivots, loads, lower, upper, incidence)

    part_shape = struct((HALF, S, K))
    scratch = [
        pltpu.VMEM((HALF, K, K), BF16),
        pltpu.SemaphoreType.DMA((HALF, 2)),
    ]

    def run_areas(first, e, moved, tie, c=None):
        return call(
            functools.partial(area_kernel, first),
            (part_shape, struct((S, wide))) + (() if first else (struct((8, 128)),)),
            in_specs=[HBM] + [VM] * (8 if first else 7),
            out_specs=(VM,) * (2 if first else 3),
            scratch_shapes=scratch,
            input_output_aliases={6: 0},
            cost_estimate=cost(4 * 10**8, 10 * 2**20),
            limit=20,
        )(matrix, load, diag, floor_box, ceil_box, e, moved, tie, *((c,) if first else ()))

    def run_last(first, e, moved, tie, x=None):
        x_shape = struct((AREA, S, K))
        return call(
            functools.partial(last_kernel, first),
            x_shape if first else (x_shape, struct((8, 128))),
            in_specs=[HBM] + [VM] * 7 + ([HBM] if first else []),
            out_specs=HBM if first else (HBM, VM),
            scratch_shapes=scratch
            + [pltpu.VMEM((HALF, S, K), F32), pltpu.SemaphoreType.DMA((HALF,))],
            input_output_aliases={8: 0} if first else {},
            cost_estimate=cost(4 * 10**8, 10 * 2**20),
            limit=20,
        )(matrix, load, diag, floor_box, ceil_box, e, moved, tie, *((x,) if first else ()))

    z_shape = struct((N_REGION, 256))
    rows2 = struct((256, 128))
    rec_shape = struct((32, 128))
    small = cost(10**7, 2**20)
    owner_first = call(
        functools.partial(owner_kernel, True, False),
        (rows2, z_shape, rows2, rec_shape, rows2, z_shape),
        in_specs=[VM] * 2,
        cost_estimate=small,
    )
    owner_mid = call(
        functools.partial(owner_kernel, False, False),
        (rows2, z_shape, rows2, rec_shape),
        in_specs=[SMEM] + [VM] * 7,
        input_output_aliases={5: 1, 6: 2, 7: 3},
        cost_estimate=small,
    )
    owner_last = call(
        functools.partial(owner_kernel, False, True),
        struct((512, 128)),
        in_specs=[SMEM] + [VM] * 7,
        cost_estimate=small,
    )
    run_slots = call(
        slot_kernel,
        (rows2, struct((S, wide)), struct((128, 128))),
        in_specs=[VM] * 8,
        input_output_aliases={4: 2},
        cost_estimate=cost(10**8, 3 * 2**20),
    )

    def iterate(step, state):
        send, e, val, z, u_far, rec, moved0, moved1 = state[:8]
        got = exchange(send)
        moved0, c, tie = run_areas(0, e, moved0, z)
        if step is None:
            back, z, u_far, rec, tags_at, inverse = owner_first(got, tie)
        else:
            tags_at, inverse = state[8:]
            at = jnp.asarray(step, jnp.int32).reshape(1)
            back, z, u_far, rec = owner_mid(at, got, tags_at, inverse, tie, z, u_far, rec)
        z_back = exchange(back)
        moved1, c = run_areas(HALF, e, moved1, z, c)
        send, e, val = run_slots(z_back, place, place_t, live, val, c, bd, bd_diag)
        return (send, e, val, z, u_far, rec, moved0, moved1, tags_at, inverse)

    zero = jnp.zeros((HALF, S, K), F32)
    state = (send, e, val, jnp.zeros((N_REGION, 256), F32), None, None, zero, zero)
    state = iterate(None, state)
    state = lax.fori_loop(1, ITERS - 1, iterate, state)
    send, e, val, z, u_far, rec, moved0, moved1, tags_at, inverse = state
    got = exchange(send)
    x, tie = run_last(0, e, moved0, z)
    back = owner_last(
        jnp.full((1,), ITERS - 1, jnp.int32), got, tags_at, inverse, tie, z, u_far, rec
    )
    z_back = exchange(back)
    x = run_last(HALF, e, moved1, back, x)
    duals, record = call(
        close_kernel, (struct((128, 128)), struct((2, ITERS))), in_specs=[VM] * 4
    )(z_back, place_t, live, val)
    return (x, duals.reshape(AREA, NB, 128), record.T)


def solution(mesh):
    area_split = (
        P(BOTH, None, None),
        P(BOTH, None, None),
        P(BOTH, None),
        P(BOTH, None),
        P(BOTH, None),
        P(BOTH, None),
        P(BOTH),
    )
    return jax.shard_map(
        on_device,
        mesh=mesh,
        in_specs=area_split,
        out_specs=(P(BOTH, None, None), P(BOTH, None, None), P()),
        check_vma=False,
    )
```

```python
import functools

import jax
import jax.numpy as jnp
from jax import lax
from jax.experimental import pallas as pl
from jax.experimental.pallas import tpu as pltpu
from jax.sharding import PartitionSpec as P

K = 1024
S = 32
AREA = 8
NB = 16
ITEMS = AREA * NB
ROWS = 4
EDGE = NB * ROWS
CAP = 8
N_REGION = 8
N_DEV = 16
WORLD = N_REGION * N_DEV
BUS_DEV = 16
ITERS = 14
RHO = 4.0
SIGMA = 1.0
HALF = AREA // 2
CELLS = 1024.0 * 128.0
BOTH = ("region", "dev")
F32 = jnp.float32
BF16 = jnp.bfloat16


def dot(left, right):
    return jnp.dot(left, right, preferred_element_type=F32)


def split3(x):
    high = x.astype(BF16)
    rest = x - high.astype(F32)
    middle = rest.astype(BF16)
    low = (rest - middle.astype(F32)).astype(BF16)
    return high, middle, low


def pick(x, onehot):
    count = x.shape[0]
    got = dot(jnp.concatenate(split3(x), axis=0), onehot)
    return got[:count] + got[count : 2 * count] + got[2 * count :]


def place_by(x, onehot):
    count = x.shape[0]
    high = x.astype(BF16)
    low = (x - high.astype(F32)).astype(BF16)
    got = dot(jnp.concatenate([high, low], axis=0), onehot)
    return got[:count] + got[count:]


def iota(shape, dim):
    return lax.broadcasted_iota(jnp.int32, shape, dim)


def edge_order(transposed=False):
    old = iota((128, 128), 1 if transposed else 0)
    new = iota((128, 128), 0 if transposed else 1)
    target = jnp.where(old < EDGE, (old & 3) * NB + (old >> 2), old)
    return jnp.where(new == target, 1.0, 0.0).astype(BF16)


def struct(shape, dtype=F32):
    return jax.ShapeDtypeStruct(shape, dtype)


def cost(flops, nbytes):
    return pl.CostEstimate(flops=flops, bytes_accessed=nbytes, transcendentals=0)


SMEM = pl.BlockSpec(memory_space=pltpu.SMEM)
VM = pl.BlockSpec(memory_space=pltpu.VMEM)
HBM = pl.BlockSpec(memory_space=pltpu.HBM)


def call(kernel, out_shape, limit=16, **kw):
    return pl.pallas_call(
        kernel,
        out_shape=out_shape,
        compiler_params=pltpu.CompilerParams(vmem_limit_bytes=limit * 2**20),
        **kw,
    )


def route(me_ref, counts_ref, inc_ref, p_ref, pt_ref, tag_ref, live_ref):
    me = me_ref[0]
    lane = iota((ITEMS, ITEMS), 1)
    sub = iota((ITEMS, ITEMS), 0)
    area_of = iota((1, ITEMS), 1) >> 4
    wide = jnp.concatenate([inc_ref[...].astype(F32), jnp.zeros((AREA, 112), F32)], axis=1)
    ids = jnp.zeros((1, ITEMS), F32)
    count = jnp.zeros((1, ITEMS), jnp.int32)
    for a in range(AREA):
        row = wide[a : a + 1, :]
        if a:
            row = pltpu.roll(row, NB * a, 1)
        ids = jnp.where(area_of == a, row, ids)
        count = jnp.where(area_of == a, counts_ref[a], count)
    live = (iota((1, ITEMS), 1) & 15) < count
    live_ref[...] = jnp.where(live, 1.0, 0.0)
    bus = ids.astype(jnp.int32)
    region = bus >> 8
    peer = (bus >> 4) & 15
    key_r = jnp.where(live, jnp.where(region == me, peer, 16 + region), -1).astype(F32)
    key_c = jnp.transpose(jnp.broadcast_to(key_r, (ITEMS, ITEMS)))
    local_c = jnp.transpose(jnp.broadcast_to((bus & 15).astype(F32), (ITEMS, ITEMS)))
    same = (key_c == key_r) & (key_r >= 0.0)
    rank_c = jnp.sum(jnp.where(same & (lane < sub), 1.0, 0.0), axis=1, keepdims=True)
    rank_r = jnp.sum(jnp.where(same & (sub < lane), 1.0, 0.0), axis=0, keepdims=True)

    def place(key, rank):
        far = ITEMS + rank * N_REGION + key - 16.0
        return jnp.where(key < 0.0, -1.0, jnp.where(key < 16.0, rank * N_DEV + key, far))

    place_c = place(key_c, jnp.broadcast_to(rank_c, (ITEMS, ITEMS)))
    place_c = jnp.concatenate([place_c, place_c], axis=1)
    local_c = jnp.concatenate([local_c, local_c], axis=1)
    hit = iota((ITEMS, 256), 1).astype(F32) == place_c
    p_ref[...] = jnp.where(hit, 1.0, 0.0).astype(BF16)
    hit_t = iota((256, ITEMS), 0).astype(F32) == place(key_r, rank_r)
    pt_ref[...] = jnp.where(hit_t, 1.0, 0.0).astype(BF16)
    tag = jnp.sum(jnp.where(hit, local_c + 1.0, 0.0), axis=0, keepdims=True) - 1.0
    tag_ref[0:1, :] = tag[:, :128]
    tag_ref[1:2, :] = tag[:, 128:]


def near_rows(width, dev):
    return pl.ds(width * dev, N_REGION, stride=width * N_DEV)


def far_rows(width, region):
    return pl.ds(width * N_DEV * region + 1, N_DEV, stride=width)


def near_tile(dev):
    return pl.ds(N_REGION * dev, N_REGION)


def far_tile(region):
    return pl.ds(WORLD + N_DEV * region, N_DEV)


def bus_sums(near, far, near_tags, far_tags):
    group = iota((N_REGION, 128), 1) >> 4
    halves = []
    for half in range(2):
        total = jnp.zeros((N_REGION, 128), F32)
        for low in range(8):
            bus = 8.0 * half + low
            acc = jnp.zeros((N_REGION, 128), F32)
            for dev in range(N_DEV):
                acc = acc + jnp.where(near_tags[dev] == bus, near[dev], 0.0)
            for shift in (16, 32, 64):
                acc = acc + pltpu.roll(acc, shift, 1)
            total = jnp.where(group == low, acc, total)
        rows = []
        for low in range(8):
            bus = 8.0 * half + low
            acc = jnp.zeros((N_DEV, 128), F32)
            for region in range(N_REGION):
                acc = acc + jnp.where(far_tags[region] == bus, far[region], 0.0)
            rows.append(acc)
        turned = jnp.transpose(jnp.concatenate(rows, axis=0))
        for c in range(CAP):
            total = total + turned[8 * c : 8 * c + 8]
        halves.append(total)
    return jnp.concatenate(halves, axis=1)


def owner_kernel(first, last, *refs):
    if first:
        got_ref, tie_ref, out_ref, z_ref, u_ref, rec_ref, tag_ref, inv_ref = refs
        near_tags = [got_ref[pl.ds(4 * d + 2, N_REGION, stride=4 * N_DEV), :] for d in range(N_DEV)]
        far_tags = [
            got_ref[pl.ds(4 * N_DEV * r + 3, N_DEV, stride=4), :] for r in range(N_REGION)
        ]
        one_n = jnp.ones((N_REGION, 128), F32)
        one_f = jnp.ones((N_DEV, 128), F32)
        counts = bus_sums([one_n] * N_DEV, [one_f] * N_REGION, near_tags, far_tags)
        inverse = 1.0 / jnp.maximum(counts, 1.0)
        inv_ref[...] = inverse
        for d in range(N_DEV):
            tag_ref[near_tile(d), :] = near_tags[d]
        for r in range(N_REGION):
            tag_ref[far_tile(r), :] = far_tags[r]
        rec_ref[...] = jnp.zeros((32, 128), F32)
        step = 0
    else:
        if last:
            step_ref, got_ref, tag_ref, inv_ref, tie_ref, prev_ref, u_in, rec_in, out_ref = refs
        else:
            (step_ref, got_ref, tag_ref, inv_ref, tie_ref, prev_ref, u_in, rec_in,
             out_ref, z_ref, u_ref, rec_ref) = refs
        near_tags = [tag_ref[near_tile(d), :] for d in range(N_DEV)]
        far_tags = [tag_ref[far_tile(r), :] for r in range(N_REGION)]
        inverse = inv_ref[...]
        step = step_ref[0]
    wide_in = 4 if first else 2
    wide_out = 4 if last else 2
    near = [got_ref[near_rows(wide_in, d), :] for d in range(N_DEV)]
    far = [got_ref[far_rows(wide_in, r), :] for r in range(N_REGION)]
    z = bus_sums(near, far, near_tags, far_tags) * inverse
    change = z if first else z - prev_ref[...]
    change = change * change
    dual = jnp.sum(change[:, :128] + change[:, 128:], axis=0, keepdims=True) * (RHO * RHO / CELLS)
    group = iota((N_REGION, 128), 1) >> 4
    spread = []
    turned = []
    for half in range(2):
        part = z[:, 128 * half : 128 * half + 128]
        for low in range(8):
            one = jnp.where(group == low, part, 0.0)
            for shift in (16, 32, 64):
                one = one + pltpu.roll(one, shift, 1)
            spread.append(one)
        turned.append(jnp.transpose(jnp.concatenate([part] * 16, axis=0)))
    primal = jnp.zeros((N_REGION, 128), F32)
    for dev in range(N_DEV):
        val = jnp.zeros((N_REGION, 128), F32)
        for bus in range(BUS_DEV):
            val = jnp.where(near_tags[dev] == float(bus), spread[bus], val)
        out_ref[near_rows(wide_out, dev), :] = val
        u = near[dev] - val
        gap = u if first else u - u_in[near_tile(dev), :]
        primal = primal + gap * gap
        if not last:
            u_ref[near_tile(dev), :] = u
    for region in range(N_REGION):
        val = jnp.zeros((N_DEV, 128), F32)
        for bus in range(BUS_DEV):
            low = bus % 8
            one = turned[bus // 8][16 * low : 16 * low + 16]
            val = jnp.where(far_tags[region] == float(bus), one, val)
        out_ref[far_rows(wide_out, region), :] = val
        u = far[region] - val
        gap = u if first else u - u_in[far_tile(region), :]
        square = gap * gap
        primal = primal + square[:8] + square[8:]
        if not last:
            u_ref[far_tile(region), :] = u
    primal = jnp.sum(primal, axis=0, keepdims=True) * (1.0 / CELLS)
    row = iota((32, 128), 0)
    if last:
        rec = jnp.where(row == step, primal, rec_in[...])
        rec = jnp.where(row == 16 + step, dual, rec)
        rec = jnp.concatenate([rec, jnp.zeros((96, 128), F32)], axis=0)
        sums = jnp.sum(jnp.transpose(rec), axis=0, keepdims=True)
        out_ref[pl.ds(2, WORLD, stride=4), :] = jnp.broadcast_to(sums, (WORLD, 128))
        out_ref[pl.ds(3, WORLD, stride=4), :] = jnp.zeros((WORLD, 128), F32)
    else:
        if not first:
            rec_ref[...] = rec_in[...]
        rec_ref[pl.ds(step, 1), :] = primal
        rec_ref[pl.ds(16 + step, 1), :] = dual
        z_ref[...] = z


def by_lane(rows):
    return jnp.concatenate([rows[S * r : S * r + S] for r in range(ROWS)], axis=1)


def by_row(lanes):
    return jnp.concatenate([lanes[:, ITEMS * r : ITEMS * r + ITEMS] for r in range(ROWS)], axis=0)


def open_exchange(c_ref, p_ref, tag_ref, send_ref, e_ref, val_ref):
    val = by_row(c_ref[...])
    val_ref[...] = val
    e_ref[...] = jnp.zeros((S, ROWS * ITEMS), F32)
    send = pick(val, p_ref[...])
    send_ref[pl.ds(0, WORLD, stride=4), :] = send[:, :128]
    send_ref[pl.ds(1, WORLD, stride=4), :] = send[:, 128:]
    send_ref[pl.ds(2, WORLD, stride=4), :] = jnp.broadcast_to(tag_ref[0:1, :], (WORLD, 128))
    send_ref[pl.ds(3, WORLD, stride=4), :] = jnp.broadcast_to(tag_ref[1:2, :], (WORLD, 128))


def take_means(z_ref, pt_ref, width):
    near = z_ref[pl.ds(0, WORLD, stride=width), :]
    far = z_ref[pl.ds(1, WORLD, stride=width), :]
    return place_by(jnp.concatenate([near, far], axis=1), pt_ref[...])


def slot_kernel(
    z_ref, p_ref, pt_ref, live_ref, val_in, c_ref, bd_ref, bdiag_ref, send_ref, e_ref, val_ref
):
    z_slot = take_means(z_ref, pt_ref, 2)
    u = val_in[...] * live_ref[...] - z_slot
    e = by_lane(RHO * (z_slot - u))
    e_ref[...] = e
    e_high = e.astype(BF16)
    e_low = (e - e_high.astype(F32)).astype(BF16)
    both = dot(jnp.concatenate([e_high, e_low], axis=0), bd_ref[...])
    edge = c_ref[...] + e * bdiag_ref[...] + both[:S] + both[S:]
    val = by_row(edge) + u
    val_ref[...] = val
    send = place_by(val, p_ref[...])
    send_ref[pl.ds(0, WORLD, stride=2), :] = send[:, :128]
    send_ref[pl.ds(1, WORLD, stride=2), :] = send[:, 128:]


def close_kernel(z_ref, pt_ref, live_ref, val_in, dual_ref, record_ref):
    z_slot = take_means(z_ref, pt_ref, 4)
    u = val_in[...] * live_ref[...] - z_slot
    old = iota((128, 128), 0)
    order = jnp.where(iota((128, 128), 1) == (old & 31) * ROWS + (old >> 5), 1.0, 0.0)
    dual_ref[...] = pick(jnp.transpose(u), order.astype(BF16))
    sums = jnp.sum(z_ref[pl.ds(2, WORLD, stride=4), :], axis=0, keepdims=True)
    both = jnp.concatenate([sums, pltpu.roll(sums, 112, 1)], axis=0)
    record_ref[...] = both[:, :ITERS]


def edge_part(right_side, m_edge, diag_edge):
    return dot(right_side.astype(BF16), m_edge) + right_side[:, :128] * diag_edge


def setup_area(area, sub, stripes, piv, load, order, m_ref, diag_ref, bd_ref, ft, g):
    piv_col = jnp.transpose(jnp.broadcast_to(piv, (128, K)))
    step = 256
    count = K // step
    head = jnp.concatenate([dot(f[sub, :, :128], order) for f in stripes], axis=0)
    g[:, :128] = (head * piv_col).astype(BF16)
    f_head = head.astype(BF16)
    for i in range(count):
        at = slice(i * step, (i + 1) * step)
        w = (i + 1) * step
        for q in range(1, w // 128):
            part = stripes[i][sub, :, 128 * q : 128 * q + 128].astype(F32)
            g[at, 128 * q : 128 * q + 128] = (part * piv_col[at]).astype(BF16)
        rows = jnp.concatenate([f_head[at], stripes[i][sub, :, 128:]], axis=1)
        ft[:w, at] = jnp.transpose(rows)
    eye = iota((step, step), 0) == iota((step, step), 1)
    fix = piv - piv.astype(BF16).astype(F32)
    fix = jnp.concatenate([pick(fix[:, :128], order), fix[:, 128:]], axis=1)
    edge_m = None
    edge_diag = None
    for i in range(count):
        at = slice(i * step, (i + 1) * step)
        w = (i + 1) * step
        column = dot(ft[:w, i * step :], g[i * step :, at])
        block = column[i * step :]
        diag = jnp.sum(jnp.where(eye, block, 0.0), axis=0, keepdims=True) + fix[:, at]
        diag_ref[pl.ds(area, 1), at] = diag
        block = jnp.where(eye, 0.0, block)
        if i == 0:
            edge_diag = diag[:, :128]
            edge_m = block[:EDGE, :128]
        m_ref[sub, at, at] = block.astype(BF16)
        if i:
            above = column[: i * step].astype(BF16)
            m_ref[sub, : i * step, at] = above
            m_ref[sub, at, : i * step] = jnp.transpose(above)
    mine = (iota((NB, 128), 1) >> 4) == area
    for r in range(ROWS):
        shift = lax.rem(area * NB + (128 - r * NB), 128)
        for r_in in range(ROWS):
            rows = edge_m[NB * r_in : NB * r_in + NB]
            rows = jnp.where(mine, pltpu.roll(rows, shift, 1), 0.0)
            at = pl.ds(pl.multiple_of(ITEMS * r_in + NB * area, NB), NB)
            bd_ref[at, ITEMS * r : ITEMS * r + ITEMS] = rows.astype(BF16)
    return edge_diag, edge_part(load, m_ref[sub, :, :128], edge_diag)


def setup_kernel(
    me_ref, counts_ref, f0_ref, f1_ref, f2_ref, f3_ref, p_ref, load_ref, lo_ref, hi_ref, inc_ref,
    m_ref, diag_ref, bd_ref, bdiag_ref, load_out, lo_out, hi_out,
    place_ref, place_t_ref, live_ref, send_ref, e_ref, val_ref,
    ft0, g0, ft1, g1, tag_ref, c_ref,
):
    pair = pl.program_id(0)
    order = edge_order()

    @pl.when(pair == 0)
    def _():
        route(me_ref, counts_ref, inc_ref, place_ref, place_t_ref, tag_ref, live_ref)
        c_ref[...] = jnp.zeros_like(c_ref)
        bdiag_ref[...] = jnp.zeros_like(bdiag_ref)
        for source, out in ((lo_ref, lo_out), (hi_ref, hi_out)):
            out[:, :128] = pick(source[:, :128], order)
            out[:, 128:] = source[:, 128:]

    stripes = (f0_ref, f1_ref, f2_ref, f3_ref)
    found = []
    for sub, (ft, g) in enumerate(((ft0, g0), (ft1, g1))):
        area = 2 * pair + sub
        piv = p_ref[pl.ds(area, 1), :]
        load = load_ref[sub]
        load = jnp.concatenate([pick(load[:, :128], order), load[:, 128:]], axis=1)
        load_out[sub] = load
        found.append(
            setup_area(area, sub, stripes, piv, load, order, m_ref, diag_ref, bd_ref, ft, g)
        )
    for sub, (edge_diag, c) in enumerate(found):
        area = 2 * pair + sub
        lane_mine = (iota((S, 128), 1) >> 4) == area
        for r in range(ROWS):
            at = slice(ITEMS * r, ITEMS * r + ITEMS)
            shift = lax.rem(area * NB + (128 - r * NB), 128)
            c_ref[:, at] = jnp.where(lane_mine, pltpu.roll(c, shift, 1), c_ref[:, at])
            moved = pltpu.roll(edge_diag, shift, 1)
            bdiag_ref[:, at] = jnp.where(lane_mine[:1], moved, bdiag_ref[:, at])

    @pl.when(pair == AREA // 2 - 1)
    def _():
        open_exchange(c_ref, place_ref, tag_ref, send_ref, e_ref, val_ref)


def fetch_areas(first, m_ref, buf, sem):
    half = K // 2
    copies = [
        [
            pltpu.make_async_copy(
                m_ref.at[first + q, pl.ds(half * n, half)],
                buf.at[q, pl.ds(half * n, half)],
                sem.at[q, n],
            )
            for n in range(2)
        ]
        for q in range(HALF)
    ]
    for group in copies:
        for copy in group:
            copy.start()
    return copies


def product(first, q, copies, buf, load_ref, diag_ref, lo_ref, hi_ref, e_ref, moved_in):
    area = first + q
    at = slice(area, area + 1)
    group = iota((S, 128), 1) >> 4
    part = jnp.zeros((S, 128), F32)
    for r in range(ROWS):
        piece = e_ref[:, ITEMS * r : ITEMS * r + ITEMS]
        shift = (NB * (r - area)) % 128
        if shift:
            piece = pltpu.roll(piece, shift, 1)
        part = jnp.where(group == r, piece, part)
    moved = moved_in[q]
    y = jnp.clip(moved, lo_ref[at, :], hi_ref[at, :])
    w = moved - y
    base = load_ref[area] + SIGMA * (y - w)
    side = jnp.concatenate([base[:, :128] + part, base[:, 128:]], axis=1)
    rounded = side.astype(BF16)
    half = K // 2
    copies[q][0].wait()
    x = side * diag_ref[at, :] + dot(rounded[:, :half], buf[q, :half])
    copies[q][1].wait()
    return x + dot(rounded[:, half:], buf[q, half:]), w


def area_kernel(
    first, m_ref, load_ref, diag_ref, lo_ref, hi_ref, e_ref, moved_in, tie_ref, *refs
):
    if first:
        c_in, moved_ref, c_ref, buf, sem = refs
    else:
        moved_ref, c_ref, tie_out, buf, sem = refs
    copies = fetch_areas(first, m_ref, buf, sem)
    group = iota((S, 128), 1) >> 4
    edges = [
        c_in[:, ITEMS * r : ITEMS * r + ITEMS] if first else jnp.zeros((S, 128), F32)
        for r in range(ROWS)
    ]
    news = []
    for q in range(HALF + 1):
        if q < HALF:
            at = slice(first + q, first + q + 1)
            x, w = product(first, q, copies, buf, load_ref, diag_ref, lo_ref, hi_ref, e_ref, moved_in)
            moved = x + w
            moved_ref[q] = moved
            y = jnp.clip(moved, lo_ref[at, :], hi_ref[at, :])
            news.append(load_ref[first + q] + SIGMA * (y - (moved - y)))
        if q > 0:
            area = first + q - 1
            diag = diag_ref[area : area + 1, :128]
            c = edge_part(news[q - 1], buf[q - 1, :, :128], diag)
            for r in range(ROWS):
                shift = (NB * (area - r)) % 128
                turned = pltpu.roll(c, shift, 1) if shift else c
                edges[r] = jnp.where(group == area, turned, edges[r])
    for r in range(ROWS):
        c_ref[:, ITEMS * r : ITEMS * r + ITEMS] = edges[r]
    if not first:
        tie_out[...] = edges[0][:8]


def last_kernel(
    first, m_ref, load_ref, diag_ref, lo_ref, hi_ref, e_ref, moved_in, tie_ref, *refs
):
    if first:
        _, x_ref, buf, sem, x_buf, x_sem = refs
    else:
        x_ref, tie_out, buf, sem, x_buf, x_sem = refs
    copies = fetch_areas(first, m_ref, buf, sem)
    order = edge_order(True)
    writes = []
    for q in range(HALF):
        x, _ = product(first, q, copies, buf, load_ref, diag_ref, lo_ref, hi_ref, e_ref, moved_in)
        x_buf[q] = jnp.concatenate([pick(x[:, :128], order), x[:, 128:]], axis=1)
        writes.append(pltpu.make_async_copy(x_buf.at[q], x_ref.at[first + q], x_sem.at[q]))
        writes[-1].start()
    if not first:
        tie_out[...] = jnp.zeros((8, 128), F32)
    for copy in writes:
        copy.wait()


def on_device(loads, factor, pivots, lower, upper, incidence, counts):
    wide = ROWS * ITEMS
    exchange = lambda x: lax.all_to_all(x, BOTH, split_axis=0, concat_axis=0, tiled=True)
    me = lax.axis_index("region").astype(jnp.int32).reshape(1)
    area_block = lambda rows: pl.BlockSpec((2, rows, K), lambda a: (a, 0, 0))
    whole = lambda *shape: pl.BlockSpec(shape, lambda a: (0,) * len(shape))
    stripe = lambda i: pl.BlockSpec((2, K // 4, (i + 1) * K // 4), lambda a: (a, i, 0))
    outs = (
        (struct((AREA, K, K), BF16), area_block(K)),
        (struct((AREA, K)), whole(AREA, K)),
        (struct((wide, wide), BF16), whole(wide, wide)),
        (struct((1, wide)), whole(1, wide)),
        (struct((AREA, S, K)), area_block(S)),
        (struct((AREA, K)), whole(AREA, K)),
        (struct((AREA, K)), whole(AREA, K)),
        (struct((ITEMS, 256), BF16), whole(ITEMS, 256)),
        (struct((256, ITEMS), BF16), whole(256, ITEMS)),
        (struct((1, ITEMS)), whole(1, ITEMS)),
        (struct((512, 128)), whole(512, 128)),
        (struct((S, wide)), whole(S, wide)),
        (struct((128, 128)), whole(128, 128)),
    )
    (matrix, diag, bd, bd_diag, load, floor_box, ceil_box, place, place_t, live, send, e, val) = call(
        setup_kernel,
        tuple(shape for shape, _ in outs),
        grid=(AREA // 2,),
        in_specs=[SMEM, SMEM] + [stripe(i) for i in range(4)]
        + [whole(AREA, K), area_block(S), whole(AREA, K), whole(AREA, K), whole(AREA, NB)],
        out_specs=tuple(spec for _, spec in outs),
        scratch_shapes=[
            pltpu.VMEM((K, K), BF16),
            pltpu.VMEM((K, K), BF16),
            pltpu.VMEM((K, K), BF16),
            pltpu.VMEM((K, K), BF16),
            pltpu.VMEM((2, ITEMS), F32),
            pltpu.VMEM((S, wide), F32),
        ],
        cost_estimate=cost(8 * 10**9, 34 * 2**20),
        limit=60,
    )(me, counts, *[factor] * 4, pivots, loads, lower, upper, incidence)

    part_shape = struct((HALF, S, K))
    scratch = [
        pltpu.VMEM((HALF, K, K), BF16),
        pltpu.SemaphoreType.DMA((HALF, 2)),
    ]

    def run_areas(first, e, moved, tie, c=None):
        return call(
            functools.partial(area_kernel, first),
            (part_shape, struct((S, wide))) + (() if first else (struct((8, 128)),)),
            in_specs=[HBM] + [VM] * (8 if first else 7),
            out_specs=(VM,) * (2 if first else 3),
            scratch_shapes=scratch,
            input_output_aliases={6: 0},
            cost_estimate=cost(4 * 10**8, 10 * 2**20),
            limit=20,
        )(matrix, load, diag, floor_box, ceil_box, e, moved, tie, *((c,) if first else ()))

    def run_last(first, e, moved, tie, x=None):
        x_shape = struct((AREA, S, K))
        return call(
            functools.partial(last_kernel, first),
            x_shape if first else (x_shape, struct((8, 128))),
            in_specs=[HBM] + [VM] * 7 + ([HBM] if first else []),
            out_specs=HBM if first else (HBM, VM),
            scratch_shapes=scratch
            + [pltpu.VMEM((HALF, S, K), F32), pltpu.SemaphoreType.DMA((HALF,))],
            input_output_aliases={8: 0} if first else {},
            cost_estimate=cost(4 * 10**8, 10 * 2**20),
            limit=20,
        )(matrix, load, diag, floor_box, ceil_box, e, moved, tie, *((x,) if first else ()))

    z_shape = struct((N_REGION, 256))
    rows2 = struct((256, 128))
    rec_shape = struct((32, 128))
    small = cost(10**7, 2**20)
    owner_first = call(
        functools.partial(owner_kernel, True, False),
        (rows2, z_shape, rows2, rec_shape, rows2, z_shape),
        in_specs=[VM] * 2,
        cost_estimate=small,
    )
    owner_mid = call(
        functools.partial(owner_kernel, False, False),
        (rows2, z_shape, rows2, rec_shape),
        in_specs=[SMEM] + [VM] * 7,
        input_output_aliases={5: 1, 6: 2, 7: 3},
        cost_estimate=small,
    )
    owner_last = call(
        functools.partial(owner_kernel, False, True),
        struct((512, 128)),
        in_specs=[SMEM] + [VM] * 7,
        cost_estimate=small,
    )
    run_slots = call(
        slot_kernel,
        (rows2, struct((S, wide)), struct((128, 128))),
        in_specs=[VM] * 8,
        input_output_aliases={4: 2},
        cost_estimate=cost(10**8, 3 * 2**20),
    )

    def iterate(step, state):
        send, e, val, z, u_far, rec, moved0, moved1 = state[:8]
        got = exchange(send)
        moved0, c, tie = run_areas(0, e, moved0, z)
        if step is None:
            back, z, u_far, rec, tags_at, inverse = owner_first(got, tie)
        else:
            tags_at, inverse = state[8:]
            at = jnp.asarray(step, jnp.int32).reshape(1)
            back, z, u_far, rec = owner_mid(at, got, tags_at, inverse, tie, z, u_far, rec)
        z_back = exchange(back)
        moved1, c = run_areas(HALF, e, moved1, z, c)
        send, e, val = run_slots(z_back, place, place_t, live, val, c, bd, bd_diag)
        return (send, e, val, z, u_far, rec, moved0, moved1, tags_at, inverse)

    zero = jnp.zeros((HALF, S, K), F32)
    state = (send, e, val, jnp.zeros((N_REGION, 256), F32), None, None, zero, zero)
    state = iterate(None, state)
    state = lax.fori_loop(1, ITERS - 1, iterate, state)
    send, e, val, z, u_far, rec, moved0, moved1, tags_at, inverse = state
    got = exchange(send)
    x, tie = run_last(0, e, moved0, z)
    back = owner_last(
        jnp.full((1,), ITERS - 1, jnp.int32), got, tags_at, inverse, tie, z, u_far, rec
    )
    z_back = exchange(back)
    x = run_last(HALF, e, moved1, back, x)
    duals, record = call(
        close_kernel, (struct((128, 128)), struct((2, ITERS))), in_specs=[VM] * 4
    )(z_back, place_t, live, val)
    return (x, duals.reshape(AREA, NB, 128), record.T)


def solution(mesh):
    area_split = (
        P(BOTH, None, None),
        P(BOTH, None, None),
        P(BOTH, None),
        P(BOTH, None),
        P(BOTH, None),
        P(BOTH, None),
        P(BOTH),
    )
    return jax.shard_map(
        on_device,
        mesh=mesh,
        in_specs=area_split,
        out_specs=(P(BOTH, None, None), P(BOTH, None, None), P()),
        check_vma=False,
    )
```
